32 devices in a mesh: dp: 8 (over z, x), replica: 4 (over y, core).
Axes of the slice: x: 2, y: 2, z: 4, core: 2. Of those that a mesh axis runs over, the one named last changes fastest.
Arguments:
- tokens: float32 [24576, 768], P(('dp', 'replica')), may hold values from -6 to 6
- patch_counts: int32 [64], replicated, may hold values from 76 to 384, as said below
- code_bits: int32 [24576, 18], P(('dp', 'replica')), may hold values from 0 to 1
- out_grad: float32 [24576, 768], P(('dp', 'replica')), may hold values from -6 to 6
- ln1_gain: float32 [768], replicated, may hold values from 0.1 to 1.9
- w_qkv: bfloat16 [768, 2304], replicated, may hold values from -0.21875 to 0.21875
- w_attn_out: bfloat16 [768, 768], replicated, may hold values from -0.875 to 0.875
- ln2_gain: float32 [768], replicated, may hold values from 0.1 to 1.9
- w_mlp_in: bfloat16 [768, 3072], replicated, may hold values from -0.21875 to 0.21875
- w_mlp_out: bfloat16 [3072, 768], replicated, may hold values from -0.109375 to 0.109375
- w_down: bfloat16 [768, 18], replicated, may hold values from -0.21875 to 0.21875
- w_up: bfloat16 [18, 768], replicated, may hold values from -1.5 to 1.5
Outputs:
- decoded: float32 [24576, 768], P(('dp', 'replica'))
- entropy_loss: float32 [], replicated
- grad_tokens: float32 [24576, 768], P(('dp', 'replica'))
- grad_ln1_gain: float32 [768], P(('dp', 'replica'))
- grad_w_qkv: float32 [768, 2304], P(('dp', 'replica'))
- grad_w_attn_out: float32 [768, 768], P(('dp', 'replica'))
- grad_ln2_gain: float32 [768], P(('dp', 'replica'))
- grad_w_mlp_in: float32 [768, 3072], P(('dp', 'replica'))
- grad_w_mlp_out: float32 [3072, 768], P(('dp', 'replica'))
- grad_w_down: float32 [768, 18], P(('dp', 'replica'))
- grad_w_up: float32 [18, 768], P(None, ('dp', 'replica'))
The draws below stay inside these ranges and needn't reach their ends.
Inputs may be any that keep to these rules, and one draw needn't show every extreme that they name: `patch_counts`: each image holds (1 + b) * 384 // 5 patches for some b of 0 to 4; the last image holds 384.
All inputs are finite; a program needn't handle non-finite values.
Results may differ from the reference program's by a relative error of at most 0.015.
Values sent between devices are 32-bit elements; how exact they have to be, the bound alone decides.
A program may use at most 192 MiB of HBM per device.

```python
import jax
import jax.numpy as jnp
from jax import lax

D = 768
HEADS = 12
HEAD = 64
FF = 3072
BITS = 18
SEQ = 384
IMAGES = 64
TOKENS = 24576


def draw_patch_counts(key, part):
    key = jax.random.fold_in(key, 11)
    image_index = jnp.arange(IMAGES, dtype=jnp.int32)
    bucket = jax.random.randint(key, (IMAGES,), 0, 2, dtype=jnp.int32) + 4 * image_index // IMAGES
    bucket = jnp.minimum(bucket, 4)
    bucket = bucket.at[IMAGES - 1].set(4)
    return (1 + bucket) * SEQ // 5


def touch_ends(result, key, low, top_value):
    index_at = [jax.random.randint(jax.random.fold_in(key, axis), (), 0, length) for axis, length in enumerate(result.shape)]
    main_axis = result.shape.index(max(result.shape))
    neighbour = index_at[:main_axis] + [(index_at[main_axis] + 1) % result.shape[main_axis]] + index_at[main_axis + 1:]
    return result.at[tuple(index_at)].set(low).at[tuple(neighbour)].set(top_value)


def levels(key, dims, pieces, least, top_value):
    factor_of, own = 1.0, jax.random.fold_in(key, 6)
    for axis_at, shards_of in pieces:
        heights = jnp.exp(jax.random.uniform(jax.random.fold_in(own, axis_at), (shards_of,), jnp.float32, least / len(pieces), top_value / len(pieces)))
        factor_of = factor_of * jnp.repeat(heights, dims[axis_at] // shards_of).reshape([-1 if axis == axis_at else 1 for axis in range(len(dims))])
    return factor_of


def noise(own_key, dims, scale, reach, cuts=(), kind=jnp.bfloat16):
    result = scale * jax.random.normal(own_key, dims, jnp.float32)
    if cuts:
        result = result * levels(own_key, dims, cuts, -0.22, 0.18)
    return jnp.clip(result, -reach, reach).astype(kind)


def setup_inputs(seed: int = 0) -> dict:
    keys = jax.random.split(jax.random.key(seed), 13)
    return {
        "tokens": noise(keys[0], (TOKENS, D), 1.0, 6.0, ((0, 32),), jnp.float32),
        "patch_counts": draw_patch_counts(jax.random.fold_in(keys[12], 71), 0),
        "code_bits": touch_ends(jax.random.randint(keys[2], (TOKENS, BITS), 0, 2), jax.random.fold_in(keys[2], 1), 0, 1).astype(jnp.int32),
        "out_grad": noise(keys[3], (TOKENS, D), 1.0, 6.0, ((0, 32),), jnp.float32),
        "ln1_gain": jnp.clip(1.0 + 0.18 * jax.random.normal(keys[4], (D,), jnp.float32), 0.1, 1.9),
        "w_qkv": noise(keys[5], (D, 3 * D), D ** -0.5, 0.21875),
        "w_attn_out": noise(keys[6], (D, D), (D // 16) ** -0.5, 0.875),
        "ln2_gain": jnp.clip(1.0 + 0.18 * jax.random.normal(keys[7], (D,), jnp.float32), 0.1, 1.9),
        "w_mlp_in": noise(keys[8], (D, FF), D ** -0.5, 0.21875),
        "w_mlp_out": noise(keys[9], (FF, D), FF ** -0.5, 0.109375),
        "w_down": noise(keys[10], (D, BITS), D ** -0.5, 0.21875),
        "w_up": noise(keys[11], (BITS, D), BITS ** -0.5, 1.5),
    }


@jax.custom_vjp
def low(v):
    return lax.optimization_barrier(v.astype(jnp.bfloat16)).astype(jnp.float32)

@jax.custom_vjp
def low_back(v):
    return v

def low_keep(v):
    return (low(v), None)

def low_pass(kept, grad):
    return (grad,)

def back_keep(v):
    return (v, None)

def back_low(kept, grad):
    return (low(grad),)
low.defvjp(low_keep, low_pass)
low_back.defvjp(back_keep, back_low)
eps_norm = 1e-06
neg_big = -1e+30
sharpness = 8.0
commit_weight = 0.25
group_images = 8
highest = lax.Precision.HIGHEST

def matmul(left, right):
    return jnp.dot(left, right, precision=highest)

def layer_norm(values, gain):
    centered = values - lax.optimization_barrier(jnp.mean(values, axis=-1, keepdims=True))
    inv_std = lax.rsqrt(lax.optimization_barrier(jnp.mean(centered * centered, axis=-1, keepdims=True)) + eps_norm)
    return centered * inv_std * gain

def encode_group(params, group_block):
    ln1_gain, w_qkv, w_attn_out, ln2_gain, w_mlp_in, w_mlp_out, w_down = params
    group_tokens, counts = group_block
    images = counts.shape[0]
    valid_keys = jnp.arange(SEQ)[None, :] < counts[:, None]
    attn_in = low(layer_norm(group_tokens, ln1_gain))
    qkv_rows = low(low_back(matmul(attn_in, w_qkv))).reshape(images, SEQ, 3, HEADS, HEAD)
    scores = low_back(jnp.einsum('bqhd,bkhd->bhqk', qkv_rows[:, :, 0], qkv_rows[:, :, 1], precision=highest))
    logits = jnp.where(valid_keys[:, None, None, :], scores * HEAD ** (-0.5), neg_big)
    row_max = lax.optimization_barrier(jnp.max(logits, axis=-1, keepdims=True))
    weights = jnp.exp(logits - row_max)
    attn_prob = low(weights / lax.optimization_barrier(jnp.sum(weights, axis=-1, keepdims=True)))
    context = jnp.einsum('bhqk,bkhd->bqhd', attn_prob, qkv_rows[:, :, 2], precision=highest)
    context = low(low_back(context)).reshape(images * SEQ, D)
    hidden1 = group_tokens + low_back(matmul(context, w_attn_out))
    mlp_in = low(layer_norm(hidden1, ln2_gain))
    activation = low(jax.nn.gelu(low_back(matmul(mlp_in, w_mlp_in)), approximate=False))
    hidden2 = hidden1 + low_back(matmul(activation, w_mlp_out))
    raw_code = low_back(matmul(low(hidden2), w_down))
    return raw_code * lax.rsqrt(lax.optimization_barrier(jnp.sum(raw_code * raw_code, axis=-1, keepdims=True)) + 1.0)

def encode_all(tokens, patch_counts, params):
    groups = IMAGES // group_images
    group_blocks = (tokens.reshape(groups, group_images * SEQ, D), patch_counts.reshape(groups, group_images))
    coded = lax.map(jax.checkpoint(lambda group_block: encode_group(params, group_block)), group_blocks)
    return coded.reshape(TOKENS, BITS)

def reference(tokens, patch_counts, code_bits, out_grad, ln1_gain, w_qkv, w_attn_out, ln2_gain, w_mlp_in, w_mlp_out, w_down, w_up):
    weights_in = (ln1_gain.astype(jnp.float32), w_qkv.astype(jnp.float32), w_attn_out.astype(jnp.float32), ln2_gain.astype(jnp.float32), w_mlp_in.astype(jnp.float32), w_mlp_out.astype(jnp.float32), w_down.astype(jnp.float32))
    up_weight = w_up.astype(jnp.float32)
    row_valid = (jnp.arange(SEQ)[None, :] < patch_counts[:, None]).reshape(TOKENS).astype(jnp.float32)[:, None]
    total_count = jnp.sum(patch_counts).astype(jnp.float32)
    target = (2.0 * code_bits.astype(jnp.float32) - 1.0) * BITS ** (-0.5)
    first_pass = encode_all(tokens, patch_counts, weights_in)
    shift_code = target - first_pass

    def forward(tokens_in, gain_one, weight_qkv, weight_out, gain_two, weight_in, weight_back, weight_down, weight_up):
        unit_code = encode_all(tokens_in, patch_counts, (gain_one, weight_qkv, weight_out, gain_two, weight_in, weight_back, weight_down))
        quant = low(unit_code + shift_code)
        decoded = row_valid * low_back(matmul(quant, weight_up))
        logit_bits = unit_code * sharpness
        soft_prob = jax.nn.sigmoid(logit_bits)
        token_ent = jax.nn.softplus(logit_bits) - soft_prob * logit_bits
        mean_prob = lax.optimization_barrier(jnp.sum(soft_prob * row_valid, axis=0)) / total_count
        code_ent = jnp.sum(-mean_prob * jnp.log(mean_prob) - (1.0 - mean_prob) * jnp.log(1.0 - mean_prob))
        code_miss = unit_code - target
        commit_sum = jnp.sum(code_miss * code_miss * row_valid)
        ent_sum = jnp.sum(token_ent * row_valid)
        entropy_loss = (commit_weight * commit_sum + ent_sum) / total_count - code_ent
        return (decoded, entropy_loss)
    outputs, pullback = jax.vjp(forward, tokens, *weights_in, up_weight)
    decoded, entropy_loss = outputs
    grads = pullback((out_grad, total_count * jnp.ones_like(entropy_loss)))
    grad_scale = TOKENS ** (-0.5)
    return (decoded, entropy_loss, grads[0], grads[1] * grad_scale, grads[2] * grad_scale, grads[3] * grad_scale, grads[4] * grad_scale, grads[5] * grad_scale, grads[6] * grad_scale, grads[7] * grad_scale, grads[8] * grad_scale)
```

```python
import functools
import math

import jax
import jax.numpy as jnp
from jax import lax
from jax.experimental import pallas as pl
from jax.experimental.pallas import tpu as pltpu
from jax.sharding import PartitionSpec as P

HEADS, HEAD, BITS, SEQ = 12, 64, 18, 384
D, FF = 768, 3072
EPS = 1e-06
bf16, f32 = jnp.bfloat16, jnp.float32

def dot(a, b, ca=1, cb=0):
    return lax.dot_general(a, b, (((ca,), (cb,)), ((), ())), preferred_element_type=f32)

def norm_stats(v):
    mean = jnp.sum(v, axis=1, keepdims=True) * (1.0 / D)
    cen = v - mean
    var = jnp.sum(cen * cen, axis=1, keepdims=True) * (1.0 / D)
    inv = lax.rsqrt(var + EPS)
    return cen * inv, inv

def cols(i, n):
    return pl.ds(pl.multiple_of(i * n, n), n)

def lanes_of(rows, width=128):
    return lax.broadcasted_iota(jnp.int32, (rows, width), 1)

def widen(bits, width=128):
    z = jnp.zeros((bits.shape[0], 32 - BITS), bits.dtype)
    one = jnp.concatenate([bits, z], axis=1)
    return jnp.concatenate([one] * 4, axis=1)

def gelu_parts(x):
    cdf = 0.5 + 0.5 * lax.erf(x * math.sqrt(0.5))
    pdf = jnp.exp(x * x * -0.5) * (1.0 / math.sqrt(2.0 * math.pi))
    return x * cdf, cdf + x * pdf

MC = 512
def forward_kernel(counts, tokens_h, wqkv_h, wao_h, win_h, wout_h, g1, g2, wdown,
                   qkv_h, e_h, linv_h, ctx_h, hid_h, mlpin_h, act_h, slope_h, raw_o, mc_o,
                   tokens, wqkv, wao, win, wout, attn_in, qkv, e, linv, ctx, hid, mlpin, act, slope, wd4, sem, osem):
    loads = [pltpu.make_async_copy(s, d, sem.at[i]) for i, (s, d) in enumerate(
        [(tokens_h, tokens), (wqkv_h, wqkv), (wao_h, wao), (wout_h, wout), (win_h, win)])]
    for l in loads: l.start()
    outs = []
    def put(src, dst):
        cp = pltpu.make_async_copy(src, dst, osem.at[len(outs)])
        cp.start(); outs.append(cp)
    loads[0].wait()
    def ln1(i, _):
        r = cols(i, 128)
        n, _inv = norm_stats(tokens[r, :])
        attn_in[r, :] = (n * g1[...]).astype(bf16)
        return 0
    lax.fori_loop(0, 6, ln1, 0)
    loads[1].wait()
    def proj(i, _):
        v = dot(attn_in[...], wqkv[:, cols(i, 256)])
        v = v * jnp.where(i < 3, 0.125, 1.0)
        qkv[pl.ds(pl.multiple_of(i // 3 * D, D), D), cols(i % 3, 256)] = v.astype(bf16)
        return 0
    lax.fori_loop(0, 9, proj, 0)
    put(qkv, qkv_h)
    first = (lax.axis_index("dp") * lax.axis_size("replica") + lax.axis_index("replica")) * 2
    def att(i, _):
        img = i // 3
        n = counts[first + img]
        r = pl.ds(pl.multiple_of(img * SEQ, SEQ), SEQ)
        ok = lax.broadcasted_iota(jnp.int32, (1, SEQ), 1) < n
        low = lanes_of(SEQ) < HEAD
        one = jnp.ones((SEQ, 128), bf16)
        for j in range(2):
            o = i % 3 * 2 + j
            q2, k2, v2 = (qkv[pl.ds(pl.multiple_of(b * D + img * SEQ, 128), SEQ), cols(o, 128)] for b in range(3))
            zero = jnp.zeros_like(q2)
            vo = jnp.concatenate([v2, one], axis=1)
            res = []
            for h in range(2):
                q = jnp.where(low, q2, zero) if h == 0 else jnp.where(low, zero, q2)
                s = jnp.where(ok, dot(q, k2, 1, 1), -1e30)
                m = jnp.max(s, axis=1, keepdims=True)
                p = jnp.exp(s - m).astype(bf16)
                e[img * HEADS + o * 2 + h] = p
                ov = dot(p, vo)
                inv = 1.0 / ov[:, 128:]
                res.append((ov[:, :128] * inv, inv))
            cs = pl.ds(pl.multiple_of(o * 128, 128), 128)
            ctx[r, cs] = jnp.where(low, res[0][0], res[1][0]).astype(bf16)
            linv[r, cs] = jnp.where(low, res[0][1], res[1][1])
        return 0
    lax.fori_loop(0, 6, att, 0)
    put(e, e_h); put(linv, linv_h); put(ctx, ctx_h)
    loads[2].wait()
    def ao(i, _):
        r = cols(i, 256)
        h = tokens[r, :] + dot(ctx[r, :], wao[...])
        hid[r, :] = h
        n, _inv = norm_stats(h)
        mlpin[r, :] = (n * g2[...]).astype(bf16)
        return 0
    lax.fori_loop(0, 3, ao, 0)
    put(hid, hid_h); put(mlpin, mlpin_h)
    loads[3].wait()
    wd4[...] = widen(wdown[...].astype(f32)).astype(bf16)
    def mcf(i, _):
        r = cols(i, 768)
        v = dot(wout[r, :], wd4[...])
        hi = v.astype(bf16).astype(f32)
        mc_o[r, :] = jnp.where(lanes_of(768) % 64 < 32, hi, v - hi).astype(bf16)
        return 0
    lax.fori_loop(0, 4, mcf, 0)
    loads[4].wait()
    def mlp(i, _):
        cs = cols(i, MC)
        a, s = gelu_parts(dot(mlpin[...], win[:, cs]))
        act[:, cs] = a.astype(bf16)
        slope[:, cs] = s.astype(bf16)
        return 0
    lax.fori_loop(0, FF // MC, mlp, 0)
    put(act, act_h); put(slope, slope_h)
    raw = dot(act[...], mc_o[...])
    raw = raw + pltpu.roll(raw, 32, 1)
    raw_o[...] = raw + dot(hid[...].astype(bf16), wd4[...])
    for o in outs: o.wait()

def forward(counts, tokens, wqkv, wao, win, wout, g1, g2, wdown):
    T = tokens.shape[0]
    any_, vm = pl.BlockSpec(memory_space=pl.ANY), pl.BlockSpec(memory_space=pltpu.VMEM)
    outs = [((3 * D, D), bf16), ((24, SEQ, SEQ), bf16), ((T, D), f32), ((T, D), bf16), ((T, D), f32), ((T, D), bf16),
            ((T, FF), bf16), ((T, FF), bf16)]
    return pl.pallas_call(forward_kernel,
        out_shape=[jax.ShapeDtypeStruct(*o) for o in outs] + [jax.ShapeDtypeStruct((T, 128), f32), jax.ShapeDtypeStruct((FF, 128), bf16)],
        in_specs=[pl.BlockSpec(memory_space=pltpu.SMEM)] + [any_] * 5 + [vm] * 3,
        out_specs=[any_] * 8 + [vm] * 2,
        scratch_shapes=[pltpu.VMEM((T, D), f32), pltpu.VMEM((D, 3 * D), bf16), pltpu.VMEM((D, D), bf16), pltpu.VMEM((D, FF), bf16), pltpu.VMEM((FF, D), bf16),
            pltpu.VMEM((T, D), bf16)] + [pltpu.VMEM(*o) for o in outs] + [pltpu.VMEM((D, 128), bf16), pltpu.SemaphoreType.DMA((5,)), pltpu.SemaphoreType.DMA((8,))],
        compiler_params=pltpu.CompilerParams(vmem_limit_bytes=63 << 20),
        name="forward")(counts, tokens, wqkv, wao, win, wout, g1.reshape(1, D), g2.reshape(1, D), wdown)

MESH = pl.DeviceIdType.MESH
W = 256
CHUNKS = 24
LAGS = (0, 1, 5, 8, 10)

def place():
    dp, rp = lax.axis_index("dp"), lax.axis_index("replica")
    return dp // 2, dp % 2, rp // 2, rp % 2

def device(z, x, y, c):
    return (z * 2 + x, y * 2 + c)

def enter():
    z, x, y, c = place()
    bar = pltpu.get_barrier_semaphore()
    peers = [device(z, x, y, 1 - c), device(z, 1 - x, y, c), device(z, x, 1 - y, c)]
    peers += [device((z + d) % 4, x, y, c) for d in (1, 2, 3)]
    for p in peers:
        pl.semaphore_signal(bar, inc=1, device_id=p, device_id_type=MESH)
    pl.semaphore_wait(bar, len(peers))

class Scatter:
    def __init__(self, n, bufs, result):
        self.n = n
        self.g, self.r0, self.r1, self.r2, self.r3, self.send, self.recv = bufs
        self.result = result
        self.ring = self.g.shape[0]
        self.z, self.x, self.y, self.c = place()
    def axes(self, par):
        z, x, y, c = self.z, self.x, self.y, self.c
        tx, ty = device(z, 1 - x, y, c), device(z, x, 1 - y, c)
        return (x, y, tx, ty) if par == 0 else (y, x, ty, tx)
    def copy(self, k, n, src, dst, to):
        return pltpu.make_async_remote_copy(src, dst, self.send.at[k, n], self.recv.at[k, n], device_id=to, device_id_type=MESH)
    def c0(self, k, par):
        return self.copy(k, 0, self.g.at[par % self.ring, 1 - self.c], self.r0.at[k], device(self.z, self.x, self.y, 1 - self.c))
    def c1(self, k, par):
        a, b, ta, tb = self.axes(par)
        return self.copy(k, 1, self.r0.at[k, 1 - a], self.r1.at[k], ta)
    def c2(self, k, par):
        a, b, ta, tb = self.axes(par)
        return self.copy(k, 2, self.r1.at[k, 1 - b], self.r2.at[k], tb)
    def c3(self, k, d):
        t = (self.z + d) % 4
        return self.copy(k, 2 + d, self.r2.at[k, t], self.r3.at[k, d - 1], device(t, self.x, self.y, self.c))
    def put(self, par, v, lane=0):
        for o in range(32):
            z, x, y, c = o // 8, o // 4 % 2, o // 2 % 2, o % 2
            a, b = (x, y) if par == 0 else (y, x)
            self.g[par % self.ring, c, a, b, z, :, lane:lane + v.shape[1]] = v[o * 24:o * 24 + 24]
    def step0(self, k, par):
        self.c0(k, par).start()
    def step1(self, k, par):
        self.c0(k, par).wait()
        self.r0[k] += self.g[par % self.ring, self.c]
        self.c1(k, par).start()
    def step2(self, k, par):
        a, b, ta, tb = self.axes(par)
        self.c1(k, par).wait()
        self.r1[k] += jnp.where(a == 0, self.r0[k, 0], self.r0[k, 1])
        self.c2(k, par).start()
    def step3(self, k, par):
        a, b, ta, tb = self.axes(par)
        self.c2(k, par).wait()
        self.r2[k] += jnp.where(b == 0, self.r1[k, 0], self.r1[k, 1])
        for d in (1, 2, 3):
            self.c3(k, d).start()
    def step4(self, k, par):
        for d in (1, 2, 3):
            self.c3(k, d).wait()
        z = self.z
        own = jnp.where(z < 2, jnp.where(z == 0, self.r2[k, 0], self.r2[k, 1]), jnp.where(z == 2, self.r2[k, 2], self.r2[k, 3]))
        self.result(k, own + self.r3[k, 0] + self.r3[k, 1] + self.r3[k, 2])
    def tick(self, t, off, start=0, end=5):
        for s in range(4, -1, -1):
            if not start <= s < end:
                continue
            k, par = t - LAGS[s], (off - LAGS[s]) % 2
            run = functools.partial(getattr(self, f"step{s}"), par=par)
            if isinstance(t, int):
                if 0 <= k < self.n:
                    run(jnp.int32(k))
            else:
                pl.when(k >= 0)(functools.partial(run, k))

def scatter_bufs(n, ring, w):
    return [pltpu.VMEM((ring, 2, 2, 2, 4, 24, w), f32), pltpu.VMEM((n, 2, 2, 4, 24, w), f32), pltpu.VMEM((n, 2, 4, 24, w), f32),
            pltpu.VMEM((n, 4, 24, w), f32), pltpu.VMEM((n, 3, 24, w), f32),
            pltpu.SemaphoreType.DMA((n, 6)), pltpu.SemaphoreType.DMA((n, 6))]

def norm_back(grad, normed, inv, gain):
    gn = grad * gain
    spread = jnp.sum(gn * normed, axis=1, keepdims=True) * (1.0 / D)
    mean = jnp.sum(gn, axis=1, keepdims=True) * (1.0 / D)
    return inv * (gn - mean - normed * spread), jnp.sum(grad * normed, axis=0, keepdims=True)

def backward_kernel(counts, raw, bits, wup, wdown, g1, g2, mc,
                    tokens_h, outgrad_h, wqkv_h, wao_h, win_h, wout_h, qkv_h, e_h, linv_h, ctx_h, hid_h, mlpin_h, act_h, slope_h,
                    gtok_h, loss_o, grads_o, small_o, tail_o,
                    big, wao, win, wout, e, ctx, hid, mlpin, act, slope, mlpinT, ainT, dattn, draw, drawT, unit_s,
                    wup4, wd4, smallT, gT, quantT, gain1, st, zs, sem, ssem, rsem, esem, osem, *bufs):
    main = Scatter(CHUNKS, bufs[0:7], lambda k, v: grads_o.__setitem__(k, v))
    small = Scatter(1, bufs[7:14], lambda k, v: small_o.__setitem__(Ellipsis, v))
    tail = Scatter(1, bufs[14:21], lambda k, v: tail_o.__setitem__(Ellipsis, v))
    z, x, y, c = place()
    names = dict(outgrad=(outgrad_h, big), mlpin=(mlpin_h, mlpin), slope=(slope_h, slope), win=(win_h, win), act=(act_h, act),
                 hid=(hid_h, hid), wout=(wout_h, wout), ctx=(ctx_h, ctx), wao=(wao_h, wao), qkv=(qkv_h, wout.at[:3 * D]),
                 linv=(linv_h, big), wqkv=(wqkv_h, win.at[:, :3 * D]), tokens=(tokens_h, big))
    order = list(names)
    loads = {n: pltpu.make_async_copy(*names[n], sem.at[i]) for i, n in enumerate(order)}
    for n in order[:9]:
        loads[n].start()
    def load_e(g, img):
        return pltpu.make_async_copy(e_h.at[pl.ds(img * HEADS + g * 4, 4)], e.at[img], esem.at[img])
    for img in range(2):
        load_e(0, img).start()
    enter()
    first = (lax.axis_index("dp") * lax.axis_size("replica") + lax.axis_index("replica")) * 2
    n0, n1 = counts[first], counts[first + 1]
    total = lax.fori_loop(0, counts.shape[0], lambda i, a: a + counts[i], jnp.int32(0)).astype(f32)
    wup4[...] = jnp.zeros_like(wup4)
    for j in range(4):
        wup4[32 * j:32 * j + BITS, :] = wup[...].astype(f32)
    wd4[...] = widen(wdown[...].astype(f32)).astype(bf16)
    RB = 128
    def live(i):
        row = lax.broadcasted_iota(jnp.int32, (RB, 128), 0) + i * RB
        return row < jnp.where(row < SEQ, n0, n1 + SEQ)
    def codes(i):
        r = cols(i, RB)
        rawv = raw[r, :]
        inv_len = lax.rsqrt(jnp.sum(rawv * rawv, axis=1, keepdims=True) * 0.25 + 1.0)
        unit = rawv * inv_len
        target = widen(2.0 * bits[r, :].astype(f32) - 1.0) * BITS ** -0.5
        both = jnp.where(live(i) & (lanes_of(RB) % 32 < BITS), 1.0, 0.0)
        return r, inv_len, unit, target, both
    def count(i, sums):
        r, inv_len, unit, target, both = codes(i)
        zl = unit * 8.0
        p = jax.nn.sigmoid(zl)
        miss = unit - target
        ent = jnp.maximum(zl, 0.0) + jnp.log1p(jnp.exp(-jnp.abs(zl))) - p * zl
        return tuple(s + jnp.sum(v * both, axis=0, keepdims=True) for s, v in zip(sums, (p, ent, miss * miss)))
    sums = lax.fori_loop(0, 768 // RB, count, (jnp.zeros((1, 128), f32),) * 3)
    rows8 = lax.broadcasted_iota(jnp.int32, (8, 128), 0)
    st[0] = jnp.where(rows8 == 0, sums[0], jnp.where(rows8 == 1, sums[1], jnp.where(rows8 == 2, sums[2], 0.0)))
    def scopy(i, to):
        return pltpu.make_async_remote_copy(st.at[2 * i], st.at[2 * i + 1], ssem.at[i], rsem.at[i], device_id=to, device_id_type=MESH)
    ring = [device(z, x, y, 1 - c), device(z, 1 - x, y, c), device(z, x, 1 - y, c)]
    def zcopy(d):
        return pltpu.make_async_remote_copy(zs.at[z], zs.at[z], ssem.at[2 + d], rsem.at[2 + d], device_id=device((z + d) % 4, x, y, c), device_id_type=MESH)
    def pass_on(i):
        scopy(i, ring[i]).wait()
        s = st[2 * i] + st[2 * i + 1]
        if i < 2:
            st[2 * i + 2] = s
            scopy(i + 1, ring[i + 1]).start()
        else:
            zs[z] = s
            for d in (1, 2, 3): zcopy(d).start()
    scopy(0, ring[0]).start()
    loads["outgrad"].wait()
    def decode(i, _):
        r = cols(i, RB)
        ok = live(i)
        for j in range(6):
            cs = slice(j * 128, (j + 1) * 128)
            dattn[r, cs] = jnp.where(ok, big[r, cs], 0.0).astype(bf16)
        target = widen(2.0 * bits[r, :].astype(f32) - 1.0) * BITS ** -0.5
        draw[r, :] = target.astype(bf16)
        return 0
    lax.fori_loop(0, 768 // RB, decode, 0)
    pass_on(0)
    wup4b = wup4[...].astype(bf16)
    unit_s[...] = dot(dattn[...], wup4b, 1, 1)
    pass_on(1)
    drawT[...] = draw[...].T
    quantT[...] = dot(drawT[...], dattn[...])
    pass_on(2)
    loads["mlpin"].wait()
    mlpinT[...] = mlpin[...].T
    for d in (1, 2, 3): zcopy(d).wait()
    zsum = zs[0] + zs[1] + zs[2] + zs[3]
    bit8 = lanes_of(8) % 32 < BITS
    mean_prob = jnp.where(bit8, zsum / total, 0.5)[0:1]
    odds = jnp.log(mean_prob / (1.0 - mean_prob))
    g0 = lanes_of(8)[0:1] < BITS
    code_ent = jnp.sum(jnp.where(g0, -mean_prob * jnp.log(mean_prob) - (1.0 - mean_prob) * jnp.log(1.0 - mean_prob), 0.0))
    other = jnp.sum(jnp.where(g0, 0.25 * zsum[2:3] + zsum[1:2], 0.0))
    loss_o[0, 0] = other / total - code_ent
    def unit_back(i, _):
        r, inv_len, unit, target, both = codes(i)
        zl = unit * 8.0
        p = jax.nn.sigmoid(zl)
        gunit = unit_s[r, :] + both * (8.0 * p * (1.0 - p) * (odds - zl) + 0.5 * (unit - target))
        graw = inv_len * (gunit - unit * (jnp.sum(gunit * unit, axis=1, keepdims=True) * 0.25))
        draw[r, :] = graw.astype(bf16)
        return 0
    lax.fori_loop(0, 768 // RB, unit_back, 0)
    loads["slope"].wait()
    def mlp(i, _):
        for j in range(2):
            t = 2 * i + j
            cs = cols(t, W)
            d = dot(draw[...], mc[cs, :], 1, 1) * 0.5
            dp = (slope[:, cs].astype(f32) * d).astype(bf16)
            slope[:, cs] = dp
            main.put(j, dot(mlpinT[...], dp))
            main.tick(t, j)
        return 0
    lax.fori_loop(0, 6, mlp, 0)
    drawT[...] = draw[...].T
    loads["act"].wait()
    gT[...] = dot(drawT[...], act[...])
    for b in range(8):
        t = gT[:, b * 384:(b + 1) * 384].T.reshape(4, 4, 24, 128)
        l4 = lax.broadcasted_iota(jnp.int32, (4, 24, 128), 2) // 32
        s = jnp.where(l4 == 0, t[:, 0], 0.0)
        for j in range(1, 4):
            s = jnp.where(l4 == j, t[:, j], s)
        for o in range(4):
            small.g[0, o % 2, b % 2, o // 2, b // 2, :, 0:128] = s[o]
    loads["hid"].wait()
    loads["wout"].wait()
    gv = gT[...]
    hi = gv.astype(bf16)
    lo = (gv - hi.astype(f32)).astype(bf16)
    gwd = dot(drawT[...], hid[...].astype(bf16)) + dot(hi, wout[...]) + dot(lo, wout[...])
    loads["win"].wait()
    loads["linv"].start()
    loads["qkv"].start()
    def ln2(i, gain2):
        r = cols(i, 256)
        dn = dot(slope[r, :], win[...], 1, 1)
        nrm, inv = norm_stats(hid[r, :])
        gin, gg = norm_back(dn, nrm, inv, g2[...])
        v = gin + dot(draw[r, :], wd4[...], 1, 1) * 0.25
        hid[r, :] = v
        dattn[r, :] = v.astype(bf16)
        return gain2 + gg
    gain2 = lax.fori_loop(0, 3, ln2, jnp.zeros((1, D), f32))
    r128 = lax.broadcasted_iota(jnp.int32, (128, D), 0)
    smallT[...] = jnp.where(r128 < 32, gwd, jnp.where(r128 < 64, quantT[...], jnp.where(r128 == 64, gain2, 0.0)))
    for i in range(6):
        unit_s[i * 128:(i + 1) * 128, :] = smallT[:, i * 128:(i + 1) * 128].T
    small.put(0, unit_s[...], 128)
    zero = jnp.int32(0)
    small.step0(zero, 0)
    loads["wqkv"].start()
    loads["ctx"].wait()
    loads["wao"].wait()
    loads["linv"].wait()
    mlpinT[...] = ctx[...].T
    def dctx(i, _):
        r = cols(i, 256)
        mlpin[r, :] = (dot(dattn[r, :], wao[...], 1, 1) * big[r, :]).astype(bf16)
        return 0
    lax.fori_loop(0, 3, dctx, 0)
    small.step1(zero, 0)
    loads["tokens"].start()
    loads["qkv"].wait()
    low = lanes_of(SEQ) < HEAD
    loads["tokens"].wait()
    for i in range(6):
        r = pl.ds(i * 128, 128)
        nrm, inv = norm_stats(big[r, :])
        ainT[:, i * 128:(i + 1) * 128] = (nrm * g1[...]).astype(bf16).T
    def group(g, _):
        t = 12 + 4 * g
        main.put(0, dot(mlpinT[...], dattn[:, cols(g, W)]))
        main.tick(t, 0)
        def image(img, _):
            load_e(g, img).wait()
            r = pl.ds(pl.multiple_of(img * SEQ, SEQ), SEQ)
            for j in range(2):
                o = g * 2 + j
                q2, k2, v2 = (wout[pl.ds(pl.multiple_of(b * D + img * SEQ, 128), SEQ), cols(o, 128)] for b in range(3))
                cs = pl.ds(pl.multiple_of(o * 128, 128), 128)
                d2, c2 = mlpin[r, cs], ctx[r, cs]
                prod = d2.astype(f32) * c2.astype(f32)
                zero_ = jnp.zeros_like(q2)
                dq = dk = dv = None
                for h in range(2):
                    mine = low if h == 0 else jnp.logical_not(low)
                    pick = lambda a: jnp.where(mine, a, zero_)
                    dh = pick(d2)
                    ev = e[img, 2 * j + h]
                    dd = jnp.sum(jnp.where(mine, prod, 0.0), axis=1, keepdims=True)
                    ds = (ev.astype(f32) * (dot(dh, v2, 1, 1) - dd)).astype(bf16)
                    a, b, cc = dot(ds, pick(k2)), dot(ds, pick(q2), 0, 0), dot(ev, dh, 0, 0)
                    dq, dk, dv = (a, b, cc) if h == 0 else (dq + a, dk + b, dv + cc)
                for b, v in enumerate((dq * 0.125, dk, dv)):
                    act[r, pl.ds(pl.multiple_of(b * D + o * 128, 128), 128)] = v.astype(bf16)
            @pl.when(g < 2)
            def _():
                load_e(g + 1, img).start()
            return 0
        lax.fori_loop(0, 2, image, 0)
        for j in range(3):
            main.put((1 + j) % 2, dot(ainT[...], act[:, pl.ds(pl.multiple_of(j * D + g * W, W), W)]))
            main.tick(t + 1 + j, (1 + j) % 2)
        return 0
    lax.fori_loop(0, 3, group, 0)
    small.step2(zero, 0)
    loads["wqkv"].wait()
    def ln1(i, gain):
        r = cols(i, 256)
        dn = dot(act[r, :3 * D], win[:, :3 * D], 1, 1)
        nrm, inv = norm_stats(big[r, :])
        gin, gg = norm_back(dn, nrm, inv, g1[...])
        hid[r, :] += gin
        gain1[...] += gg
        return 0
    gain1[...] = jnp.zeros_like(gain1)
    lax.fori_loop(0, 3, ln1, 0)
    gtok = pltpu.make_async_copy(hid, gtok_h, osem)
    gtok.start()
    small.step3(zero, 0)
    quantT[...] = jnp.broadcast_to(gain1[...], (128, D))
    for i in range(6):
        unit_s[i * 128:(i + 1) * 128, :] = quantT[:, i * 128:(i + 1) * 128].T
    tail.put(1, unit_s[...])
    tail.step0(zero, 1)
    for t in range(CHUNKS, CHUNKS + LAGS[4] + 1):
        main.tick(t, t % 2)
        if t == CHUNKS: tail.step1(zero, 1)
        if t == CHUNKS + LAGS[2] - 1: tail.step2(zero, 1)
        if t == CHUNKS + LAGS[3] - 1: tail.step3(zero, 1); small.step4(zero, 0)
    tail.step4(zero, 1)
    gtok.wait()

def backward(counts, raw, bits, wup, wdown, g1, g2, mc, tokens, outgrad, wqkv, wao, win, wout, qkv, e, linv, ctx, hid, mlpin, act, slope):
    T = 768
    any_, vm, sm = pl.BlockSpec(memory_space=pl.ANY), pl.BlockSpec(memory_space=pltpu.VMEM), pl.BlockSpec(memory_space=pltpu.SMEM)
    V = pltpu.VMEM
    return pl.pallas_call(backward_kernel,
        out_shape=[jax.ShapeDtypeStruct(s, f32) for s in [(T, D), (1, 1), (CHUNKS, 24, W), (24, 256), (24, 128)]],
        in_specs=[sm] + [vm] * 7 + [any_] * 14,
        out_specs=[any_, sm, vm, vm, vm],
        scratch_shapes=[V((T, D), f32), V((D, D), bf16), V((D, FF), bf16), V((FF, D), bf16), V((2, 4, SEQ, SEQ), bf16),
            V((T, D), bf16), V((T, D), f32), V((T, D), bf16), V((T, FF), bf16), V((T, FF), bf16), V((D, T), bf16), V((D, T), bf16),
            V((T, D), bf16), V((T, 128), bf16), V((128, T), bf16), V((T, 128), f32),
            V((128, D), f32), V((D, 128), bf16), V((128, D), f32), V((128, FF), f32), V((128, D), f32), V((1, D), f32), V((6, 8, 128), f32), V((4, 8, 128), f32),
            pltpu.SemaphoreType.DMA((13,)), pltpu.SemaphoreType.DMA((6,)), pltpu.SemaphoreType.DMA((6,)), pltpu.SemaphoreType.DMA((2,)), pltpu.SemaphoreType.DMA(())]
            + scatter_bufs(CHUNKS, 2, W) + scatter_bufs(1, 1, W) + scatter_bufs(1, 1, 128),
        compiler_params=pltpu.CompilerParams(vmem_limit_bytes=64 << 20, collective_id=1, has_side_effects=True),
        name="backward")(counts, raw, bits, wup, wdown, g1.reshape(1, D), g2.reshape(1, D), mc, tokens, outgrad, wqkv, wao, win, wout, qkv, e, linv, ctx, hid, mlpin, act, slope)

def kernel_body(tokens, counts, bits, outgrad, g1, wqkv, wao, g2, win, wout, wdown, wup):
    qkv, e, linv, ctx, hid, mlpin, act, slope, raw, mc = forward(counts, tokens, wqkv, wao, win, wout, g1, g2, wdown)
    gtok, loss, grads, small, tail = backward(counts, raw, bits, wup, wdown, g1, g2, mc, tokens, outgrad, wqkv, wao, win, wout, qkv, e, linv, ctx, hid, mlpin, act, slope)
    T = tokens.shape[0]
    scale = (T * 32) ** -0.5
    first = (lax.axis_index("dp") * lax.axis_size("replica") + lax.axis_index("replica")) * 2
    cn = lax.dynamic_slice_in_dim(counts, first, 2)
    valid = (jnp.arange(SEQ)[None] < cn[:, None]).reshape(T, 1)
    target = ((2.0 * bits.astype(f32) - 1.0) * BITS ** -0.5).astype(bf16)
    decoded = jnp.where(valid, jnp.dot(target, wup, preferred_element_type=f32), 0.0)
    grads = grads * scale
    small = small * scale
    gwin = grads[:12].transpose(1, 0, 2).reshape(24, FF)
    grp = grads[12:].reshape(3, 4, 24, 256)
    gwao = grp[:, 0].transpose(1, 0, 2).reshape(24, D)
    gwqkv = grp[:, 1:].transpose(2, 1, 0, 3).reshape(24, 3 * D)
    G = small[:, :128].reshape(24, 4, 32)[:, :, :BITS].transpose(1, 0, 2).reshape(96, BITS)
    gwout = jnp.dot(G, wdown.astype(f32).T, precision=lax.Precision.HIGHEST)
    return (decoded, loss.reshape(()), gtok, tail[:, 0] * scale, gwqkv, gwao, small[:, 128 + 64], gwin, gwout, small[:, 128:128 + BITS], small[:, 160:160 + BITS].T)


eps_norm = 1e-06
neg_big = -1e30
sharpness = 8.0
commit_weight = 0.25


def exact_gelu(values):
    return jax.nn.gelu(values, approximate=False)


def layer_norm(values, gain):
    centered = values - jnp.mean(values, axis=-1, keepdims=True)
    inv_std = lax.rsqrt(jnp.mean(centered * centered, axis=-1, keepdims=True) + eps_norm)
    normed = centered * inv_std
    return (normed * gain, normed, inv_std)


def plain_norm_back(grad_out, normed, inv_std, gain):
    grad_normed = grad_out * gain
    grad_gain = jnp.sum(grad_out * normed, axis=0)
    spread_part = jnp.mean(grad_normed * normed, axis=-1, keepdims=True)
    grad_in = inv_std * (
        grad_normed - jnp.mean(grad_normed, axis=-1, keepdims=True) - normed * spread_part
    )
    return (grad_in, grad_gain)


def inner_rows(left, right):
    return lax.dot_general(
        left, right, (((0,), (0,)), ((), ())), preferred_element_type=jnp.float32
    )


def times_transposed(left, right):
    return lax.dot_general(
        left, right, (((1,), (1,)), ((), ())), preferred_element_type=jnp.float32
    )


def attention_logits(queries, key_rows, key_valid):
    scores = jnp.einsum("bqhd,bkhd->bhqk", queries, key_rows, preferred_element_type=jnp.float32)
    return jnp.where(key_valid, scores * HEAD ** (-0.5), neg_big)


def plain_body(
    tokens,
    patch_counts,
    code_bits,
    out_grad,
    ln1_gain,
    w_qkv,
    w_attn_out,
    ln2_gain,
    w_mlp_in,
    w_mlp_out,
    w_down,
    w_up,
):
    row_count = tokens.shape[0]
    images = row_count // SEQ
    width_all = tokens.shape[1]
    first_image = lax.axis_index(("dp", "replica")) * images
    counts = lax.dynamic_slice_in_dim(patch_counts, first_image, images)
    total_count = jnp.sum(patch_counts).astype(jnp.float32)
    valid_slots = jnp.arange(SEQ, dtype=jnp.int32)[None, :] < counts[:, None]
    key_valid = valid_slots[:, None, None, :]
    row_valid = valid_slots.reshape(row_count).astype(jnp.float32)[:, None]
    target = (2.0 * code_bits.astype(jnp.float32) - 1.0) * BITS ** (-0.5)
    normed1_out, normed1, inv_std1 = layer_norm(tokens, ln1_gain)
    attn_in = normed1_out.astype(jnp.bfloat16)
    qkv_rows = jnp.dot(attn_in, w_qkv, preferred_element_type=jnp.float32).astype(jnp.bfloat16)
    qkv_rows = qkv_rows.reshape(images, SEQ, 3, HEADS, HEAD)
    queries = qkv_rows[:, :, 0]
    key_rows = qkv_rows[:, :, 1]
    value_rows = qkv_rows[:, :, 2]
    logits = attention_logits(queries, key_rows, key_valid)
    row_max = jnp.max(logits, axis=-1, keepdims=True)
    weights = jnp.exp(logits - row_max)
    row_total = jnp.sum(weights, axis=-1, keepdims=True)
    log_total = row_max + jnp.log(row_total)
    prob_low = (weights / row_total).astype(jnp.bfloat16)
    context = jnp.einsum(
        "bhqk,bkhd->bqhd", prob_low, value_rows, preferred_element_type=jnp.float32
    )
    context_low = context.astype(jnp.bfloat16).reshape(row_count, width_all)
    hidden1 = tokens + jnp.dot(context_low, w_attn_out, preferred_element_type=jnp.float32)
    normed2_out, normed2, inv_std2 = layer_norm(hidden1, ln2_gain)
    mlp_in = normed2_out.astype(jnp.bfloat16)
    pre_act = jnp.dot(mlp_in, w_mlp_in, preferred_element_type=jnp.float32)
    activation, gelu_back = jax.vjp(exact_gelu, pre_act)
    activation_low = activation.astype(jnp.bfloat16)
    hidden2 = hidden1 + jnp.dot(activation_low, w_mlp_out, preferred_element_type=jnp.float32)
    hidden2_low = hidden2.astype(jnp.bfloat16)
    raw_code = jnp.dot(hidden2_low, w_down, preferred_element_type=jnp.float32)
    inv_len = lax.rsqrt(jnp.sum(raw_code * raw_code, axis=-1, keepdims=True) + 1.0)
    unit_code = raw_code * inv_len
    quant_low = target.astype(jnp.bfloat16)
    decoded = row_valid * jnp.dot(quant_low, w_up, preferred_element_type=jnp.float32)
    logit_bits = unit_code * sharpness
    soft_prob = jax.nn.sigmoid(logit_bits)
    token_ent = jax.nn.softplus(logit_bits) - soft_prob * logit_bits
    code_miss = unit_code - target
    prob_sum = jnp.sum(soft_prob * row_valid, axis=0)
    ent_sum = jnp.sum(token_ent * row_valid)
    commit_sum = jnp.sum(code_miss * code_miss * row_valid)
    prob_sum, ent_sum, commit_sum = lax.psum((prob_sum, ent_sum, commit_sum), ("dp", "replica"))
    mean_prob = prob_sum / total_count
    code_ent = jnp.sum(
        -mean_prob * jnp.log(mean_prob) - (1.0 - mean_prob) * jnp.log(1.0 - mean_prob)
    )
    entropy_loss = (commit_weight * commit_sum + ent_sum) / total_count - code_ent
    grad_dec_low = (row_valid * out_grad).astype(jnp.bfloat16)
    grad_w_up = inner_rows(quant_low, grad_dec_low)
    grad_quant = times_transposed(grad_dec_low, w_up)
    prob_logit = jnp.log(mean_prob / (1.0 - mean_prob))
    loss_part = (
        sharpness * soft_prob * (1.0 - soft_prob) * (prob_logit - logit_bits)
        + 2.0 * commit_weight * code_miss
    )
    grad_unit = grad_quant + row_valid * loss_part
    grad_raw = inv_len * (
        grad_unit - unit_code * jnp.sum(grad_unit * unit_code, axis=-1, keepdims=True)
    )
    grad_raw_low = grad_raw.astype(jnp.bfloat16)
    grad_w_down = inner_rows(hidden2_low, grad_raw_low)
    grad_hidden2 = times_transposed(grad_raw_low, w_down)
    grad_mlp_low = grad_hidden2.astype(jnp.bfloat16)
    grad_w_mlp_out = inner_rows(activation_low, grad_mlp_low)
    grad_activation = times_transposed(grad_mlp_low, w_mlp_out)
    grad_pre_low = gelu_back(grad_activation)[0].astype(jnp.bfloat16)
    grad_w_mlp_in = inner_rows(mlp_in, grad_pre_low)
    grad_norm2_in = times_transposed(grad_pre_low, w_mlp_in)
    grad_from_norm2, grad_ln2 = plain_norm_back(grad_norm2_in, normed2, inv_std2, ln2_gain)
    grad_hidden1 = grad_hidden2 + grad_from_norm2
    grad_attn_low = grad_hidden1.astype(jnp.bfloat16)
    grad_w_attn_out = inner_rows(context_low, grad_attn_low)
    grad_context = times_transposed(grad_attn_low, w_attn_out).astype(jnp.bfloat16)
    grad_context = grad_context.reshape(images, SEQ, HEADS, HEAD)
    grad_values = jnp.einsum(
        "bhqk,bqhd->bkhd", prob_low, grad_context, preferred_element_type=jnp.float32
    )
    grad_prob = jnp.einsum(
        "bqhd,bkhd->bhqk", grad_context, value_rows, preferred_element_type=jnp.float32
    )
    attn_prob = jnp.exp(attention_logits(queries, key_rows, key_valid) - log_total)
    grad_scores = (
        attn_prob
        * (grad_prob - jnp.sum(grad_prob * attn_prob, axis=-1, keepdims=True))
        * HEAD ** (-0.5)
    )
    grad_scores_low = grad_scores.astype(jnp.bfloat16)
    grad_queries = jnp.einsum(
        "bhqk,bkhd->bqhd", grad_scores_low, key_rows, preferred_element_type=jnp.float32
    )
    grad_keys = jnp.einsum(
        "bhqk,bqhd->bkhd", grad_scores_low, queries, preferred_element_type=jnp.float32
    )
    grad_qkv = jnp.stack((grad_queries, grad_keys, grad_values), axis=2).reshape(
        row_count, 3 * width_all
    )
    grad_qkv_low = grad_qkv.astype(jnp.bfloat16)
    grad_w_qkv = inner_rows(attn_in, grad_qkv_low)
    grad_norm1_in = times_transposed(grad_qkv_low, w_qkv)
    grad_from_norm1, grad_ln1 = plain_norm_back(grad_norm1_in, normed1, inv_std1, ln1_gain)
    grad_tokens = grad_hidden1 + grad_from_norm1
    summed = (
        lax.psum_scatter(grad_ln1, ("dp", "replica"), scatter_dimension=0, tiled=True),
        lax.psum_scatter(grad_w_qkv, ("dp", "replica"), scatter_dimension=0, tiled=True),
        lax.psum_scatter(grad_w_attn_out, ("dp", "replica"), scatter_dimension=0, tiled=True),
        lax.psum_scatter(grad_ln2, ("dp", "replica"), scatter_dimension=0, tiled=True),
        lax.psum_scatter(grad_w_mlp_in, ("dp", "replica"), scatter_dimension=0, tiled=True),
        lax.psum_scatter(grad_w_mlp_out, ("dp", "replica"), scatter_dimension=0, tiled=True),
        lax.psum_scatter(grad_w_down, ("dp", "replica"), scatter_dimension=0, tiled=True),
        lax.psum_scatter(grad_w_up, ("dp", "replica"), scatter_dimension=1, tiled=True),
    )
    grad_scale = (row_count * lax.axis_size(("dp", "replica"))) ** (-0.5)
    return (
        decoded,
        entropy_loss,
        grad_tokens,
        summed[0] * grad_scale,
        summed[1] * grad_scale,
        summed[2] * grad_scale,
        summed[3] * grad_scale,
        summed[4] * grad_scale,
        summed[5] * grad_scale,
        summed[6] * grad_scale,
        summed[7] * grad_scale,
    )


def solution(mesh):
    in_specs = (
        P(("dp", "replica"), None),
        P(),
        P(("dp", "replica"), None),
        P(("dp", "replica"), None),
        P(),
        P(),
        P(),
        P(),
        P(),
        P(),
        P(),
        P(),
    )
    out_specs = (
        P(("dp", "replica"), None),
        P(),
        P(("dp", "replica"), None),
        P(("dp", "replica")),
        P(("dp", "replica"), None),
        P(("dp", "replica"), None),
        P(("dp", "replica")),
        P(("dp", "replica"), None),
        P(("dp", "replica"), None),
        P(("dp", "replica"), None),
        P(None, ("dp", "replica")),
    )
    body = kernel_body if (mesh.shape["dp"], mesh.shape["replica"]) == (8, 4) else plain_body
    return jax.shard_map(body, mesh=mesh, in_specs=in_specs, out_specs=out_specs, check_vma=False)
```

```python
import functools
import math

import jax
import jax.numpy as jnp
from jax import lax
from jax.experimental import pallas as pl
from jax.experimental.pallas import tpu as pltpu
from jax.sharding import PartitionSpec as P

HEADS, HEAD, BITS, SEQ = 12, 64, 18, 384
D, FF = 768, 3072
EPS = 1e-06
bf16, f32 = jnp.bfloat16, jnp.float32

def dot(a, b, ca=1, cb=0):
    return lax.dot_general(a, b, (((ca,), (cb,)), ((), ())), preferred_element_type=f32)

def norm_stats(v):
    mean = jnp.sum(v, axis=1, keepdims=True) * (1.0 / D)
    cen = v - mean
    var = jnp.sum(cen * cen, axis=1, keepdims=True) * (1.0 / D)
    inv = lax.rsqrt(var + EPS)
    return cen * inv, inv

def cols(i, n):
    return pl.ds(pl.multiple_of(i * n, n), n)

def lanes_of(rows, width=128):
    return lax.broadcasted_iota(jnp.int32, (rows, width), 1)

def widen(ref, rows):
    ref[...] = jnp.zeros_like(ref)
    for j in range(4):
        ref[32 * j:32 * j + BITS, :] = rows

def gelu_parts(x):
    cdf = 0.5 + 0.5 * lax.erf(x * math.sqrt(0.5))
    pdf = jnp.exp(x * x * -0.5) * (1.0 / math.sqrt(2.0 * math.pi))
    return x * cdf, cdf + x * pdf

MC = 512
def forward_kernel(counts, tokens_h, wqkv_h, wao_h, win_h, wout_h, g1, g2, wdownT, bitsT, wup,
                   qkv_h, e_h, linv_h, ctx_h, hid_h, mlpin_h, act_h, slope_h, dec_h, raw_o, mc_o,
                   tokens, wqkv, wao, win, wout, attn_in, qkv, e, linv, ctx, hid, mlpin, act, slope, dec, wide, wd4, sem, osem):
    loads = [pltpu.make_async_copy(s, d, sem.at[i]) for i, (s, d) in enumerate(
        [(tokens_h, tokens), (wqkv_h, wqkv), (wao_h, wao), (wout_h, wout), (win_h, win)])]
    for l in loads: l.start()
    outs = []
    def put(src, dst):
        cp = pltpu.make_async_copy(src, dst, osem.at[len(outs)])
        cp.start(); outs.append(cp)
    first = (lax.axis_index("dp") * lax.axis_size("replica") + lax.axis_index("replica")) * 2
    n0, n1 = counts[first], counts[first + 1]
    widen(wide, wup[...].astype(f32))
    up = wide[...].astype(bf16)
    widen(wide, (2.0 * bitsT[...].astype(f32) - 1.0) * BITS ** -0.5)
    wide_t = (wide[...].T * 0.25).astype(bf16)
    for i in range(3):
        r = pl.ds(i * 256, 256)
        row = lax.broadcasted_iota(jnp.int32, (256, D), 0) + i * 256
        live = row < jnp.where(row < SEQ, n0, n1 + SEQ)
        dec[r, :] = jnp.where(live, dot(wide_t[i * 256:(i + 1) * 256], up), 0.0)
    put(dec, dec_h)
    widen(wide, wdownT[...].astype(f32))
    wd4[...] = wide[...].T.astype(bf16)
    loads[0].wait()
    def ln1(i, _):
        r = cols(i, 128)
        n, _inv = norm_stats(tokens[r, :])
        attn_in[r, :] = (n * g1[...].reshape(1, D)).astype(bf16)
        return 0
    lax.fori_loop(0, 6, ln1, 0)
    loads[1].wait()
    def proj(i, _):
        v = dot(attn_in[...], wqkv[:, cols(i, 256)])
        v = v * jnp.where(i < 3, 0.125, 1.0)
        qkv[pl.ds(pl.multiple_of(i // 3 * D, D), D), cols(i % 3, 256)] = v.astype(bf16)
        return 0
    lax.fori_loop(0, 9, proj, 0)
    put(qkv, qkv_h)
    def att(i, _):
        img = i // 3
        n = jnp.where(img == 0, n0, n1)
        r = pl.ds(pl.multiple_of(img * SEQ, SEQ), SEQ)
        ok = lax.broadcasted_iota(jnp.int32, (1, SEQ), 1) < n
        low = lanes_of(SEQ) < HEAD
        one = jnp.ones((SEQ, 128), bf16)
        for j in range(2):
            o = i % 3 * 2 + j
            q2, k2, v2 = (qkv[pl.ds(pl.multiple_of(b * D + img * SEQ, 128), SEQ), cols(o, 128)] for b in range(3))
            zero = jnp.zeros_like(q2)
            vo = jnp.concatenate([v2, one], axis=1)
            res = []
            for h in range(2):
                q = jnp.where(low, q2, zero) if h == 0 else jnp.where(low, zero, q2)
                s = jnp.where(ok, dot(q, k2, 1, 1), -1e30)
                m = jnp.max(s, axis=1, keepdims=True)
                p = jnp.exp(s - m).astype(bf16)
                e[img * HEADS + o * 2 + h] = p
                ov = dot(p, vo)
                inv = 1.0 / ov[:, 128:]
                res.append((ov[:, :128] * inv, inv))
            cs = pl.ds(pl.multiple_of(o * 128, 128), 128)
            ctx[r, cs] = jnp.where(low, res[0][0], res[1][0]).astype(bf16)
            linv[r, cs] = jnp.where(low, res[0][1], res[1][1])
        return 0
    lax.fori_loop(0, 6, att, 0)
    put(e, e_h); put(linv, linv_h); put(ctx, ctx_h)
    loads[2].wait()
    def ao(i, _):
        r = cols(i, 256)
        h = tokens[r, :] + dot(ctx[r, :], wao[...])
        hid[r, :] = h
        n, _inv = norm_stats(h)
        mlpin[r, :] = (n * g2[...].reshape(1, D)).astype(bf16)
        return 0
    lax.fori_loop(0, 3, ao, 0)
    put(hid, hid_h); put(mlpin, mlpin_h)
    loads[3].wait()
    def mcf(i, _):
        r = cols(i, 768)
        v = dot(wout[r, :], wd4[...])
        hi = v.astype(bf16).astype(f32)
        mc_o[r, :] = jnp.where(lanes_of(768) % 64 < 32, hi, v - hi).astype(bf16)
        return 0
    lax.fori_loop(0, 4, mcf, 0)
    loads[4].wait()
    def mlp(i, _):
        cs = cols(i, MC)
        a, s = gelu_parts(dot(mlpin[...], win[:, cs]))
        act[:, cs] = a.astype(bf16)
        slope[:, cs] = s.astype(bf16)
        return 0
    lax.fori_loop(0, FF // MC, mlp, 0)
    put(act, act_h); put(slope, slope_h)
    raw = dot(act[...], mc_o[...])
    raw = raw + pltpu.roll(raw, 32, 1)
    raw_o[...] = raw + dot(hid[...].astype(bf16), wd4[...])
    for o in outs: o.wait()

def forward(counts, tokens, wqkv, wao, win, wout, g1, g2, wdownT, bitsT, wup):
    T = tokens.shape[0]
    any_, vm = pl.BlockSpec(memory_space=pl.ANY), pl.BlockSpec(memory_space=pltpu.VMEM)
    outs = [((3 * D, D), bf16), ((24, SEQ, SEQ), bf16), ((T, D), f32), ((T, D), bf16), ((T, D), f32), ((T, D), bf16),
            ((T, FF), bf16), ((T, FF), bf16), ((T, D), f32)]
    return pl.pallas_call(forward_kernel,
        out_shape=[jax.ShapeDtypeStruct(*o) for o in outs] + [jax.ShapeDtypeStruct((T, 128), f32), jax.ShapeDtypeStruct((FF, 128), bf16)],
        in_specs=[pl.BlockSpec(memory_space=pltpu.SMEM)] + [any_] * 5 + [vm] * 5,
        out_specs=[any_] * 9 + [vm] * 2,
        scratch_shapes=[pltpu.VMEM((T, D), f32), pltpu.VMEM((D, 3 * D), bf16), pltpu.VMEM((D, D), bf16), pltpu.VMEM((D, FF), bf16), pltpu.VMEM((FF, D), bf16),
            pltpu.VMEM((T, D), bf16)] + [pltpu.VMEM(*o) for o in outs] + [pltpu.VMEM((128, D), f32), pltpu.VMEM((D, 128), bf16), pltpu.SemaphoreType.DMA((5,)), pltpu.SemaphoreType.DMA((9,))],
        compiler_params=pltpu.CompilerParams(vmem_limit_bytes=63 << 20),
        name="forward")(counts, tokens, wqkv, wao, win, wout, g1, g2, wdownT, bitsT, wup)

MESH = pl.DeviceIdType.MESH
W = 256
CHUNKS = 25
LAGS = (0, 1, 5, 7, 9, 10)

def place():
    dp, rp = lax.axis_index("dp"), lax.axis_index("replica")
    return dp // 2, dp % 2, rp // 2, rp % 2

def device(z, x, y, c):
    return (z * 2 + x, y * 2 + c)

def near():
    z, x, y, c = place()
    flip = lambda v, n: 1 - v if n else v
    return [device(z, flip(x, n & 4), flip(y, n & 2), flip(c, n & 1)) for n in range(1, 8)]

def column():
    z, x, y, c = place()
    return [device((z + d) % 4, x, y, c) for d in (1, 2, 3)]

def enter():
    bar = pltpu.get_barrier_semaphore()
    peers = near() + column()
    for p in peers:
        pl.semaphore_signal(bar, inc=1, device_id=p, device_id_type=MESH)
    pl.semaphore_wait(bar, len(peers))

def planar(k):
    if isinstance(k, int):
        return int(k % 4 == 0 if k <= 12 else k % 2 == 1)
    return jnp.where(k <= 12, jnp.where(lax.rem(k, 4) == 0, 1, 0), lax.rem(k, 2))

class Scatter:
    def __init__(self, bufs, result):
        self.g, self.r, (self.send, self.recv) = bufs[0], bufs[1:6], bufs[6:8]
        self.result = result
        self.at = place()
    def route(self, k, h, n):
        z, x, y, c = self.at
        p, zl, zh = planar(k), z % 2, z // 2
        tz = [(z + 1 - 2 * zl, 1 - p), (z + 2 - 4 * zh, 1 - p)]
        first, other = (x, y) if h == 0 else (y, x)
        def to(flip_first, flip_other, nz):
            f, o = first + flip_first * (1 - 2 * first), other + flip_other * (1 - 2 * other)
            return device(nz, *((f, o) if h == 0 else (o, f)), c)
        lowz, highz = z + 1 - 2 * zl, z + 2 - 4 * zh
        if n == 1:
            return first, to(1, 0, z)
        if n == 2:
            return p * other + (1 - p) * zl, to(0, p, p * z + (1 - p) * lowz)
        if n == 3:
            return p * zl + (1 - p) * zh, to(0, 0, p * lowz + (1 - p) * highz)
        return p * zh + (1 - p) * other, to(0, 1 - p, p * highz + (1 - p) * z)
    def copy(self, k, h, n):
        _, to = self.route(k, h, n)
        bit = self.route(k, h, n)[0]
        i = 2 * n - 1 + h
        return pltpu.make_async_remote_copy(self.r[n - 1].at[k, h, 1 - bit], self.r[n].at[k, h], self.send.at[k, i], self.recv.at[k, i],
                                            device_id=to, device_id_type=MESH)
    def pair(self, k, slot):
        z, x, y, c = self.at
        return pltpu.make_async_remote_copy(self.g.at[slot, 1 - c], self.r[0].at[k], self.send.at[k, 0], self.recv.at[k, 0],
                                            device_id=device(z, x, y, 1 - c), device_id_type=MESH)
    def put(self, slot, p, v, h):
        for o in range(32):
            z, x, y, c = o // 8, o // 4 % 2, o // 2 % 2, o % 2
            f, s = (x, y) if h == 0 else (y, x)
            order = (f, s, z % 2, z // 2) if p else (f, z % 2, z // 2, s)
            self.g[(slot, c, h, *order)] = v[o * 24:o * 24 + 24]
    def kept(self, k, h, n):
        bit, _ = self.route(k, h, n)
        return jnp.where(bit == 0, self.r[n - 1][k, h, 0], self.r[n - 1][k, h, 1])
    def step(self, s, k):
        for h in range(2):
            self.copy(k, h, s - 1).wait()
            v = self.r[s - 1][k, h] + self.kept(k, h, s - 1)
            if s == 5:
                self.result(k, h, v)
            else:
                self.r[s - 1][k, h] = v
                self.copy(k, h, s).start()
    def begin(self, k, slot):
        self.pair(k, slot).start()
    def join(self, k, slot):
        self.pair(k, slot).wait()
        self.r[0][k] += self.g[slot, self.at[3]]
        for h in range(2):
            self.copy(k, h, 1).start()
    def late(self, t):
        for s in (5, 4, 3, 2):
            k = t - LAGS[s]
            if isinstance(t, int):
                if 0 <= k < CHUNKS:
                    self.step(s, k)
            else:
                pl.when(k >= 0)(functools.partial(self.step, s, k))
    def early(self, t, slot):
        k = t - 1
        if isinstance(t, int):
            if k >= 0:
                self.join(k, 1 - slot)
            if t < CHUNKS:
                self.begin(t, slot)
        else:
            pl.when(k >= 0)(functools.partial(self.join, k, 1 - slot))
            self.begin(t, slot)

def scatter_bufs():
    blocks = [(2,) * (5 - n) for n in range(5)]
    return [pltpu.VMEM((2, 2, 2, 2, 2, 2, 2, 24, 128), f32)] + [pltpu.VMEM((CHUNKS,) + b + (24, 128), f32) for b in blocks] + [pltpu.SemaphoreType.DMA((CHUNKS, 9))] * 2

def norm_back(grad, normed, inv, gain):
    gn = grad * gain
    spread = jnp.sum(gn * normed, axis=1, keepdims=True) * (1.0 / D)
    mean = jnp.sum(gn, axis=1, keepdims=True) * (1.0 / D)
    return inv * (gn - mean - normed * spread)

RB = 128
def backward_kernel(counts, raw, bitsT, wup, wdownT, g1, g2, mc,
                    tokens_h, outgrad_h, wqkv_h, wao_h, win_h, wout_h, qkv_h, e_h, linv_h, ctx_h, hid_h, mlpin_h, act_h, slope_h,
                    gtok_h, loss_o, grads_o,
                    big, wao, win, wout, e, ctx, hid, mlpin, act, slope, mlpinT, ainT, dattn, draw, drawT, unit_s, target,
                    wide, wd4t, smallT, gT, quantT, s8, zs, sem, ssem, rsem, esem, osem, *bufs):
    def result(k, h, v):
        grads_o[k, :, h * 128:(h + 1) * 128] = v
    main = Scatter(bufs, result)
    z, x, y, c = place()
    names = dict(outgrad=(outgrad_h, big), mlpin=(mlpin_h, mlpin), slope=(slope_h, slope), act=(act_h, act), hid=(hid_h, hid),
                 wout=(wout_h, wout), win=(win_h, win), ctx=(ctx_h, ctx), wao=(wao_h, wao), qkv=(qkv_h, wout.at[:3 * D]),
                 linv=(linv_h, big), wqkv=(wqkv_h, win.at[:, :3 * D]), tokens=(tokens_h, big))
    order = list(names)
    loads = {n: pltpu.make_async_copy(*names[n], sem.at[i]) for i, n in enumerate(order)}
    for n in order[:9]:
        loads[n].start()
    def load_e(g, img):
        return pltpu.make_async_copy(e_h.at[pl.ds(img * HEADS + g * 4, 4)], e.at[img], esem.at[img])
    for img in range(2):
        load_e(0, img).start()
    enter()
    first = (lax.axis_index("dp") * lax.axis_size("replica") + lax.axis_index("replica")) * 2
    n0, n1 = counts[first], counts[first + 1]
    total = lax.fori_loop(0, counts.shape[0], lambda i, a: a + counts[i], jnp.int32(0)).astype(f32)
    widen(wide, (2.0 * bitsT[...].astype(f32) - 1.0) * BITS ** -0.5)
    target[...] = wide[...].T
    def live(i):
        row = lax.broadcasted_iota(jnp.int32, (RB, 128), 0) + i * RB
        return row < jnp.where(row < SEQ, n0, n1 + SEQ)
    def codes(i):
        r = cols(i, RB)
        rawv = raw[r, :]
        inv_len = lax.rsqrt(jnp.sum(rawv * rawv, axis=1, keepdims=True) * 0.25 + 1.0)
        both = jnp.where(live(i) & (lanes_of(RB) % 32 < BITS), 1.0, 0.0)
        return r, inv_len, rawv * inv_len, both
    def count(i, sums):
        r, inv_len, unit, both = codes(i)
        zl = unit * 8.0
        p = jax.nn.sigmoid(zl)
        miss = unit - target[r, :]
        ent = jnp.maximum(zl, 0.0) + jnp.log1p(jnp.exp(-jnp.abs(zl))) - p * zl
        return tuple(s + jnp.sum(v * both, axis=0, keepdims=True) for s, v in zip(sums, (p, ent, miss * miss)))
    sums = lax.fori_loop(0, 768 // RB, count, (jnp.zeros((1, 128), f32),) * 3)
    rows8 = lax.broadcasted_iota(jnp.int32, (8, 128), 0)
    own = x * 4 + y * 2 + c
    s8[own] = jnp.where(rows8 == 0, sums[0], jnp.where(rows8 == 1, sums[1], jnp.where(rows8 == 2, sums[2], 0.0)))
    def tell(ref, slot, i, to):
        return pltpu.make_async_remote_copy(ref.at[slot], ref.at[slot], ssem.at[i], rsem.at[i], device_id=to, device_id_type=MESH)
    tells = [tell(s8, own, i, p) for i, p in enumerate(near())]
    for t in tells: t.start()
    loads["outgrad"].wait()
    def decode(i, _):
        r = cols(i, RB)
        ok = live(i)
        for j in range(6):
            cs = slice(j * 128, (j + 1) * 128)
            dattn[r, cs] = jnp.where(ok, big[r, cs], 0.0).astype(bf16)
        return 0
    lax.fori_loop(0, 768 // RB, decode, 0)
    quantT[...] = dot(wide[...].astype(bf16), dattn[...])
    for t in tells: t.wait_recv()
    s = s8[0]
    for i in range(1, 8):
        s = s + s8[i]
    zs[z] = s
    ztells = [tell(zs, z, 7 + i, p) for i, p in enumerate(column())]
    for t in ztells: t.start()
    for t in tells: t.wait_send()
    widen(wide, wup[...].astype(f32))
    unit_s[...] = dot(dattn[...], wide[...].astype(bf16), 1, 1)
    loads["mlpin"].wait()
    mlpinT[...] = mlpin[...].T
    widen(wide, wdownT[...].astype(f32))
    wd4t[...] = wide[...].astype(bf16)
    for t in ztells: t.wait()
    zsum = zs[0] + zs[1] + zs[2] + zs[3]
    bit8 = lanes_of(8) % 32 < BITS
    mean_prob = jnp.where(bit8, zsum / total, 0.5)[0:1]
    odds = jnp.log(mean_prob / (1.0 - mean_prob))
    g0 = lanes_of(8)[0:1] < BITS
    code_ent = jnp.sum(jnp.where(g0, -mean_prob * jnp.log(mean_prob) - (1.0 - mean_prob) * jnp.log(1.0 - mean_prob), 0.0))
    other = jnp.sum(jnp.where(g0, 0.25 * zsum[2:3] + zsum[1:2], 0.0))
    loss_o[0, 0] = other / total - code_ent
    def unit_back(i, _):
        r, inv_len, unit, both = codes(i)
        zl = unit * 8.0
        p = jax.nn.sigmoid(zl)
        gunit = unit_s[r, :] + both * (8.0 * p * (1.0 - p) * (odds - zl) + 0.5 * (unit - target[r, :]))
        graw = inv_len * (gunit - unit * (jnp.sum(gunit * unit, axis=1, keepdims=True) * 0.25))
        draw[r, :] = graw.astype(bf16)
        return 0
    lax.fori_loop(0, 768 // RB, unit_back, 0)
    loads["slope"].wait()
    def put(t, p, v):
        for h in range(2):
            main.put(t % 2, p, v[:, h * 128:(h + 1) * 128], h)
    def mlp(i, _):
        for j in range(4):
            t = 4 * i + j
            cs = cols(t, W)
            d = dot(draw[...], mc[cs, :], 1, 1) * 0.5
            dp = (slope[:, cs].astype(f32) * d).astype(bf16)
            slope[:, cs] = dp
            main.late(t)
            put(j, planar(j), dot(mlpinT[...], dp))
            main.early(t, j % 2)
        return 0
    lax.fori_loop(0, 3, mlp, 0)
    main.late(12)
    drawT[...] = draw[...].T
    loads["act"].wait()
    gT[...] = dot(drawT[...], act[...])
    for b in range(8):
        t = gT[:, b * 384:(b + 1) * 384].T.reshape(4, 4, 24, 128)
        l4 = lax.broadcasted_iota(jnp.int32, (4, 24, 128), 2) // 32
        s = jnp.where(l4 == 0, t[:, 0], 0.0)
        for j in range(1, 4):
            s = jnp.where(l4 == j, t[:, j], s)
        unit_s[b * 96:(b + 1) * 96, :] = s.reshape(96, 128)
    main.put(0, 1, unit_s[...], 0)
    loads["hid"].wait()
    loads["wout"].wait()
    gv = gT[...]
    hi = gv.astype(bf16)
    lo = (gv - hi.astype(f32)).astype(bf16)
    gwd = dot(drawT[...], hid[...].astype(bf16)) + dot(hi, wout[...]) + dot(lo, wout[...])
    r128 = lax.broadcasted_iota(jnp.int32, (128, D), 0)
    smallT[...] = jnp.where(r128 < 32, gwd, quantT[...])
    for i in range(6):
        unit_s[i * 128:(i + 1) * 128, :] = smallT[:, i * 128:(i + 1) * 128].T
    main.put(0, 1, unit_s[...], 1)
    main.early(12, 0)
    loads["win"].wait()
    loads["linv"].start()
    loads["qkv"].start()
    main.late(13)
    def ln2(i, _):
        r = cols(i, 256)
        dn = dot(slope[r, :], win[...], 1, 1)
        nrm, inv = norm_stats(hid[r, :])
        v = norm_back(dn, nrm, inv, g2[...].reshape(1, D)) + dot(draw[r, :], wd4t[...]) * 0.25
        hid[r, :] = v
        dattn[r, :] = v.astype(bf16)
        return 0
    lax.fori_loop(0, 3, ln2, 0)
    loads["wqkv"].start()
    main.late(14)
    loads["ctx"].wait()
    loads["wao"].wait()
    loads["linv"].wait()
    mlpinT[...] = ctx[...].T
    def dctx(i, _):
        r = cols(i, 256)
        mlpin[r, :] = (dot(dattn[r, :], wao[...], 1, 1) * big[r, :]).astype(bf16)
        return 0
    lax.fori_loop(0, 3, dctx, 0)
    loads["tokens"].start()
    loads["qkv"].wait()
    low = lanes_of(SEQ) < HEAD
    loads["tokens"].wait()
    for i in range(6):
        r = pl.ds(i * 128, 128)
        nrm, inv = norm_stats(big[r, :])
        ainT[:, i * 128:(i + 1) * 128] = (nrm * g1[...].reshape(1, D)).astype(bf16).T
    def group(g, _):
        t0 = 13 + 4 * g
        main.late(t0 + 2)
        put(1, 1, dot(mlpinT[...], dattn[:, cols(g, W)]))
        main.early(t0, 1)
        def image(img, _):
            load_e(g, img).wait()
            r = pl.ds(pl.multiple_of(img * SEQ, SEQ), SEQ)
            for j in range(2):
                o = g * 2 + j
                q2, k2, v2 = (wout[pl.ds(pl.multiple_of(b * D + img * SEQ, 128), SEQ), cols(o, 128)] for b in range(3))
                cs = pl.ds(pl.multiple_of(o * 128, 128), 128)
                d2, c2 = mlpin[r, cs], ctx[r, cs]
                prod = d2.astype(f32) * c2.astype(f32)
                zero_ = jnp.zeros_like(q2)
                dq = dk = dv = None
                for h in range(2):
                    mine = low if h == 0 else jnp.logical_not(low)
                    pick = lambda a: jnp.where(mine, a, zero_)
                    dh = pick(d2)
                    ev = e[img, 2 * j + h]
                    dd = jnp.sum(jnp.where(mine, prod, 0.0), axis=1, keepdims=True)
                    ds = (ev.astype(f32) * (dot(dh, v2, 1, 1) - dd)).astype(bf16)
                    a, b, cc = dot(ds, pick(k2)), dot(ds, pick(q2), 0, 0), dot(ev, dh, 0, 0)
                    dq, dk, dv = (a, b, cc) if h == 0 else (dq + a, dk + b, dv + cc)
                for b, v in enumerate((dq * 0.125, dk, dv)):
                    act[r, pl.ds(pl.multiple_of(b * D + o * 128, 128), 128)] = v.astype(bf16)
            @pl.when(g < 2)
            def _():
                load_e(g + 1, img).start()
            main.late(t0 + 3 + img)
            return 0
        lax.fori_loop(0, 2, image, 0)
        for j in range(3):
            put(j, j % 2, dot(ainT[...], act[:, pl.ds(pl.multiple_of(j * D + g * W, W), W)]))
            main.early(t0 + 1 + j, j % 2)
            if j == 1:
                main.late(t0 + 5)
        return 0
    lax.fori_loop(0, 3, group, 0)
    main.early(25, 1)
    main.late(27)
    loads["wqkv"].wait()
    def ln1(i, _):
        r = cols(i, 256)
        dn = dot(act[r, :3 * D], win[:, :3 * D], 1, 1)
        nrm, inv = norm_stats(big[r, :])
        hid[r, :] += norm_back(dn, nrm, inv, g1[...].reshape(1, D))
        return 0
    lax.fori_loop(0, 3, ln1, 0)
    gtok = pltpu.make_async_copy(hid, gtok_h, osem)
    gtok.start()
    for t in range(28, CHUNKS + LAGS[5]):
        main.late(t)
    gtok.wait()

def backward(counts, raw, bitsT, wup, wdownT, g1, g2, mc, *arrays):
    T = 768
    any_, vm, sm = pl.BlockSpec(memory_space=pl.ANY), pl.BlockSpec(memory_space=pltpu.VMEM), pl.BlockSpec(memory_space=pltpu.SMEM)
    V, S = pltpu.VMEM, pltpu.SemaphoreType.DMA
    return pl.pallas_call(backward_kernel,
        out_shape=[jax.ShapeDtypeStruct(s, f32) for s in [(T, D), (1, 1), (CHUNKS, 24, W)]],
        in_specs=[sm] + [vm] * 7 + [any_] * 14,
        out_specs=[any_, sm, vm],
        scratch_shapes=[V((T, D), f32), V((D, D), bf16), V((D, FF), bf16), V((FF, D), bf16), V((2, 4, SEQ, SEQ), bf16),
            V((T, D), bf16), V((T, D), f32), V((T, D), bf16), V((T, FF), bf16), V((T, FF), bf16), V((D, T), bf16), V((D, T), bf16),
            V((T, D), bf16), V((T, 128), bf16), V((128, T), bf16), V((T, 128), f32), V((T, 128), f32),
            V((128, D), f32), V((128, D), bf16), V((128, D), f32), V((128, FF), f32), V((128, D), f32), V((8, 8, 128), f32), V((4, 8, 128), f32),
            S((13,)), S((10,)), S((10,)), S((2,)), S(())] + scatter_bufs(),
        compiler_params=pltpu.CompilerParams(vmem_limit_bytes=64 << 20, collective_id=1, has_side_effects=True),
        name="backward")(counts, raw, bitsT, wup, wdownT, g1, g2, mc, *arrays)

def finish_kernel(scale, gtok_i, loss_i, wqkv_h, win_h, grads, wdownT, g1, g2,
                  gtok_o, loss_o, gln1, gwqkv, gwao, gln2, gwin, gwout, gwdown, gwup, wq, wi, wide, held, sem):
    copy = pltpu.make_async_copy(gtok_i, held, sem.at[0])
    copy.start()
    me = lax.axis_index("dp") * lax.axis_size("replica") + lax.axis_index("replica")
    start = pl.multiple_of((me * 24) // 16 * 16, 16)
    reads = [pltpu.make_async_copy(h.at[pl.ds(start, 32)], v, sem.at[i]) for i, (h, v) in ((1, (wqkv_h, wq)), (2, (win_h, wi)))]
    for r in reads: r.start()
    loss_o[0, 0] = loss_i[0, 0]
    copy.wait()
    copy = pltpu.make_async_copy(held, gtok_o, sem.at[0])
    copy.start()
    for k in range(12):
        gwin[:, k * W:(k + 1) * W] = grads[k] * scale
    for g in range(3):
        gwao[:, g * W:(g + 1) * W] = grads[13 + 4 * g] * scale
        for j in range(3):
            gwqkv[:, j * D + g * W:j * D + (g + 1) * W] = grads[14 + 4 * g + j] * scale
    widen(wide, wdownT[...].astype(f32))
    wd = wide[...].astype(bf16)
    code, other = grads[12, :, :128] * scale, grads[12, :, 128:] * scale
    lane = lanes_of(24)
    for j in range(4):
        v = jnp.where(lane // 32 == j, code, 0.0)
        hi = v.astype(bf16)
        lo = (v - hi.astype(f32)).astype(bf16)
        gwout[24 * j:24 * j + 24, :] = dot(hi, wd) + dot(lo, wd)
    gwdown[...] = other[:, :BITS]
    for r in reads: r.wait()
    odd = me % 2
    def gain(weights, grad, lane_at, into):
        w = weights[...].astype(f32)
        w = jnp.where(odd == 1, w[8:32], w[0:24])
        return jnp.where(lane == lane_at, jnp.sum(w * grad[...], axis=1, keepdims=True), into)
    flat = gain(wi, gwin, 65, gain(wq, gwqkv, 64, other))
    turned = jnp.concatenate([flat, jnp.zeros((104, 128), f32)], axis=0).T
    gwup[...] = turned[32:32 + BITS, :24]
    def mine(g):
        rows = jnp.broadcast_to(g[...].reshape(1, D), (8, D))
        out = jnp.ones((8, 24), f32)
        for i in range(32):
            out = jnp.where(me == i, rows[:, 24 * i:24 * i + 24], out)
        return out[0:1]
    gln1[...] = (turned[64:65, :24] / mine(g1))
    gln2[...] = (turned[65:66, :24] / mine(g2))
    copy.wait()

def finish(scale, gtok, loss, wqkv, win, grads, wdownT, g1, g2):
    any_, vm, sm = pl.BlockSpec(memory_space=pl.ANY), pl.BlockSpec(memory_space=pltpu.VMEM), pl.BlockSpec(memory_space=pltpu.SMEM)
    shapes = [gtok.shape, (1, 1), (1, 24), (24, 3 * D), (24, D), (1, 24), (24, FF), (96, D), (24, BITS), (BITS, 24)]
    return pl.pallas_call(functools.partial(finish_kernel, scale),
        out_shape=[jax.ShapeDtypeStruct(s, f32) for s in shapes],
        in_specs=[any_, sm, any_, any_] + [vm] * 4,
        out_specs=[any_, sm] + [vm] * 8,
        scratch_shapes=[pltpu.VMEM((32, 3 * D), bf16), pltpu.VMEM((32, FF), bf16), pltpu.VMEM((128, D), f32), pltpu.VMEM(gtok.shape, f32), pltpu.SemaphoreType.DMA((3,))],
        name="finish")(gtok, loss, wqkv, win, grads, wdownT, g1, g2)

def kernel_body(tokens, counts, bits, outgrad, g1, wqkv, wao, g2, win, wout, wdown, wup):
    bitsT, wdownT = bits.T, wdown.T
    qkv, e, linv, ctx, hid, mlpin, act, slope, decoded, raw, mc = forward(counts, tokens, wqkv, wao, win, wout, g1, g2, wdownT, bitsT, wup)
    gtok, loss, grads = backward(counts, raw, bitsT, wup, wdownT, g1, g2, mc, tokens, outgrad, wqkv, wao, win, wout, qkv, e, linv, ctx, hid, mlpin, act, slope)
    scale = (tokens.shape[0] * lax.axis_size(("dp", "replica"))) ** -0.5
    gtok, loss, gln1, gwqkv, gwao, gln2, gwin, gwout, gwdown, gwup = finish(scale, gtok, loss, wqkv, win, grads, wdownT, g1, g2)
    return (decoded, loss.reshape(()), gtok, gln1.reshape(24), gwqkv, gwao, gln2.reshape(24), gwin, gwout, gwdown, gwup)

eps_norm = 1e-06
neg_big = -1e30
sharpness = 8.0
commit_weight = 0.25


def exact_gelu(values):
    return jax.nn.gelu(values, approximate=False)


def layer_norm(values, gain):
    centered = values - jnp.mean(values, axis=-1, keepdims=True)
    inv_std = lax.rsqrt(jnp.mean(centered * centered, axis=-1, keepdims=True) + eps_norm)
    normed = centered * inv_std
    return (normed * gain, normed, inv_std)


def plain_norm_back(grad_out, normed, inv_std, gain):
    grad_normed = grad_out * gain
    grad_gain = jnp.sum(grad_out * normed, axis=0)
    spread_part = jnp.mean(grad_normed * normed, axis=-1, keepdims=True)
    grad_in = inv_std * (
        grad_normed - jnp.mean(grad_normed, axis=-1, keepdims=True) - normed * spread_part
    )
    return (grad_in, grad_gain)


def inner_rows(left, right):
    return lax.dot_general(
        left, right, (((0,), (0,)), ((), ())), preferred_element_type=jnp.float32
    )


def times_transposed(left, right):
    return lax.dot_general(
        left, right, (((1,), (1,)), ((), ())), preferred_element_type=jnp.float32
    )


def attention_logits(queries, key_rows, key_valid):
    scores = jnp.einsum("bqhd,bkhd->bhqk", queries, key_rows, preferred_element_type=jnp.float32)
    return jnp.where(key_valid, scores * HEAD ** (-0.5), neg_big)


def plain_body(
    tokens,
    patch_counts,
    code_bits,
    out_grad,
    ln1_gain,
    w_qkv,
    w_attn_out,
    ln2_gain,
    w_mlp_in,
    w_mlp_out,
    w_down,
    w_up,
):
    row_count = tokens.shape[0]
    images = row_count // SEQ
    width_all = tokens.shape[1]
    first_image = lax.axis_index(("dp", "replica")) * images
    counts = lax.dynamic_slice_in_dim(patch_counts, first_image, images)
    total_count = jnp.sum(patch_counts).astype(jnp.float32)
    valid_slots = jnp.arange(SEQ, dtype=jnp.int32)[None, :] < counts[:, None]
    key_valid = valid_slots[:, None, None, :]
    row_valid = valid_slots.reshape(row_count).astype(jnp.float32)[:, None]
    target = (2.0 * code_bits.astype(jnp.float32) - 1.0) * BITS ** (-0.5)
    normed1_out, normed1, inv_std1 = layer_norm(tokens, ln1_gain)
    attn_in = normed1_out.astype(jnp.bfloat16)
    qkv_rows = jnp.dot(attn_in, w_qkv, preferred_element_type=jnp.float32).astype(jnp.bfloat16)
    qkv_rows = qkv_rows.reshape(images, SEQ, 3, HEADS, HEAD)
    queries = qkv_rows[:, :, 0]
    key_rows = qkv_rows[:, :, 1]
    value_rows = qkv_rows[:, :, 2]
    logits = attention_logits(queries, key_rows, key_valid)
    row_max = jnp.max(logits, axis=-1, keepdims=True)
    weights = jnp.exp(logits - row_max)
    row_total = jnp.sum(weights, axis=-1, keepdims=True)
    log_total = row_max + jnp.log(row_total)
    prob_low = (weights / row_total).astype(jnp.bfloat16)
    context = jnp.einsum(
        "bhqk,bkhd->bqhd", prob_low, value_rows, preferred_element_type=jnp.float32
    )
    context_low = context.astype(jnp.bfloat16).reshape(row_count, width_all)
    hidden1 = tokens + jnp.dot(context_low, w_attn_out, preferred_element_type=jnp.float32)
    normed2_out, normed2, inv_std2 = layer_norm(hidden1, ln2_gain)
    mlp_in = normed2_out.astype(jnp.bfloat16)
    pre_act = jnp.dot(mlp_in, w_mlp_in, preferred_element_type=jnp.float32)
    activation, gelu_back = jax.vjp(exact_gelu, pre_act)
    activation_low = activation.astype(jnp.bfloat16)
    hidden2 = hidden1 + jnp.dot(activation_low, w_mlp_out, preferred_element_type=jnp.float32)
    hidden2_low = hidden2.astype(jnp.bfloat16)
    raw_code = jnp.dot(hidden2_low, w_down, preferred_element_type=jnp.float32)
    inv_len = lax.rsqrt(jnp.sum(raw_code * raw_code, axis=-1, keepdims=True) + 1.0)
    unit_code = raw_code * inv_len
    quant_low = target.astype(jnp.bfloat16)
    decoded = row_valid * jnp.dot(quant_low, w_up, preferred_element_type=jnp.float32)
    logit_bits = unit_code * sharpness
    soft_prob = jax.nn.sigmoid(logit_bits)
    token_ent = jax.nn.softplus(logit_bits) - soft_prob * logit_bits
    code_miss = unit_code - target
    prob_sum = jnp.sum(soft_prob * row_valid, axis=0)
    ent_sum = jnp.sum(token_ent * row_valid)
    commit_sum = jnp.sum(code_miss * code_miss * row_valid)
    prob_sum, ent_sum, commit_sum = lax.psum((prob_sum, ent_sum, commit_sum), ("dp", "replica"))
    mean_prob = prob_sum / total_count
    code_ent = jnp.sum(
        -mean_prob * jnp.log(mean_prob) - (1.0 - mean_prob) * jnp.log(1.0 - mean_prob)
    )
    entropy_loss = (commit_weight * commit_sum + ent_sum) / total_count - code_ent
    grad_dec_low = (row_valid * out_grad).astype(jnp.bfloat16)
    grad_w_up = inner_rows(quant_low, grad_dec_low)
    grad_quant = times_transposed(grad_dec_low, w_up)
    prob_logit = jnp.log(mean_prob / (1.0 - mean_prob))
    loss_part = (
        sharpness * soft_prob * (1.0 - soft_prob) * (prob_logit - logit_bits)
        + 2.0 * commit_weight * code_miss
    )
    grad_unit = grad_quant + row_valid * loss_part
    grad_raw = inv_len * (
        grad_unit - unit_code * jnp.sum(grad_unit * unit_code, axis=-1, keepdims=True)
    )
    grad_raw_low = grad_raw.astype(jnp.bfloat16)
    grad_w_down = inner_rows(hidden2_low, grad_raw_low)
    grad_hidden2 = times_transposed(grad_raw_low, w_down)
    grad_mlp_low = grad_hidden2.astype(jnp.bfloat16)
    grad_w_mlp_out = inner_rows(activation_low, grad_mlp_low)
    grad_activation = times_transposed(grad_mlp_low, w_mlp_out)
    grad_pre_low = gelu_back(grad_activation)[0].astype(jnp.bfloat16)
    grad_w_mlp_in = inner_rows(mlp_in, grad_pre_low)
    grad_norm2_in = times_transposed(grad_pre_low, w_mlp_in)
    grad_from_norm2, grad_ln2 = plain_norm_back(grad_norm2_in, normed2, inv_std2, ln2_gain)
    grad_hidden1 = grad_hidden2 + grad_from_norm2
    grad_attn_low = grad_hidden1.astype(jnp.bfloat16)
    grad_w_attn_out = inner_rows(context_low, grad_attn_low)
    grad_context = times_transposed(grad_attn_low, w_attn_out).astype(jnp.bfloat16)
    grad_context = grad_context.reshape(images, SEQ, HEADS, HEAD)
    grad_values = jnp.einsum(
        "bhqk,bqhd->bkhd", prob_low, grad_context, preferred_element_type=jnp.float32
    )
    grad_prob = jnp.einsum(
        "bqhd,bkhd->bhqk", grad_context, value_rows, preferred_element_type=jnp.float32
    )
    attn_prob = jnp.exp(attention_logits(queries, key_rows, key_valid) - log_total)
    grad_scores = (
        attn_prob
        * (grad_prob - jnp.sum(grad_prob * attn_prob, axis=-1, keepdims=True))
        * HEAD ** (-0.5)
    )
    grad_scores_low = grad_scores.astype(jnp.bfloat16)
    grad_queries = jnp.einsum(
        "bhqk,bkhd->bqhd", grad_scores_low, key_rows, preferred_element_type=jnp.float32
    )
    grad_keys = jnp.einsum(
        "bhqk,bqhd->bkhd", grad_scores_low, queries, preferred_element_type=jnp.float32
    )
    grad_qkv = jnp.stack((grad_queries, grad_keys, grad_values), axis=2).reshape(
        row_count, 3 * width_all
    )
    grad_qkv_low = grad_qkv.astype(jnp.bfloat16)
    grad_w_qkv = inner_rows(attn_in, grad_qkv_low)
    grad_norm1_in = times_transposed(grad_qkv_low, w_qkv)
    grad_from_norm1, grad_ln1 = plain_norm_back(grad_norm1_in, normed1, inv_std1, ln1_gain)
    grad_tokens = grad_hidden1 + grad_from_norm1
    summed = (
        lax.psum_scatter(grad_ln1, ("dp", "replica"), scatter_dimension=0, tiled=True),
        lax.psum_scatter(grad_w_qkv, ("dp", "replica"), scatter_dimension=0, tiled=True),
        lax.psum_scatter(grad_w_attn_out, ("dp", "replica"), scatter_dimension=0, tiled=True),
        lax.psum_scatter(grad_ln2, ("dp", "replica"), scatter_dimension=0, tiled=True),
        lax.psum_scatter(grad_w_mlp_in, ("dp", "replica"), scatter_dimension=0, tiled=True),
        lax.psum_scatter(grad_w_mlp_out, ("dp", "replica"), scatter_dimension=0, tiled=True),
        lax.psum_scatter(grad_w_down, ("dp", "replica"), scatter_dimension=0, tiled=True),
        lax.psum_scatter(grad_w_up, ("dp", "replica"), scatter_dimension=1, tiled=True),
    )
    grad_scale = (row_count * lax.axis_size(("dp", "replica"))) ** (-0.5)
    return (
        decoded,
        entropy_loss,
        grad_tokens,
        summed[0] * grad_scale,
        summed[1] * grad_scale,
        summed[2] * grad_scale,
        summed[3] * grad_scale,
        summed[4] * grad_scale,
        summed[5] * grad_scale,
        summed[6] * grad_scale,
        summed[7] * grad_scale,
    )


def solution(mesh):
    in_specs = (
        P(("dp", "replica"), None),
        P(),
        P(("dp", "replica"), None),
        P(("dp", "replica"), None),
        P(),
        P(),
        P(),
        P(),
        P(),
        P(),
        P(),
        P(),
    )
    out_specs = (
        P(("dp", "replica"), None),
        P(),
        P(("dp", "replica"), None),
        P(("dp", "replica")),
        P(("dp", "replica"), None),
        P(("dp", "replica"), None),
        P(("dp", "replica")),
        P(("dp", "replica"), None),
        P(("dp", "replica"), None),
        P(("dp", "replica"), None),
        P(None, ("dp", "replica")),
    )
    body = kernel_body if (mesh.shape["dp"], mesh.shape["replica"]) == (8, 4) else plain_body
    return jax.shard_map(body, mesh=mesh, in_specs=in_specs, out_specs=out_specs, check_vma=False)
```

```python
import functools
import math

import jax
import jax.numpy as jnp
from jax import lax
from jax.experimental import pallas as pl
from jax.experimental.pallas import tpu as pltpu
from jax.sharding import PartitionSpec as P

HEADS, HEAD, BITS, SEQ = 12, 64, 18, 384
D, FF = 768, 3072
EPS = 1e-06
bf16, f32 = jnp.bfloat16, jnp.float32

def dot(a, b, ca=1, cb=0):
    return lax.dot_general(a, b, (((ca,), (cb,)), ((), ())), preferred_element_type=f32)

def norm_stats(v):
    mean = jnp.sum(v, axis=1, keepdims=True) * (1.0 / D)
    cen = v - mean
    var = jnp.sum(cen * cen, axis=1, keepdims=True) * (1.0 / D)
    inv = lax.rsqrt(var + EPS)
    return cen * inv, inv

def cols(i, n):
    return pl.ds(pl.multiple_of(i * n, n), n)

def lanes_of(rows, width=128):
    return lax.broadcasted_iota(jnp.int32, (rows, width), 1)

def widen(ref, rows):
    ref[...] = jnp.zeros_like(ref)
    for j in range(4):
        ref[32 * j:32 * j + BITS, :] = rows

def gelu_parts(x):
    cdf = 0.5 + 0.5 * lax.erf(x * math.sqrt(0.5))
    pdf = jnp.exp(x * x * -0.5) * (1.0 / math.sqrt(2.0 * math.pi))
    return x * cdf, cdf + x * pdf

MESH = pl.DeviceIdType.MESH
W = 256
CHUNKS = 25
LAGS = (0, 1, 6, 10, 13, 16)

def place():
    dp, rp = lax.axis_index("dp"), lax.axis_index("replica")
    return dp // 2, dp % 2, rp // 2, rp % 2

def device(z, x, y, c):
    return (z * 2 + x, y * 2 + c)

def near():
    z, x, y, c = place()
    flip = lambda v, n: 1 - v if n else v
    return [device(z, flip(x, n & 4), flip(y, n & 2), flip(c, n & 1)) for n in range(1, 8)]

def column():
    z, x, y, c = place()
    return [device((z + d) % 4, x, y, c) for d in (1, 2, 3)]

def arrive():
    for p in near() + column():
        pl.semaphore_signal(pltpu.get_barrier_semaphore(), inc=1, device_id=p, device_id_type=MESH)

def all_arrived():
    pl.semaphore_wait(pltpu.get_barrier_semaphore(), len(near() + column()))

def planar(k):
    if isinstance(k, int):
        return int((k % 3 if k <= 12 else (k + 3) % 4) == 0)
    return jnp.where(jnp.where(k <= 12, lax.rem(k, 3), lax.rem(k + 3, 4)) == 0, 1, 0)

class Scatter:
    def __init__(self, bufs, result):
        self.g, self.r, (self.send, self.recv) = bufs[0], bufs[1:6], bufs[6:8]
        self.result = result
        self.at = place()
    def route(self, k, h, n):
        z, x, y, c = self.at
        p, zl, zh = planar(k), z % 2, z // 2
        tz = [(z + 1 - 2 * zl, 1 - p), (z + 2 - 4 * zh, 1 - p)]
        first, other = (x, y) if h == 0 else (y, x)
        def to(flip_first, flip_other, nz):
            f, o = first + flip_first * (1 - 2 * first), other + flip_other * (1 - 2 * other)
            return device(nz, *((f, o) if h == 0 else (o, f)), c)
        lowz, highz = z + 1 - 2 * zl, z + 2 - 4 * zh
        if n == 1:
            return first, to(1, 0, z)
        if n == 2:
            return p * other + (1 - p) * zl, to(0, p, p * z + (1 - p) * lowz)
        if n == 3:
            return p * zl + (1 - p) * zh, to(0, 0, p * lowz + (1 - p) * highz)
        return p * zh + (1 - p) * other, to(0, 1 - p, p * highz + (1 - p) * z)
    def copy(self, k, h, n):
        _, to = self.route(k, h, n)
        bit = self.route(k, h, n)[0]
        i = 2 * n - 1 + h
        return pltpu.make_async_remote_copy(self.r[n - 1].at[k, h, 1 - bit], self.r[n].at[k, h], self.send.at[k, i], self.recv.at[k, i],
                                            device_id=to, device_id_type=MESH)
    def pair(self, k, slot):
        z, x, y, c = self.at
        return pltpu.make_async_remote_copy(self.g.at[slot, 1 - c], self.r[0].at[k], self.send.at[k, 0], self.recv.at[k, 0],
                                            device_id=device(z, x, y, 1 - c), device_id_type=MESH)
    def put(self, slot, p, v, h):
        for o in range(32):
            z, x, y, c = o // 8, o // 4 % 2, o // 2 % 2, o % 2
            f, s = (x, y) if h == 0 else (y, x)
            order = (f, s, z % 2, z // 2) if p else (f, z % 2, z // 2, s)
            self.g[(slot, c, h, *order)] = v[o * 24:o * 24 + 24]
    def kept(self, k, h, n):
        bit, _ = self.route(k, h, n)
        return jnp.where(bit == 0, self.r[n - 1][k, h, 0], self.r[n - 1][k, h, 1])
    def step(self, s, k):
        for h in range(2):
            self.copy(k, h, s - 1).wait()
            v = self.r[s - 1][k, h] + self.kept(k, h, s - 1)
            if s == 5:
                self.result(k, h, v)
            else:
                self.r[s - 1][k, h] = v
                self.copy(k, h, s).start()
    def begin(self, k, slot):
        self.pair(k, slot).start()
    def join(self, k, slot):
        self.pair(k, slot).wait()
        self.r[0][k] += self.g[slot, self.at[3]]
        for h in range(2):
            self.copy(k, h, 1).start()
    def late(self, t):
        for s in (5, 4, 3, 2):
            k = t - LAGS[s]
            if isinstance(t, int):
                if 0 <= k < CHUNKS:
                    self.step(s, k)
            else:
                pl.when(k >= 0)(functools.partial(self.step, s, k))
    def early(self, t, slot):
        k = t - 1
        if isinstance(t, int):
            if k >= 0:
                self.join(k, 1 - slot)
            if t < CHUNKS:
                self.begin(t, slot)
        else:
            pl.when(k >= 0)(functools.partial(self.join, k, 1 - slot))
            self.begin(t, slot)

def scatter_bufs():
    blocks = [(2,) * (5 - n) for n in range(5)]
    return [pltpu.VMEM((2, 2, 2, 2, 2, 2, 2, 24, 128), f32)] + [pltpu.VMEM((CHUNKS,) + b + (24, 128), f32) for b in blocks] + [pltpu.SemaphoreType.DMA((CHUNKS, 9))] * 2

def norm_back(grad, normed, inv, gain):
    gn = grad * gain
    spread = jnp.sum(gn * normed, axis=1, keepdims=True) * (1.0 / D)
    mean = jnp.sum(gn, axis=1, keepdims=True) * (1.0 / D)
    return inv * (gn - mean - normed * spread)

RB = 128
MC = 512
def train_kernel(counts, bitsT, wup, wdownT, g1, g2, tokens_h, outgrad_h, wqkv_h, wao_h, win_h, wout_h,
                 gtok_h, loss_o, grads_o, qkv_h, e_h, linv_h,
                 hid, big, win, wout, wao, e, ctx, mlpin, act, slope, mlpinT, ainT, dattn, draw, drawT, unit_s, target, raw, mc,
                 wide, wd4t, smallT, quantT, s8, zs, sem, osem, ssem, rsem, esem, *bufs):
    def result(k, h, v):
        grads_o[k, :, h * 128:(h + 1) * 128] = v
    main = Scatter(bufs, result)
    z, x, y, c = place()
    loads = {n: pltpu.make_async_copy(src, dst, sem.at[i]) for i, (n, src, dst) in enumerate((
        ("tokens", tokens_h, hid), ("wqkv", wqkv_h, win.at[:, :3 * D]), ("wao", wao_h, wao), ("win", win_h, win), ("wout", wout_h, wout),
        ("outgrad", outgrad_h, big), ("qkv", qkv_h, wout.at[:3 * D]), ("linv", linv_h, big), ("wqkv2", wqkv_h, win.at[:, :3 * D]), ("tokens2", tokens_h, big)))}
    saves = {n: pltpu.make_async_copy(src, dst, osem.at[i]) for i, (n, src, dst) in enumerate((
        ("qkv", wout.at[:3 * D], qkv_h), ("linv", big, linv_h), ("gtok", hid, gtok_h)))}
    def load_e(g, img):
        return pltpu.make_async_copy(e_h.at[pl.ds(img * HEADS + g * 4, 4)], e.at[img], esem.at[img])
    def save_e(g, img):
        return pltpu.make_async_copy(e.at[img], e_h.at[pl.ds(img * HEADS + g * 4, 4)], esem.at[2 + img])
    arrive()
    for n in ("tokens", "wqkv", "wao"):
        loads[n].start()
    first = (lax.axis_index("dp") * lax.axis_size("replica") + lax.axis_index("replica")) * 2
    n0, n1 = counts[first], counts[first + 1]
    total = lax.fori_loop(0, counts.shape[0], lambda i, a: a + counts[i], jnp.int32(0)).astype(f32)
    def live(i):
        row = lax.broadcasted_iota(jnp.int32, (RB, 128), 0) + i * RB
        return row < jnp.where(row < SEQ, n0, n1 + SEQ)
    low = lanes_of(SEQ) < HEAD
    widen(wide, wdownT[...].astype(f32))
    wd4t[...] = wide[...].astype(bf16)
    widen(wide, (2.0 * bitsT[...].astype(f32) - 1.0) * BITS ** -0.5)
    target[...] = wide[...].T
    loads["tokens"].wait()
    def fwd_ln1(i, _):
        r = cols(i, 128)
        n, _inv = norm_stats(hid[r, :])
        dattn[r, :] = (n * g1[...].reshape(1, D)).astype(bf16)
        return 0
    lax.fori_loop(0, 6, fwd_ln1, 0)
    loads["wqkv"].wait()
    def proj(i, _):
        v = dot(dattn[...], win[:, cols(i, 256)])
        v = v * jnp.where(i < 3, 0.125, 1.0)
        wout[pl.ds(pl.multiple_of(i // 3 * D, D), D), cols(i % 3, 256)] = v.astype(bf16)
        return 0
    lax.fori_loop(0, 9, proj, 0)
    loads["win"].start()
    saves["qkv"].start()
    def heads_of(img, o):
        return (wout[pl.ds(pl.multiple_of(b * D + img * SEQ, 128), SEQ), cols(o, 128)] for b in range(3))
    def att(g, _):
        def image(img, _):
            n = jnp.where(img == 0, n0, n1)
            r = pl.ds(pl.multiple_of(img * SEQ, SEQ), SEQ)
            ok = lax.broadcasted_iota(jnp.int32, (1, SEQ), 1) < n
            one = jnp.ones((SEQ, 128), bf16)
            @pl.when(g > 0)
            def _():
                save_e(g - 1, img).wait()
            for j in range(2):
                o = g * 2 + j
                q2, k2, v2 = heads_of(img, o)
                zero = jnp.zeros_like(q2)
                vo = jnp.concatenate([v2, one], axis=1)
                res = []
                for h in range(2):
                    q = jnp.where(low, q2, zero) if h == 0 else jnp.where(low, zero, q2)
                    s = jnp.where(ok, dot(q, k2, 1, 1), -1e30)
                    m = jnp.max(s, axis=1, keepdims=True)
                    p = jnp.exp(s - m).astype(bf16)
                    e[img, 2 * j + h] = p
                    ov = dot(p, vo)
                    inv = 1.0 / ov[:, 128:]
                    res.append((ov[:, :128] * inv, inv))
                ctx[r, cols(o, 128)] = jnp.where(low, res[0][0], res[1][0]).astype(bf16)
                big[r, cols(o, 128)] = jnp.where(low, res[0][1], res[1][1])
            save_e(g, img).start()
            return 0
        lax.fori_loop(0, 2, image, 0)
        return 0
    lax.fori_loop(0, 3, att, 0)
    saves["linv"].start()
    saves["qkv"].wait()
    loads["wout"].start()
    loads["wao"].wait()
    def ao(i, _):
        r = cols(i, 256)
        h = hid[r, :] + dot(ctx[r, :], wao[...])
        hid[r, :] = h
        n, _inv = norm_stats(h)
        mlpin[r, :] = (n * g2[...].reshape(1, D)).astype(bf16)
        return 0
    lax.fori_loop(0, 3, ao, 0)
    saves["linv"].wait()
    loads["outgrad"].start()
    loads["wout"].wait()
    def mcf(i, _):
        r = cols(i, 768)
        v = dot(wout[r, :], wd4t[...], 1, 1)
        hi = v.astype(bf16).astype(f32)
        mc[r, :] = jnp.where(lanes_of(768) % 64 < 32, hi, v - hi).astype(bf16)
        return 0
    lax.fori_loop(0, 4, mcf, 0)
    loads["win"].wait()
    for img in range(2):
        save_e(2, img).wait()
        load_e(0, img).start()
    def fwd_mlp(i, _):
        cs = cols(i, MC)
        a, s = gelu_parts(dot(mlpin[...], win[:, cs]))
        act[:, cs] = a.astype(bf16)
        slope[:, cs] = s.astype(bf16)
        return 0
    lax.fori_loop(0, FF // MC, fwd_mlp, 0)
    rawv = dot(act[...], mc[...])
    raw[...] = rawv + pltpu.roll(rawv, 32, 1) + dot(hid[...].astype(bf16), wd4t[...], 1, 1)
    all_arrived()
    def codes(i):
        r = cols(i, RB)
        rawv = raw[r, :]
        inv_len = lax.rsqrt(jnp.sum(rawv * rawv, axis=1, keepdims=True) * 0.25 + 1.0)
        both = jnp.where(live(i) & (lanes_of(RB) % 32 < BITS), 1.0, 0.0)
        return r, inv_len, rawv * inv_len, both
    def count(i, sums):
        r, inv_len, unit, both = codes(i)
        zl = unit * 8.0
        p = jax.nn.sigmoid(zl)
        miss = unit - target[r, :]
        ent = jnp.maximum(zl, 0.0) + jnp.log1p(jnp.exp(-jnp.abs(zl))) - p * zl
        return tuple(s + jnp.sum(v * both, axis=0, keepdims=True) for s, v in zip(sums, (p, ent, miss * miss)))
    sums = lax.fori_loop(0, 768 // RB, count, (jnp.zeros((1, 128), f32),) * 3)
    rows8 = lax.broadcasted_iota(jnp.int32, (8, 128), 0)
    own = x * 4 + y * 2 + c
    s8[own] = jnp.where(rows8 == 0, sums[0], jnp.where(rows8 == 1, sums[1], jnp.where(rows8 == 2, sums[2], 0.0)))
    def tell(ref, slot, i, to):
        return pltpu.make_async_remote_copy(ref.at[slot], ref.at[slot], ssem.at[i], rsem.at[i], device_id=to, device_id_type=MESH)
    tells = [tell(s8, own, i, p) for i, p in enumerate(near())]
    for t in tells: t.start()
    loads["outgrad"].wait()
    def decode(i, _):
        r = cols(i, RB)
        ok = live(i)
        for j in range(6):
            cs = slice(j * 128, (j + 1) * 128)
            dattn[r, cs] = jnp.where(ok, big[r, cs], 0.0).astype(bf16)
        return 0
    lax.fori_loop(0, 768 // RB, decode, 0)
    quantT[...] = dot(target[...].astype(bf16), dattn[...], 0, 0)
    for t in tells: t.wait_recv()
    s = s8[0]
    for i in range(1, 8):
        s = s + s8[i]
    zs[z] = s
    ztells = [tell(zs, z, 7 + i, p) for i, p in enumerate(column())]
    for t in ztells: t.start()
    for t in tells: t.wait_send()
    widen(wide, wup[...].astype(f32))
    unit_s[...] = dot(dattn[...], wide[...].astype(bf16), 1, 1)
    mlpinT[...] = mlpin[...].T
    for t in ztells: t.wait()
    zsum = zs[0] + zs[1] + zs[2] + zs[3]
    bit8 = lanes_of(8) % 32 < BITS
    mean_prob = jnp.where(bit8, zsum / total, 0.5)[0:1]
    odds = jnp.log(mean_prob / (1.0 - mean_prob))
    g0 = lanes_of(8)[0:1] < BITS
    code_ent = jnp.sum(jnp.where(g0, -mean_prob * jnp.log(mean_prob) - (1.0 - mean_prob) * jnp.log(1.0 - mean_prob), 0.0))
    other = jnp.sum(jnp.where(g0, 0.25 * zsum[2:3] + zsum[1:2], 0.0))
    loss_o[0, 0] = other / total - code_ent
    def unit_back(i, _):
        r, inv_len, unit, both = codes(i)
        zl = unit * 8.0
        p = jax.nn.sigmoid(zl)
        gunit = unit_s[r, :] + both * (8.0 * p * (1.0 - p) * (odds - zl) + 0.5 * (unit - target[r, :]))
        graw = inv_len * (gunit - unit * (jnp.sum(gunit * unit, axis=1, keepdims=True) * 0.25))
        draw[r, :] = graw.astype(bf16)
        return 0
    lax.fori_loop(0, 768 // RB, unit_back, 0)
    def put(t, p, v):
        for h in range(2):
            main.put(t % 2, p, v[:, h * 128:(h + 1) * 128], h)
    def mlp(i, _):
        for j in range(6):
            t = 6 * i + j
            cs = cols(t, W)
            d = dot(draw[...], mc[cs, :], 1, 1) * 0.5
            dp = (slope[:, cs].astype(f32) * d).astype(bf16)
            slope[:, cs] = dp
            main.late(t)
            put(j, planar(j), dot(mlpinT[...], dp))
            main.early(t, j % 2)
        return 0
    lax.fori_loop(0, 2, mlp, 0)
    main.late(12)
    drawT[...] = draw[...].T
    for q in range(4):
        big[128 * q:128 * q + 128, :] = dot(drawT[...], act[:, q * D:(q + 1) * D])
    for b in range(8):
        t = big[b // 2 * 128:b // 2 * 128 + 128, b % 2 * 384:b % 2 * 384 + 384].T.reshape(4, 4, 24, 128)
        l4 = lax.broadcasted_iota(jnp.int32, (4, 24, 128), 2) // 32
        s = jnp.where(l4 == 0, t[:, 0], 0.0)
        for j in range(1, 4):
            s = jnp.where(l4 == j, t[:, j], s)
        unit_s[b * 96:(b + 1) * 96, :] = s.reshape(96, 128)
    main.put(0, 1, unit_s[...], 0)
    gwd = dot(drawT[...], hid[...].astype(bf16))
    for q in range(4):
        gv = big[128 * q:128 * q + 128, :]
        hi = gv.astype(bf16)
        lo = (gv - hi.astype(f32)).astype(bf16)
        w = wout[q * D:(q + 1) * D, :]
        gwd = gwd + (dot(hi, w) + dot(lo, w))
    r128 = lax.broadcasted_iota(jnp.int32, (128, D), 0)
    smallT[...] = jnp.where(r128 < 32, gwd, quantT[...])
    for i in range(6):
        unit_s[i * 128:(i + 1) * 128, :] = smallT[:, i * 128:(i + 1) * 128].T
    main.put(0, 1, unit_s[...], 1)
    main.early(12, 0)
    loads["linv"].start()
    loads["qkv"].start()
    main.late(13)
    def ln2(i, _):
        r = cols(i, 256)
        dn = dot(slope[r, :], win[...], 1, 1)
        nrm, inv = norm_stats(hid[r, :])
        v = norm_back(dn, nrm, inv, g2[...].reshape(1, D)) + dot(draw[r, :], wd4t[...]) * 0.25
        hid[r, :] = v
        dattn[r, :] = v.astype(bf16)
        return 0
    lax.fori_loop(0, 3, ln2, 0)
    loads["wqkv2"].start()
    loads["linv"].wait()
    mlpinT[...] = ctx[...].T
    def dctx(i, _):
        r = cols(i, 256)
        mlpin[r, :] = (dot(dattn[r, :], wao[...], 1, 1) * big[r, :]).astype(bf16)
        return 0
    lax.fori_loop(0, 3, dctx, 0)
    loads["tokens2"].start()
    loads["qkv"].wait()
    loads["tokens2"].wait()
    for i in range(6):
        r = pl.ds(i * 128, 128)
        nrm, inv = norm_stats(big[r, :])
        ainT[:, i * 128:(i + 1) * 128] = (nrm * g1[...].reshape(1, D)).astype(bf16).T
    def group(g, _):
        t0 = 13 + 4 * g
        main.late(t0 + 1)
        put(1, 1, dot(mlpinT[...], dattn[:, cols(g, W)]))
        main.early(t0, 1)
        def image(img, _):
            load_e(g, img).wait()
            r = pl.ds(pl.multiple_of(img * SEQ, SEQ), SEQ)
            for j in range(2):
                o = g * 2 + j
                q2, k2, v2 = heads_of(img, o)
                cs = cols(o, 128)
                d2, c2 = mlpin[r, cs], ctx[r, cs]
                prod = d2.astype(f32) * c2.astype(f32)
                zero_ = jnp.zeros_like(q2)
                dq = dk = dv = None
                for h in range(2):
                    mine = low if h == 0 else jnp.logical_not(low)
                    pick = lambda a: jnp.where(mine, a, zero_)
                    dh = pick(d2)
                    ev = e[img, 2 * j + h]
                    dd = jnp.sum(jnp.where(mine, prod, 0.0), axis=1, keepdims=True)
                    ds = (ev.astype(f32) * (dot(dh, v2, 1, 1) - dd)).astype(bf16)
                    a, b, cc = dot(ds, pick(k2)), dot(ds, pick(q2), 0, 0), dot(ev, dh, 0, 0)
                    dq, dk, dv = (a, b, cc) if h == 0 else (dq + a, dk + b, dv + cc)
                for b, v in enumerate((dq * 0.125, dk, dv)):
                    act[r, pl.ds(pl.multiple_of(b * D + o * 128, 128), 128)] = v.astype(bf16)
            @pl.when(g < 2)
            def _():
                load_e(g + 1, img).start()
            main.late(t0 + 2 + img)
            return 0
        lax.fori_loop(0, 2, image, 0)
        for j in range(3):
            put(j, 0, dot(ainT[...], act[:, pl.ds(pl.multiple_of(j * D + g * W, W), W)]))
            main.early(t0 + 1 + j, j % 2)
            if j == 1:
                main.late(t0 + 4)
        return 0
    lax.fori_loop(0, 3, group, 0)
    main.early(25, 1)
    main.late(26)
    loads["wqkv2"].wait()
    def ln1(i, _):
        r = cols(i, 256)
        dn = dot(act[r, :3 * D], win[:, :3 * D], 1, 1)
        nrm, inv = norm_stats(big[r, :])
        hid[r, :] += norm_back(dn, nrm, inv, g1[...].reshape(1, D))
        return 0
    lax.fori_loop(0, 3, ln1, 0)
    saves["gtok"].start()
    for t in range(27, CHUNKS + LAGS[5]):
        main.late(t)
    saves["gtok"].wait()

def train(*args):
    T = 768
    any_, vm, sm = pl.BlockSpec(memory_space=pl.ANY), pl.BlockSpec(memory_space=pltpu.VMEM), pl.BlockSpec(memory_space=pltpu.SMEM)
    V, S = pltpu.VMEM, pltpu.SemaphoreType.DMA
    shapes = [((T, D), f32), ((1, 1), f32), ((CHUNKS, 24, W), f32), ((3 * T, D), bf16), ((24, SEQ, SEQ), bf16), ((T, D), f32)]
    return pl.pallas_call(train_kernel,
        out_shape=[jax.ShapeDtypeStruct(*s) for s in shapes],
        in_specs=[sm] + [vm] * 5 + [any_] * 6,
        out_specs=[any_, sm, vm] + [any_] * 3,
        scratch_shapes=[V((T, D), f32), V((T, D), f32), V((D, FF), bf16), V((FF, D), bf16), V((D, D), bf16), V((2, 4, SEQ, SEQ), bf16),
            V((T, D), bf16), V((T, D), bf16), V((T, FF), bf16), V((T, FF), bf16), V((D, T), bf16), V((D, T), bf16), V((T, D), bf16),
            V((T, 128), bf16), V((128, T), bf16), V((T, 128), f32), V((T, 128), f32), V((T, 128), f32), V((FF, 128), bf16),
            V((128, D), f32), V((128, D), bf16), V((128, D), f32), V((128, D), f32), V((8, 8, 128), f32), V((4, 8, 128), f32),
            S((10,)), S((3,)), S((10,)), S((10,)), S((4,))] + scatter_bufs(),
        compiler_params=pltpu.CompilerParams(vmem_limit_bytes=64 << 20, collective_id=1, has_side_effects=True),
        name="train")(*args)

PIECES = 4
def finish_kernel(scale, counts, gtok_i, loss_i, wqkv_h, win_h, grads, wdownT, g1, g2, bitsT, wup,
                  dec_h, gtok_o, loss_o, gln1, gwqkv, gwao, gln2, gwin, gwout, gwdown, gwup, wq, wi, wide, held, dec, sem, csem):
    part = lambda i: pl.ds(i * (768 // PIECES), 768 // PIECES)
    take = [pltpu.make_async_copy(gtok_i.at[part(i)], held.at[part(i)], csem.at[0, i]) for i in range(PIECES)]
    give = [pltpu.make_async_copy(held.at[part(i)], gtok_o.at[part(i)], csem.at[1, i]) for i in range(PIECES)]
    show = [pltpu.make_async_copy(dec.at[part(i)], dec_h.at[part(i)], csem.at[2, i]) for i in range(PIECES)]
    for t in take: t.start()
    me = lax.axis_index("dp") * lax.axis_size("replica") + lax.axis_index("replica")
    start = pl.multiple_of((me * 24) // 16 * 16, 16)
    reads = [pltpu.make_async_copy(h.at[pl.ds(start, 32)], v, sem.at[i]) for i, (h, v) in ((0, (wqkv_h, wq)), (1, (win_h, wi)))]
    for r in reads: r.start()
    loss_o[0, 0] = loss_i[0, 0]
    n0, n1 = counts[2 * me], counts[2 * me + 1]
    widen(wide, wup[...].astype(f32))
    up = wide[...].astype(bf16)
    widen(wide, (2.0 * bitsT[...].astype(f32) - 1.0) * BITS ** -0.5)
    target = (wide[...].T * 0.25).astype(bf16)
    rows = 768 // PIECES
    for i in range(PIECES):
        row = lax.broadcasted_iota(jnp.int32, (rows, D), 0) + i * rows
        live = row < jnp.where(row < SEQ, n0, n1 + SEQ)
        dec[part(i), :] = jnp.where(live, dot(target[i * rows:(i + 1) * rows], up), 0.0)
        show[i].start()
        take[i].wait()
        give[i].start()
    for k in range(12):
        gwin[:, k * W:(k + 1) * W] = grads[k] * scale
    for g in range(3):
        gwao[:, g * W:(g + 1) * W] = grads[13 + 4 * g] * scale
        for j in range(3):
            gwqkv[:, j * D + g * W:j * D + (g + 1) * W] = grads[14 + 4 * g + j] * scale
    widen(wide, wdownT[...].astype(f32))
    wd = wide[...].astype(bf16)
    code, other = grads[12, :, :128] * scale, grads[12, :, 128:] * scale
    lane = lanes_of(24)
    for j in range(4):
        v = jnp.where(lane // 32 == j, code, 0.0)
        hi = v.astype(bf16)
        lo = (v - hi.astype(f32)).astype(bf16)
        gwout[24 * j:24 * j + 24, :] = dot(hi, wd) + dot(lo, wd)
    gwdown[...] = other[:, :BITS]
    for r in reads: r.wait()
    odd = me % 2
    def gain(weights, grad, lane_at, into):
        w = weights[...].astype(f32)
        w = jnp.where(odd == 1, w[8:32], w[0:24])
        return jnp.where(lane == lane_at, jnp.sum(w * grad[...], axis=1, keepdims=True), into)
    flat = gain(wi, gwin, 65, gain(wq, gwqkv, 64, other))
    turned = jnp.concatenate([flat, jnp.zeros((104, 128), f32)], axis=0).T
    gwup[...] = turned[32:32 + BITS, :24]
    def mine(g):
        rows = jnp.broadcast_to(g[...].reshape(1, D), (8, D))
        out = jnp.ones((8, 24), f32)
        for i in range(32):
            out = jnp.where(me == i, rows[:, 24 * i:24 * i + 24], out)
        return out[0:1]
    gln1[...] = (turned[64:65, :24] / mine(g1))
    gln2[...] = (turned[65:66, :24] / mine(g2))
    for t in give + show: t.wait()

def finish(scale, counts, gtok, *rest):
    any_, vm, sm = pl.BlockSpec(memory_space=pl.ANY), pl.BlockSpec(memory_space=pltpu.VMEM), pl.BlockSpec(memory_space=pltpu.SMEM)
    shapes = [gtok.shape, gtok.shape, (1, 1), (1, 24), (24, 3 * D), (24, D), (1, 24), (24, FF), (96, D), (24, BITS), (BITS, 24)]
    return pl.pallas_call(functools.partial(finish_kernel, scale),
        out_shape=[jax.ShapeDtypeStruct(s, f32) for s in shapes],
        in_specs=[sm, any_, sm, any_, any_] + [vm] * 6,
        out_specs=[any_, any_, sm] + [vm] * 8,
        scratch_shapes=[pltpu.VMEM((32, 3 * D), bf16), pltpu.VMEM((32, FF), bf16), pltpu.VMEM((128, D), f32), pltpu.VMEM(gtok.shape, f32), pltpu.VMEM(gtok.shape, f32),
            pltpu.SemaphoreType.DMA((2,)), pltpu.SemaphoreType.DMA((3, PIECES))],
        name="finish")(counts, gtok, *rest)

def kernel_body(tokens, counts, bits, outgrad, g1, wqkv, wao, g2, win, wout, wdown, wup):
    bitsT, wdownT = bits.T, wdown.T
    gtok, loss, grads = train(counts, bitsT, wup, wdownT, g1, g2, tokens, outgrad, wqkv, wao, win, wout)[:3]
    scale = (tokens.shape[0] * lax.axis_size(("dp", "replica"))) ** -0.5
    decoded, gtok, loss, gln1, gwqkv, gwao, gln2, gwin, gwout, gwdown, gwup = finish(scale, counts, gtok, loss, wqkv, win, grads, wdownT, g1, g2, bitsT, wup)
    return (decoded, loss.reshape(()), gtok, gln1.reshape(24), gwqkv, gwao, gln2.reshape(24), gwin, gwout, gwdown, gwup)

eps_norm = 1e-06
neg_big = -1e30
sharpness = 8.0
commit_weight = 0.25


def exact_gelu(values):
    return jax.nn.gelu(values, approximate=False)


def layer_norm(values, gain):
    centered = values - jnp.mean(values, axis=-1, keepdims=True)
    inv_std = lax.rsqrt(jnp.mean(centered * centered, axis=-1, keepdims=True) + eps_norm)
    normed = centered * inv_std
    return (normed * gain, normed, inv_std)


def plain_norm_back(grad_out, normed, inv_std, gain):
    grad_normed = grad_out * gain
    grad_gain = jnp.sum(grad_out * normed, axis=0)
    spread_part = jnp.mean(grad_normed * normed, axis=-1, keepdims=True)
    grad_in = inv_std * (
        grad_normed - jnp.mean(grad_normed, axis=-1, keepdims=True) - normed * spread_part
    )
    return (grad_in, grad_gain)


def inner_rows(left, right):
    return lax.dot_general(
        left, right, (((0,), (0,)), ((), ())), preferred_element_type=jnp.float32
    )


def times_transposed(left, right):
    return lax.dot_general(
        left, right, (((1,), (1,)), ((), ())), preferred_element_type=jnp.float32
    )


def attention_logits(queries, key_rows, key_valid):
    scores = jnp.einsum("bqhd,bkhd->bhqk", queries, key_rows, preferred_element_type=jnp.float32)
    return jnp.where(key_valid, scores * HEAD ** (-0.5), neg_big)


def plain_body(
    tokens,
    patch_counts,
    code_bits,
    out_grad,
    ln1_gain,
    w_qkv,
    w_attn_out,
    ln2_gain,
    w_mlp_in,
    w_mlp_out,
    w_down,
    w_up,
):
    row_count = tokens.shape[0]
    images = row_count // SEQ
    width_all = tokens.shape[1]
    first_image = lax.axis_index(("dp", "replica")) * images
    counts = lax.dynamic_slice_in_dim(patch_counts, first_image, images)
    total_count = jnp.sum(patch_counts).astype(jnp.float32)
    valid_slots = jnp.arange(SEQ, dtype=jnp.int32)[None, :] < counts[:, None]
    key_valid = valid_slots[:, None, None, :]
    row_valid = valid_slots.reshape(row_count).astype(jnp.float32)[:, None]
    target = (2.0 * code_bits.astype(jnp.float32) - 1.0) * BITS ** (-0.5)
    normed1_out, normed1, inv_std1 = layer_norm(tokens, ln1_gain)
    attn_in = normed1_out.astype(jnp.bfloat16)
    qkv_rows = jnp.dot(attn_in, w_qkv, preferred_element_type=jnp.float32).astype(jnp.bfloat16)
    qkv_rows = qkv_rows.reshape(images, SEQ, 3, HEADS, HEAD)
    queries = qkv_rows[:, :, 0]
    key_rows = qkv_rows[:, :, 1]
    value_rows = qkv_rows[:, :, 2]
    logits = attention_logits(queries, key_rows, key_valid)
    row_max = jnp.max(logits, axis=-1, keepdims=True)
    weights = jnp.exp(logits - row_max)
    row_total = jnp.sum(weights, axis=-1, keepdims=True)
    log_total = row_max + jnp.log(row_total)
    prob_low = (weights / row_total).astype(jnp.bfloat16)
    context = jnp.einsum(
        "bhqk,bkhd->bqhd", prob_low, value_rows, preferred_element_type=jnp.float32
    )
    context_low = context.astype(jnp.bfloat16).reshape(row_count, width_all)
    hidden1 = tokens + jnp.dot(context_low, w_attn_out, preferred_element_type=jnp.float32)
    normed2_out, normed2, inv_std2 = layer_norm(hidden1, ln2_gain)
    mlp_in = normed2_out.astype(jnp.bfloat16)
    pre_act = jnp.dot(mlp_in, w_mlp_in, preferred_element_type=jnp.float32)
    activation, gelu_back = jax.vjp(exact_gelu, pre_act)
    activation_low = activation.astype(jnp.bfloat16)
    hidden2 = hidden1 + jnp.dot(activation_low, w_mlp_out, preferred_element_type=jnp.float32)
    hidden2_low = hidden2.astype(jnp.bfloat16)
    raw_code = jnp.dot(hidden2_low, w_down, preferred_element_type=jnp.float32)
    inv_len = lax.rsqrt(jnp.sum(raw_code * raw_code, axis=-1, keepdims=True) + 1.0)
    unit_code = raw_code * inv_len
    quant_low = target.astype(jnp.bfloat16)
    decoded = row_valid * jnp.dot(quant_low, w_up, preferred_element_type=jnp.float32)
    logit_bits = unit_code * sharpness
    soft_prob = jax.nn.sigmoid(logit_bits)
    token_ent = jax.nn.softplus(logit_bits) - soft_prob * logit_bits
    code_miss = unit_code - target
    prob_sum = jnp.sum(soft_prob * row_valid, axis=0)
    ent_sum = jnp.sum(token_ent * row_valid)
    commit_sum = jnp.sum(code_miss * code_miss * row_valid)
    prob_sum, ent_sum, commit_sum = lax.psum((prob_sum, ent_sum, commit_sum), ("dp", "replica"))
    mean_prob = prob_sum / total_count
    code_ent = jnp.sum(
        -mean_prob * jnp.log(mean_prob) - (1.0 - mean_prob) * jnp.log(1.0 - mean_prob)
    )
    entropy_loss = (commit_weight * commit_sum + ent_sum) / total_count - code_ent
    grad_dec_low = (row_valid * out_grad).astype(jnp.bfloat16)
    grad_w_up = inner_rows(quant_low, grad_dec_low)
    grad_quant = times_transposed(grad_dec_low, w_up)
    prob_logit = jnp.log(mean_prob / (1.0 - mean_prob))
    loss_part = (
        sharpness * soft_prob * (1.0 - soft_prob) * (prob_logit - logit_bits)
        + 2.0 * commit_weight * code_miss
    )
    grad_unit = grad_quant + row_valid * loss_part
    grad_raw = inv_len * (
        grad_unit - unit_code * jnp.sum(grad_unit * unit_code, axis=-1, keepdims=True)
    )
    grad_raw_low = grad_raw.astype(jnp.bfloat16)
    grad_w_down = inner_rows(hidden2_low, grad_raw_low)
    grad_hidden2 = times_transposed(grad_raw_low, w_down)
    grad_mlp_low = grad_hidden2.astype(jnp.bfloat16)
    grad_w_mlp_out = inner_rows(activation_low, grad_mlp_low)
    grad_activation = times_transposed(grad_mlp_low, w_mlp_out)
    grad_pre_low = gelu_back(grad_activation)[0].astype(jnp.bfloat16)
    grad_w_mlp_in = inner_rows(mlp_in, grad_pre_low)
    grad_norm2_in = times_transposed(grad_pre_low, w_mlp_in)
    grad_from_norm2, grad_ln2 = plain_norm_back(grad_norm2_in, normed2, inv_std2, ln2_gain)
    grad_hidden1 = grad_hidden2 + grad_from_norm2
    grad_attn_low = grad_hidden1.astype(jnp.bfloat16)
    grad_w_attn_out = inner_rows(context_low, grad_attn_low)
    grad_context = times_transposed(grad_attn_low, w_attn_out).astype(jnp.bfloat16)
    grad_context = grad_context.reshape(images, SEQ, HEADS, HEAD)
    grad_values = jnp.einsum(
        "bhqk,bqhd->bkhd", prob_low, grad_context, preferred_element_type=jnp.float32
    )
    grad_prob = jnp.einsum(
        "bqhd,bkhd->bhqk", grad_context, value_rows, preferred_element_type=jnp.float32
    )
    attn_prob = jnp.exp(attention_logits(queries, key_rows, key_valid) - log_total)
    grad_scores = (
        attn_prob
        * (grad_prob - jnp.sum(grad_prob * attn_prob, axis=-1, keepdims=True))
        * HEAD ** (-0.5)
    )
    grad_scores_low = grad_scores.astype(jnp.bfloat16)
    grad_queries = jnp.einsum(
        "bhqk,bkhd->bqhd", grad_scores_low, key_rows, preferred_element_type=jnp.float32
    )
    grad_keys = jnp.einsum(
        "bhqk,bqhd->bkhd", grad_scores_low, queries, preferred_element_type=jnp.float32
    )
    grad_qkv = jnp.stack((grad_queries, grad_keys, grad_values), axis=2).reshape(
        row_count, 3 * width_all
    )
    grad_qkv_low = grad_qkv.astype(jnp.bfloat16)
    grad_w_qkv = inner_rows(attn_in, grad_qkv_low)
    grad_norm1_in = times_transposed(grad_qkv_low, w_qkv)
    grad_from_norm1, grad_ln1 = plain_norm_back(grad_norm1_in, normed1, inv_std1, ln1_gain)
    grad_tokens = grad_hidden1 + grad_from_norm1
    summed = (
        lax.psum_scatter(grad_ln1, ("dp", "replica"), scatter_dimension=0, tiled=True),
        lax.psum_scatter(grad_w_qkv, ("dp", "replica"), scatter_dimension=0, tiled=True),
        lax.psum_scatter(grad_w_attn_out, ("dp", "replica"), scatter_dimension=0, tiled=True),
        lax.psum_scatter(grad_ln2, ("dp", "replica"), scatter_dimension=0, tiled=True),
        lax.psum_scatter(grad_w_mlp_in, ("dp", "replica"), scatter_dimension=0, tiled=True),
        lax.psum_scatter(grad_w_mlp_out, ("dp", "replica"), scatter_dimension=0, tiled=True),
        lax.psum_scatter(grad_w_down, ("dp", "replica"), scatter_dimension=0, tiled=True),
        lax.psum_scatter(grad_w_up, ("dp", "replica"), scatter_dimension=1, tiled=True),
    )
    grad_scale = (row_count * lax.axis_size(("dp", "replica"))) ** (-0.5)
    return (
        decoded,
        entropy_loss,
        grad_tokens,
        summed[0] * grad_scale,
        summed[1] * grad_scale,
        summed[2] * grad_scale,
        summed[3] * grad_scale,
        summed[4] * grad_scale,
        summed[5] * grad_scale,
        summed[6] * grad_scale,
        summed[7] * grad_scale,
    )


def solution(mesh):
    in_specs = (
        P(("dp", "replica"), None),
        P(),
        P(("dp", "replica"), None),
        P(("dp", "replica"), None),
        P(),
        P(),
        P(),
        P(),
        P(),
        P(),
        P(),
        P(),
    )
    out_specs = (
        P(("dp", "replica"), None),
        P(),
        P(("dp", "replica"), None),
        P(("dp", "replica")),
        P(("dp", "replica"), None),
        P(("dp", "replica"), None),
        P(("dp", "replica")),
        P(("dp", "replica"), None),
        P(("dp", "replica"), None),
        P(("dp", "replica"), None),
        P(None, ("dp", "replica")),
    )
    body = kernel_body if (mesh.shape["dp"], mesh.shape["replica"]) == (8, 4) else plain_body
    return jax.shard_map(body, mesh=mesh, in_specs=in_specs, out_specs=out_specs, check_vma=False)
```

```python
import functools
import math

import jax
import jax.numpy as jnp
from jax import lax
from jax.experimental import pallas as pl
from jax.experimental.pallas import tpu as pltpu
from jax.sharding import PartitionSpec as P

HEADS, HEAD, BITS, SEQ = 12, 64, 18, 384
D, FF = 768, 3072
EPS = 1e-06
bf16, f32 = jnp.bfloat16, jnp.float32

def dot(a, b, ca=1, cb=0):
    return lax.dot_general(a, b, (((ca,), (cb,)), ((), ())), preferred_element_type=f32)

def norm_stats(v):
    mean = jnp.sum(v, axis=1, keepdims=True) * (1.0 / D)
    cen = v - mean
    var = jnp.sum(cen * cen, axis=1, keepdims=True) * (1.0 / D)
    inv = lax.rsqrt(var + EPS)
    return cen * inv, inv

def cols(i, n):
    return pl.ds(pl.multiple_of(i * n, n), n)

def lanes_of(rows, width=128):
    return lax.broadcasted_iota(jnp.int32, (rows, width), 1)

def widen(ref, rows):
    ref[...] = jnp.zeros_like(ref)
    for j in range(4):
        ref[32 * j:32 * j + BITS, :] = rows

def gelu_parts(x):
    cdf = 0.5 + 0.5 * lax.erf(x * math.sqrt(0.5))
    pdf = jnp.exp(x * x * -0.5) * (1.0 / math.sqrt(2.0 * math.pi))
    return x * cdf, cdf + x * pdf

MESH = pl.DeviceIdType.MESH
W = 256
CHUNKS = 25
LAGS = (0, 1, 6, 10, 13, 16)

def place():
    dp, rp = lax.axis_index("dp"), lax.axis_index("replica")
    return dp // 2, dp % 2, rp // 2, rp % 2

def device(z, x, y, c):
    return (z * 2 + x, y * 2 + c)

def near():
    z, x, y, c = place()
    flip = lambda v, n: 1 - v if n else v
    return [device(z, flip(x, n & 4), flip(y, n & 2), flip(c, n & 1)) for n in range(1, 8)]

def column():
    z, x, y, c = place()
    return [device((z + d) % 4, x, y, c) for d in (1, 2, 3)]

def arrive():
    for p in near() + column():
        pl.semaphore_signal(pltpu.get_barrier_semaphore(), inc=1, device_id=p, device_id_type=MESH)

def all_arrived():
    pl.semaphore_wait(pltpu.get_barrier_semaphore(), len(near() + column()))

def planar(k):
    if isinstance(k, int):
        return int(k >= 13 and (k + 3) % 4 != 0)
    return jnp.where(k <= 12, 0, jnp.where(lax.rem(k + 3, 4) == 0, 0, 1))

class Scatter:
    def __init__(self, bufs, result):
        self.g, self.r, (self.send, self.recv) = bufs[0], bufs[1:6], bufs[6:8]
        self.result = result
        self.at = place()
    def route(self, k, h, n):
        z, x, y, c = self.at
        p, zl, zh = planar(k), z % 2, z // 2
        tz = [(z + 1 - 2 * zl, 1 - p), (z + 2 - 4 * zh, 1 - p)]
        first, other = (x, y) if h == 0 else (y, x)
        def to(flip_first, flip_other, nz):
            f, o = first + flip_first * (1 - 2 * first), other + flip_other * (1 - 2 * other)
            return device(nz, *((f, o) if h == 0 else (o, f)), c)
        lowz, highz = z + 1 - 2 * zl, z + 2 - 4 * zh
        if n == 1:
            return first, to(1, 0, z)
        if n == 2:
            return p * other + (1 - p) * zl, to(0, p, p * z + (1 - p) * lowz)
        if n == 3:
            return p * zl + (1 - p) * zh, to(0, 0, p * lowz + (1 - p) * highz)
        return p * zh + (1 - p) * other, to(0, 1 - p, p * highz + (1 - p) * z)
    def copy(self, k, h, n):
        _, to = self.route(k, h, n)
        bit = self.route(k, h, n)[0]
        i = 2 * n - 1 + h
        return pltpu.make_async_remote_copy(self.r[n - 1].at[k, h, 1 - bit], self.r[n].at[k, h], self.send.at[k, i], self.recv.at[k, i],
                                            device_id=to, device_id_type=MESH)
    def pair(self, k, slot):
        z, x, y, c = self.at
        return pltpu.make_async_remote_copy(self.g.at[slot, 1 - c], self.r[0].at[k], self.send.at[k, 0], self.recv.at[k, 0],
                                            device_id=device(z, x, y, 1 - c), device_id_type=MESH)
    def put(self, slot, p, v, h):
        for o in range(32):
            z, x, y, c = o // 8, o // 4 % 2, o // 2 % 2, o % 2
            f, s = (x, y) if h == 0 else (y, x)
            order = (f, s, z % 2, z // 2) if p else (f, z % 2, z // 2, s)
            self.g[(slot, c, h, *order)] = v[o * 24:o * 24 + 24]
    def kept(self, k, h, n):
        bit, _ = self.route(k, h, n)
        return jnp.where(bit == 0, self.r[n - 1][k, h, 0], self.r[n - 1][k, h, 1])
    def step(self, s, k):
        for h in range(2):
            self.copy(k, h, s - 1).wait()
            v = self.r[s - 1][k, h] + self.kept(k, h, s - 1)
            if s == 5:
                self.result(k, h, v)
            else:
                self.r[s - 1][k, h] = v
                self.copy(k, h, s).start()
    def begin(self, k, slot):
        self.pair(k, slot).start()
    def join(self, k, slot):
        self.pair(k, slot).wait()
        self.r[0][k] += self.g[slot, self.at[3]]
        for h in range(2):
            self.copy(k, h, 1).start()
    def late(self, t):
        for s in (5, 4, 3, 2):
            k = t - LAGS[s]
            if isinstance(t, int):
                if 0 <= k < CHUNKS:
                    self.step(s, k)
            else:
                pl.when(k >= 0)(functools.partial(self.step, s, k))
    def early(self, t, slot):
        k = t - 1
        if isinstance(t, int):
            if k >= 0:
                self.join(k, 1 - slot)
            if t < CHUNKS:
                self.begin(t, slot)
        else:
            pl.when(k >= 0)(functools.partial(self.join, k, 1 - slot))
            self.begin(t, slot)

def scatter_bufs():
    blocks = [(2,) * (5 - n) for n in range(5)]
    return [pltpu.VMEM((2, 2, 2, 2, 2, 2, 2, 24, 128), f32)] + [pltpu.VMEM((CHUNKS,) + b + (24, 128), f32) for b in blocks] + [pltpu.SemaphoreType.DMA((CHUNKS, 9))] * 2

def norm_back(grad, normed, inv, gain):
    gn = grad * gain
    spread = jnp.sum(gn * normed, axis=1, keepdims=True) * (1.0 / D)
    mean = jnp.sum(gn, axis=1, keepdims=True) * (1.0 / D)
    return inv * (gn - mean - normed * spread)

RB = 128
MC = 512
def train_kernel(counts, bitsT, wup, wdownT, g1, g2, tokens_h, outgrad_h, wqkv_h, wao_h, win_h, wout_h,
                 gtok_h, loss_o, grads_o, qkv_h, e_h, linv_h,
                 hid, big, win, wout, wao, e, ctx, mlpin, act, slope, mlpinT, ainT, dattn, draw, drawT, unit_s, target, raw, mc,
                 wide, wd4t, smallT, quantT, s8, zs, sem, osem, ssem, rsem, esem, *bufs):
    def result(k, h, v):
        grads_o[k, :, h * 128:(h + 1) * 128] = v
    main = Scatter(bufs, result)
    z, x, y, c = place()
    loads = {n: pltpu.make_async_copy(src, dst, sem.at[i]) for i, (n, src, dst) in enumerate((
        ("tokens", tokens_h, hid), ("wqkv", wqkv_h, win.at[:, :3 * D]), ("wao", wao_h, wao), ("win", win_h, win), ("wout", wout_h, wout),
        ("outgrad", outgrad_h, big), ("qkv", qkv_h, wout.at[:3 * D]), ("linv", linv_h, big), ("wqkv2", wqkv_h, win.at[:, :3 * D]), ("tokens2", tokens_h, big)))}
    saves = {n: pltpu.make_async_copy(src, dst, osem.at[i]) for i, (n, src, dst) in enumerate((
        ("qkv", wout.at[:3 * D], qkv_h), ("linv", big, linv_h), ("gtok", hid, gtok_h)))}
    def load_e(g, img):
        return pltpu.make_async_copy(e_h.at[pl.ds(img * HEADS + g * 4, 4)], e.at[img], esem.at[img])
    def save_e(g, img):
        return pltpu.make_async_copy(e.at[img], e_h.at[pl.ds(img * HEADS + g * 4, 4)], esem.at[2 + img])
    arrive()
    for n in ("tokens", "wqkv", "wao"):
        loads[n].start()
    first = (lax.axis_index("dp") * lax.axis_size("replica") + lax.axis_index("replica")) * 2
    n0, n1 = counts[first], counts[first + 1]
    total = lax.fori_loop(0, counts.shape[0], lambda i, a: a + counts[i], jnp.int32(0)).astype(f32)
    def live(i):
        row = lax.broadcasted_iota(jnp.int32, (RB, 128), 0) + i * RB
        return row < jnp.where(row < SEQ, n0, n1 + SEQ)
    low = lanes_of(SEQ) < HEAD
    widen(wide, wdownT[...].astype(f32))
    wd4t[...] = wide[...].astype(bf16)
    widen(wide, (2.0 * bitsT[...].astype(f32) - 1.0) * BITS ** -0.5)
    target[...] = wide[...].T
    loads["tokens"].wait()
    def fwd_ln1(i, _):
        r = cols(i, 128)
        n, _inv = norm_stats(hid[r, :])
        dattn[r, :] = (n * g1[...].reshape(1, D)).astype(bf16)
        return 0
    lax.fori_loop(0, 6, fwd_ln1, 0)
    loads["wqkv"].wait()
    def proj(i, _):
        v = dot(dattn[...], win[:, cols(i, 768)])
        v = v * jnp.where(i == 0, 0.125, 1.0)
        wout[cols(i, D), :] = v.astype(bf16)
        return 0
    lax.fori_loop(0, 3, proj, 0)
    loads["win"].start()
    saves["qkv"].start()
    def heads_of(img, o):
        return (wout[pl.ds(pl.multiple_of(b * D + img * SEQ, 128), SEQ), cols(o, 128)] for b in range(3))
    def att(g, _):
        def image(img, _):
            n = jnp.where(img == 0, n0, n1)
            r = pl.ds(pl.multiple_of(img * SEQ, SEQ), SEQ)
            ok = lax.broadcasted_iota(jnp.int32, (1, SEQ), 1) < n
            one = jnp.ones((SEQ, 128), bf16)
            @pl.when(g > 0)
            def _():
                save_e(g - 1, img).wait()
            for j in range(2):
                o = g * 2 + j
                q2, k2, v2 = heads_of(img, o)
                zero = jnp.zeros_like(q2)
                vo = jnp.concatenate([v2, one], axis=1)
                res = []
                for h in range(2):
                    q = jnp.where(low, q2, zero) if h == 0 else jnp.where(low, zero, q2)
                    s = jnp.where(ok, dot(q, k2, 1, 1), -1e30)
                    m = jnp.max(s, axis=1, keepdims=True)
                    p = jnp.exp(s - m).astype(bf16)
                    e[img, 2 * j + h] = p
                    ov = dot(p, vo)
                    inv = 1.0 / ov[:, 128:]
                    res.append((ov[:, :128] * inv, inv))
                ctx[r, cols(o, 128)] = jnp.where(low, res[0][0], res[1][0]).astype(bf16)
                big[r, cols(o, 128)] = jnp.where(low, res[0][1], res[1][1])
            save_e(g, img).start()
            return 0
        lax.fori_loop(0, 2, image, 0)
        return 0
    lax.fori_loop(0, 3, att, 0)
    saves["linv"].start()
    saves["qkv"].wait()
    loads["wout"].start()
    loads["wao"].wait()
    def ao(i, _):
        r = cols(i, 256)
        h = hid[r, :] + dot(ctx[r, :], wao[...])
        hid[r, :] = h
        n, _inv = norm_stats(h)
        mlpin[r, :] = (n * g2[...].reshape(1, D)).astype(bf16)
        return 0
    lax.fori_loop(0, 3, ao, 0)
    saves["linv"].wait()
    loads["outgrad"].start()
    loads["win"].wait()
    for img in range(2):
        save_e(2, img).wait()
        load_e(0, img).start()
    def fwd_mlp(i, _):
        cs = cols(i, MC)
        a, s = gelu_parts(dot(mlpin[...], win[:, cs]))
        act[:, cs] = a.astype(bf16)
        slope[:, cs] = s.astype(bf16)
        return 0
    lax.fori_loop(0, FF // MC, fwd_mlp, 0)
    loads["wout"].wait()
    def mcf(i, _):
        r = cols(i, 768)
        v = dot(wout[r, :], wd4t[...], 1, 1)
        hi = v.astype(bf16).astype(f32)
        mc[r, :] = jnp.where(lanes_of(768) % 64 < 32, hi, v - hi).astype(bf16)
        return 0
    lax.fori_loop(0, 4, mcf, 0)
    rawv = dot(act[...], mc[...])
    raw[...] = rawv + pltpu.roll(rawv, 32, 1) + dot(hid[...].astype(bf16), wd4t[...], 1, 1)
    all_arrived()
    def codes(i):
        r = cols(i, RB)
        rawv = raw[r, :]
        inv_len = lax.rsqrt(jnp.sum(rawv * rawv, axis=1, keepdims=True) * 0.25 + 1.0)
        both = jnp.where(live(i) & (lanes_of(RB) % 32 < BITS), 1.0, 0.0)
        return r, inv_len, rawv * inv_len, both
    def count(i, sums):
        r, inv_len, unit, both = codes(i)
        zl = unit * 8.0
        p = jax.nn.sigmoid(zl)
        miss = unit - target[r, :]
        ent = jnp.maximum(zl, 0.0) + jnp.log1p(jnp.exp(-jnp.abs(zl))) - p * zl
        return tuple(s + jnp.sum(v * both, axis=0, keepdims=True) for s, v in zip(sums, (p, ent, miss * miss)))
    sums = lax.fori_loop(0, 768 // RB, count, (jnp.zeros((1, 128), f32),) * 3)
    rows8 = lax.broadcasted_iota(jnp.int32, (8, 128), 0)
    own = x * 4 + y * 2 + c
    s8[own] = jnp.where(rows8 == 0, sums[0], jnp.where(rows8 == 1, sums[1], jnp.where(rows8 == 2, sums[2], 0.0)))
    def tell(ref, slot, i, to):
        return pltpu.make_async_remote_copy(ref.at[slot], ref.at[slot], ssem.at[i], rsem.at[i], device_id=to, device_id_type=MESH)
    tells = [tell(s8, own, i, p) for i, p in enumerate(near())]
    for t in tells: t.start()
    loads["outgrad"].wait()
    def decode(i, _):
        r = cols(i, RB)
        ok = live(i)
        for j in range(6):
            cs = slice(j * 128, (j + 1) * 128)
            dattn[r, cs] = jnp.where(ok, big[r, cs], 0.0).astype(bf16)
        return 0
    lax.fori_loop(0, 768 // RB, decode, 0)
    quantT[...] = dot(target[...].astype(bf16), dattn[...], 0, 0)
    for t in tells: t.wait_recv()
    s = s8[0]
    for i in range(1, 8):
        s = s + s8[i]
    zs[z] = s
    ztells = [tell(zs, z, 7 + i, p) for i, p in enumerate(column())]
    for t in ztells: t.start()
    for t in tells: t.wait_send()
    widen(wide, wup[...].astype(f32))
    unit_s[...] = dot(dattn[...], wide[...].astype(bf16), 1, 1)
    mlpinT[...] = mlpin[...].T
    for t in ztells: t.wait()
    zsum = zs[0] + zs[1] + zs[2] + zs[3]
    bit8 = lanes_of(8) % 32 < BITS
    mean_prob = jnp.where(bit8, zsum / total, 0.5)[0:1]
    odds = jnp.log(mean_prob / (1.0 - mean_prob))
    g0 = lanes_of(8)[0:1] < BITS
    code_ent = jnp.sum(jnp.where(g0, -mean_prob * jnp.log(mean_prob) - (1.0 - mean_prob) * jnp.log(1.0 - mean_prob), 0.0))
    other = jnp.sum(jnp.where(g0, 0.25 * zsum[2:3] + zsum[1:2], 0.0))
    loss_o[0, 0] = other / total - code_ent
    def unit_back(i, _):
        r, inv_len, unit, both = codes(i)
        zl = unit * 8.0
        p = jax.nn.sigmoid(zl)
        gunit = unit_s[r, :] + both * (8.0 * p * (1.0 - p) * (odds - zl) + 0.5 * (unit - target[r, :]))
        graw = inv_len * (gunit - unit * (jnp.sum(gunit * unit, axis=1, keepdims=True) * 0.25))
        draw[r, :] = graw.astype(bf16)
        return 0
    lax.fori_loop(0, 768 // RB, unit_back, 0)
    def put(t, p, v):
        for h in range(2):
            main.put(t % 2, p, v[:, h * 128:(h + 1) * 128], h)
    def mlp(i, _):
        for j in range(6):
            t = 6 * i + j
            cs = cols(t, W)
            d = dot(draw[...], mc[cs, :], 1, 1) * 0.5
            dp = (slope[:, cs].astype(f32) * d).astype(bf16)
            slope[:, cs] = dp
            main.late(t)
            put(j, 0, dot(mlpinT[...], dp))
            main.early(t, j % 2)
        return 0
    lax.fori_loop(0, 2, mlp, 0)
    main.late(12)
    drawT[...] = draw[...].T
    for q in range(4):
        big[128 * q:128 * q + 128, :] = dot(drawT[...], act[:, q * D:(q + 1) * D])
    for b in range(8):
        t = big[b // 2 * 128:b // 2 * 128 + 128, b % 2 * 384:b % 2 * 384 + 384].T.reshape(4, 4, 24, 128)
        l4 = lax.broadcasted_iota(jnp.int32, (4, 24, 128), 2) // 32
        s = jnp.where(l4 == 0, t[:, 0], 0.0)
        for j in range(1, 4):
            s = jnp.where(l4 == j, t[:, j], s)
        unit_s[b * 96:(b + 1) * 96, :] = s.reshape(96, 128)
    main.put(0, 0, unit_s[...], 0)
    gwd = dot(drawT[...], hid[...].astype(bf16))
    for q in range(4):
        gv = big[128 * q:128 * q + 128, :]
        hi = gv.astype(bf16)
        lo = (gv - hi.astype(f32)).astype(bf16)
        w = wout[q * D:(q + 1) * D, :]
        gwd = gwd + (dot(hi, w) + dot(lo, w))
    r128 = lax.broadcasted_iota(jnp.int32, (128, D), 0)
    smallT[...] = jnp.where(r128 < 32, gwd, quantT[...])
    for i in range(6):
        unit_s[i * 128:(i + 1) * 128, :] = smallT[:, i * 128:(i + 1) * 128].T
    main.put(0, 0, unit_s[...], 1)
    main.early(12, 0)
    loads["linv"].start()
    loads["qkv"].start()
    main.late(13)
    def ln2(i, _):
        r = cols(i, 256)
        dn = dot(slope[r, :], win[...], 1, 1)
        nrm, inv = norm_stats(hid[r, :])
        v = norm_back(dn, nrm, inv, g2[...].reshape(1, D)) + dot(draw[r, :], wd4t[...]) * 0.25
        hid[r, :] = v
        dattn[r, :] = v.astype(bf16)
        return 0
    lax.fori_loop(0, 3, ln2, 0)
    loads["wqkv2"].start()
    loads["linv"].wait()
    mlpinT[...] = ctx[...].T
    def dctx(i, _):
        r = cols(i, 256)
        mlpin[r, :] = (dot(dattn[r, :], wao[...], 1, 1) * big[r, :]).astype(bf16)
        return 0
    lax.fori_loop(0, 3, dctx, 0)
    loads["tokens2"].start()
    loads["qkv"].wait()
    loads["tokens2"].wait()
    for i in range(6):
        r = pl.ds(i * 128, 128)
        nrm, inv = norm_stats(big[r, :])
        ainT[:, i * 128:(i + 1) * 128] = (nrm * g1[...].reshape(1, D)).astype(bf16).T
    def group(g, _):
        t0 = 13 + 4 * g
        main.late(t0 + 1)
        put(1, 0, dot(mlpinT[...], dattn[:, cols(g, W)]))
        main.early(t0, 1)
        def image(img, _):
            load_e(g, img).wait()
            r = pl.ds(pl.multiple_of(img * SEQ, SEQ), SEQ)
            for j in range(2):
                o = g * 2 + j
                q2, k2, v2 = heads_of(img, o)
                cs = cols(o, 128)
                d2, c2 = mlpin[r, cs], ctx[r, cs]
                prod = d2.astype(f32) * c2.astype(f32)
                zero_ = jnp.zeros_like(q2)
                dq = dk = dv = None
                for h in range(2):
                    mine = low if h == 0 else jnp.logical_not(low)
                    pick = lambda a: jnp.where(mine, a, zero_)
                    dh = pick(d2)
                    ev = e[img, 2 * j + h]
                    dd = jnp.sum(jnp.where(mine, prod, 0.0), axis=1, keepdims=True)
                    ds = (ev.astype(f32) * (dot(dh, v2, 1, 1) - dd)).astype(bf16)
                    a, b, cc = dot(ds, pick(k2)), dot(ds, pick(q2), 0, 0), dot(ev, dh, 0, 0)
                    dq, dk, dv = (a, b, cc) if h == 0 else (dq + a, dk + b, dv + cc)
                for b, v in enumerate((dq * 0.125, dk, dv)):
                    act[r, pl.ds(pl.multiple_of(b * D + o * 128, 128), 128)] = v.astype(bf16)
            @pl.when(g < 2)
            def _():
                load_e(g + 1, img).start()
            main.late(t0 + 2 + img)
            return 0
        lax.fori_loop(0, 2, image, 0)
        for j in range(3):
            put(j, 1, dot(ainT[...], act[:, pl.ds(pl.multiple_of(j * D + g * W, W), W)]))
            main.early(t0 + 1 + j, j % 2)
            if j == 1:
                main.late(t0 + 4)
        return 0
    lax.fori_loop(0, 3, group, 0)
    main.early(25, 1)
    main.late(26)
    loads["wqkv2"].wait()
    def ln1(i, _):
        r = cols(i, 256)
        dn = dot(act[r, :3 * D], win[:, :3 * D], 1, 1)
        nrm, inv = norm_stats(big[r, :])
        hid[r, :] += norm_back(dn, nrm, inv, g1[...].reshape(1, D))
        main.late(27 + i)
        return 0
    lax.fori_loop(0, 3, ln1, 0)
    saves["gtok"].start()
    for t in range(30, CHUNKS + LAGS[5]):
        main.late(t)
    saves["gtok"].wait()

def train(*args):
    T = 768
    any_, vm, sm = pl.BlockSpec(memory_space=pl.ANY), pl.BlockSpec(memory_space=pltpu.VMEM), pl.BlockSpec(memory_space=pltpu.SMEM)
    V, S = pltpu.VMEM, pltpu.SemaphoreType.DMA
    shapes = [((T, D), f32), ((1, 1), f32), ((CHUNKS, 24, W), f32), ((3 * T, D), bf16), ((24, SEQ, SEQ), bf16), ((T, D), f32)]
    return pl.pallas_call(train_kernel,
        out_shape=[jax.ShapeDtypeStruct(*s) for s in shapes],
        in_specs=[sm] + [vm] * 5 + [any_] * 6,
        out_specs=[any_, sm, vm] + [any_] * 3,
        scratch_shapes=[V((T, D), f32), V((T, D), f32), V((D, FF), bf16), V((FF, D), bf16), V((D, D), bf16), V((2, 4, SEQ, SEQ), bf16),
            V((T, D), bf16), V((T, D), bf16), V((T, FF), bf16), V((T, FF), bf16), V((D, T), bf16), V((D, T), bf16), V((T, D), bf16),
            V((T, 128), bf16), V((128, T), bf16), V((T, 128), f32), V((T, 128), f32), V((T, 128), f32), V((FF, 128), bf16),
            V((128, D), f32), V((128, D), bf16), V((128, D), f32), V((128, D), f32), V((8, 8, 128), f32), V((4, 8, 128), f32),
            S((10,)), S((3,)), S((10,)), S((10,)), S((4,))] + scatter_bufs(),
        compiler_params=pltpu.CompilerParams(vmem_limit_bytes=64 << 20, collective_id=1, has_side_effects=True),
        name="train")(*args)

PIECES = 4
def finish_kernel(scale, counts, gtok_i, loss_i, wqkv_h, win_h, grads, wdownT, g1, g2, bitsT, wup,
                  dec_h, gtok_o, loss_o, gln1, gwqkv, gwao, gln2, gwin, gwout, gwdown, gwup, wq, wi, wide, held, dec, sem, csem):
    part = lambda i: pl.ds(i * (768 // PIECES), 768 // PIECES)
    take = [pltpu.make_async_copy(gtok_i.at[part(i)], held.at[part(i)], csem.at[0, i]) for i in range(PIECES)]
    give = [pltpu.make_async_copy(held.at[part(i)], gtok_o.at[part(i)], csem.at[1, i]) for i in range(PIECES)]
    show = [pltpu.make_async_copy(dec.at[part(i)], dec_h.at[part(i)], csem.at[2, i]) for i in range(PIECES)]
    for t in take: t.start()
    me = lax.axis_index("dp") * lax.axis_size("replica") + lax.axis_index("replica")
    start = pl.multiple_of((me * 24) // 16 * 16, 16)
    reads = [pltpu.make_async_copy(h.at[pl.ds(start, 32)], v, sem.at[i]) for i, (h, v) in ((0, (wqkv_h, wq)), (1, (win_h, wi)))]
    for r in reads: r.start()
    loss_o[0, 0] = loss_i[0, 0]
    n0, n1 = counts[2 * me], counts[2 * me + 1]
    widen(wide, wup[...].astype(f32))
    up = wide[...].astype(bf16)
    widen(wide, (2.0 * bitsT[...].astype(f32) - 1.0) * BITS ** -0.5)
    target = (wide[...].T * 0.25).astype(bf16)
    rows = 768 // PIECES
    for i in range(PIECES):
        row = lax.broadcasted_iota(jnp.int32, (rows, D), 0) + i * rows
        live = row < jnp.where(row < SEQ, n0, n1 + SEQ)
        dec[part(i), :] = jnp.where(live, dot(target[i * rows:(i + 1) * rows], up), 0.0)
        show[i].start()
        take[i].wait()
        give[i].start()
    for k in range(12):
        gwin[:, k * W:(k + 1) * W] = grads[k] * scale
    for g in range(3):
        gwao[:, g * W:(g + 1) * W] = grads[13 + 4 * g] * scale
        for j in range(3):
            gwqkv[:, j * D + g * W:j * D + (g + 1) * W] = grads[14 + 4 * g + j] * scale
    widen(wide, wdownT[...].astype(f32))
    wd = wide[...].astype(bf16)
    code, other = grads[12, :, :128] * scale, grads[12, :, 128:] * scale
    lane = lanes_of(24)
    for j in range(4):
        v = jnp.where(lane // 32 == j, code, 0.0)
        hi = v.astype(bf16)
        lo = (v - hi.astype(f32)).astype(bf16)
        gwout[24 * j:24 * j + 24, :] = dot(hi, wd) + dot(lo, wd)
    gwdown[...] = other[:, :BITS]
    for r in reads: r.wait()
    odd = me % 2
    own = lax.broadcasted_iota(jnp.int32, (24, D), 1) == lax.broadcasted_iota(jnp.int32, (24, D), 0) + me * 24
    def gain(weights, grad, g, lane_at, into):
        w = weights[...].astype(f32)
        w = jnp.where(odd == 1, w[8:32], w[0:24])
        mine = jnp.sum(jnp.where(own, g[...].reshape(1, D), 0.0), axis=1, keepdims=True)
        return jnp.where(lane == lane_at, jnp.sum(w * grad[...], axis=1, keepdims=True) / mine, into)
    flat = gain(wi, gwin, g2, 65, gain(wq, gwqkv, g1, 64, other))
    turned = jnp.concatenate([flat, jnp.zeros((104, 128), f32)], axis=0).T
    gwup[...] = turned[32:32 + BITS, :24]
    gln1[...] = turned[64:65, :24]
    gln2[...] = turned[65:66, :24]
    for t in give + show: t.wait()

def finish(scale, counts, gtok, *rest):
    any_, vm, sm = pl.BlockSpec(memory_space=pl.ANY), pl.BlockSpec(memory_space=pltpu.VMEM), pl.BlockSpec(memory_space=pltpu.SMEM)
    shapes = [gtok.shape, gtok.shape, (1, 1), (1, 24), (24, 3 * D), (24, D), (1, 24), (24, FF), (96, D), (24, BITS), (BITS, 24)]
    return pl.pallas_call(functools.partial(finish_kernel, scale),
        out_shape=[jax.ShapeDtypeStruct(s, f32) for s in shapes],
        in_specs=[sm, any_, sm, any_, any_] + [vm] * 6,
        out_specs=[any_, any_, sm] + [vm] * 8,
        scratch_shapes=[pltpu.VMEM((32, 3 * D), bf16), pltpu.VMEM((32, FF), bf16), pltpu.VMEM((128, D), f32), pltpu.VMEM(gtok.shape, f32), pltpu.VMEM(gtok.shape, f32),
            pltpu.SemaphoreType.DMA((2,)), pltpu.SemaphoreType.DMA((3, PIECES))],
        name="finish")(counts, gtok, *rest)

def kernel_body(tokens, counts, bits, outgrad, g1, wqkv, wao, g2, win, wout, wdown, wup):
    bitsT, wdownT = bits.T, wdown.T
    gtok, loss, grads = train(counts, bitsT, wup, wdownT, g1, g2, tokens, outgrad, wqkv, wao, win, wout)[:3]
    scale = (tokens.shape[0] * lax.axis_size(("dp", "replica"))) ** -0.5
    decoded, gtok, loss, gln1, gwqkv, gwao, gln2, gwin, gwout, gwdown, gwup = finish(scale, counts, gtok, loss, wqkv, win, grads, wdownT, g1, g2, bitsT, wup)
    return (decoded, loss.reshape(()), gtok, gln1.reshape(24), gwqkv, gwao, gln2.reshape(24), gwin, gwout, gwdown, gwup)

eps_norm = 1e-06
neg_big = -1e30
sharpness = 8.0
commit_weight = 0.25


def exact_gelu(values):
    return jax.nn.gelu(values, approximate=False)


def layer_norm(values, gain):
    centered = values - jnp.mean(values, axis=-1, keepdims=True)
    inv_std = lax.rsqrt(jnp.mean(centered * centered, axis=-1, keepdims=True) + eps_norm)
    normed = centered * inv_std
    return (normed * gain, normed, inv_std)


def plain_norm_back(grad_out, normed, inv_std, gain):
    grad_normed = grad_out * gain
    grad_gain = jnp.sum(grad_out * normed, axis=0)
    spread_part = jnp.mean(grad_normed * normed, axis=-1, keepdims=True)
    grad_in = inv_std * (
        grad_normed - jnp.mean(grad_normed, axis=-1, keepdims=True) - normed * spread_part
    )
    return (grad_in, grad_gain)


def inner_rows(left, right):
    return lax.dot_general(
        left, right, (((0,), (0,)), ((), ())), preferred_element_type=jnp.float32
    )


def times_transposed(left, right):
    return lax.dot_general(
        left, right, (((1,), (1,)), ((), ())), preferred_element_type=jnp.float32
    )


def attention_logits(queries, key_rows, key_valid):
    scores = jnp.einsum("bqhd,bkhd->bhqk", queries, key_rows, preferred_element_type=jnp.float32)
    return jnp.where(key_valid, scores * HEAD ** (-0.5), neg_big)


def plain_body(
    tokens,
    patch_counts,
    code_bits,
    out_grad,
    ln1_gain,
    w_qkv,
    w_attn_out,
    ln2_gain,
    w_mlp_in,
    w_mlp_out,
    w_down,
    w_up,
):
    row_count = tokens.shape[0]
    images = row_count // SEQ
    width_all = tokens.shape[1]
    first_image = lax.axis_index(("dp", "replica")) * images
    counts = lax.dynamic_slice_in_dim(patch_counts, first_image, images)
    total_count = jnp.sum(patch_counts).astype(jnp.float32)
    valid_slots = jnp.arange(SEQ, dtype=jnp.int32)[None, :] < counts[:, None]
    key_valid = valid_slots[:, None, None, :]
    row_valid = valid_slots.reshape(row_count).astype(jnp.float32)[:, None]
    target = (2.0 * code_bits.astype(jnp.float32) - 1.0) * BITS ** (-0.5)
    normed1_out, normed1, inv_std1 = layer_norm(tokens, ln1_gain)
    attn_in = normed1_out.astype(jnp.bfloat16)
    qkv_rows = jnp.dot(attn_in, w_qkv, preferred_element_type=jnp.float32).astype(jnp.bfloat16)
    qkv_rows = qkv_rows.reshape(images, SEQ, 3, HEADS, HEAD)
    queries = qkv_rows[:, :, 0]
    key_rows = qkv_rows[:, :, 1]
    value_rows = qkv_rows[:, :, 2]
    logits = attention_logits(queries, key_rows, key_valid)
    row_max = jnp.max(logits, axis=-1, keepdims=True)
    weights = jnp.exp(logits - row_max)
    row_total = jnp.sum(weights, axis=-1, keepdims=True)
    log_total = row_max + jnp.log(row_total)
    prob_low = (weights / row_total).astype(jnp.bfloat16)
    context = jnp.einsum(
        "bhqk,bkhd->bqhd", prob_low, value_rows, preferred_element_type=jnp.float32
    )
    context_low = context.astype(jnp.bfloat16).reshape(row_count, width_all)
    hidden1 = tokens + jnp.dot(context_low, w_attn_out, preferred_element_type=jnp.float32)
    normed2_out, normed2, inv_std2 = layer_norm(hidden1, ln2_gain)
    mlp_in = normed2_out.astype(jnp.bfloat16)
    pre_act = jnp.dot(mlp_in, w_mlp_in, preferred_element_type=jnp.float32)
    activation, gelu_back = jax.vjp(exact_gelu, pre_act)
    activation_low = activation.astype(jnp.bfloat16)
    hidden2 = hidden1 + jnp.dot(activation_low, w_mlp_out, preferred_element_type=jnp.float32)
    hidden2_low = hidden2.astype(jnp.bfloat16)
    raw_code = jnp.dot(hidden2_low, w_down, preferred_element_type=jnp.float32)
    inv_len = lax.rsqrt(jnp.sum(raw_code * raw_code, axis=-1, keepdims=True) + 1.0)
    unit_code = raw_code * inv_len
    quant_low = target.astype(jnp.bfloat16)
    decoded = row_valid * jnp.dot(quant_low, w_up, preferred_element_type=jnp.float32)
    logit_bits = unit_code * sharpness
    soft_prob = jax.nn.sigmoid(logit_bits)
    token_ent = jax.nn.softplus(logit_bits) - soft_prob * logit_bits
    code_miss = unit_code - target
    prob_sum = jnp.sum(soft_prob * row_valid, axis=0)
    ent_sum = jnp.sum(token_ent * row_valid)
    commit_sum = jnp.sum(code_miss * code_miss * row_valid)
    prob_sum, ent_sum, commit_sum = lax.psum((prob_sum, ent_sum, commit_sum), ("dp", "replica"))
    mean_prob = prob_sum / total_count
    code_ent = jnp.sum(
        -mean_prob * jnp.log(mean_prob) - (1.0 - mean_prob) * jnp.log(1.0 - mean_prob)
    )
    entropy_loss = (commit_weight * commit_sum + ent_sum) / total_count - code_ent
    grad_dec_low = (row_valid * out_grad).astype(jnp.bfloat16)
    grad_w_up = inner_rows(quant_low, grad_dec_low)
    grad_quant = times_transposed(grad_dec_low, w_up)
    prob_logit = jnp.log(mean_prob / (1.0 - mean_prob))
    loss_part = (
        sharpness * soft_prob * (1.0 - soft_prob) * (prob_logit - logit_bits)
        + 2.0 * commit_weight * code_miss
    )
    grad_unit = grad_quant + row_valid * loss_part
    grad_raw = inv_len * (
        grad_unit - unit_code * jnp.sum(grad_unit * unit_code, axis=-1, keepdims=True)
    )
    grad_raw_low = grad_raw.astype(jnp.bfloat16)
    grad_w_down = inner_rows(hidden2_low, grad_raw_low)
    grad_hidden2 = times_transposed(grad_raw_low, w_down)
    grad_mlp_low = grad_hidden2.astype(jnp.bfloat16)
    grad_w_mlp_out = inner_rows(activation_low, grad_mlp_low)
    grad_activation = times_transposed(grad_mlp_low, w_mlp_out)
    grad_pre_low = gelu_back(grad_activation)[0].astype(jnp.bfloat16)
    grad_w_mlp_in = inner_rows(mlp_in, grad_pre_low)
    grad_norm2_in = times_transposed(grad_pre_low, w_mlp_in)
    grad_from_norm2, grad_ln2 = plain_norm_back(grad_norm2_in, normed2, inv_std2, ln2_gain)
    grad_hidden1 = grad_hidden2 + grad_from_norm2
    grad_attn_low = grad_hidden1.astype(jnp.bfloat16)
    grad_w_attn_out = inner_rows(context_low, grad_attn_low)
    grad_context = times_transposed(grad_attn_low, w_attn_out).astype(jnp.bfloat16)
    grad_context = grad_context.reshape(images, SEQ, HEADS, HEAD)
    grad_values = jnp.einsum(
        "bhqk,bqhd->bkhd", prob_low, grad_context, preferred_element_type=jnp.float32
    )
    grad_prob = jnp.einsum(
        "bqhd,bkhd->bhqk", grad_context, value_rows, preferred_element_type=jnp.float32
    )
    attn_prob = jnp.exp(attention_logits(queries, key_rows, key_valid) - log_total)
    grad_scores = (
        attn_prob
        * (grad_prob - jnp.sum(grad_prob * attn_prob, axis=-1, keepdims=True))
        * HEAD ** (-0.5)
    )
    grad_scores_low = grad_scores.astype(jnp.bfloat16)
    grad_queries = jnp.einsum(
        "bhqk,bkhd->bqhd", grad_scores_low, key_rows, preferred_element_type=jnp.float32
    )
    grad_keys = jnp.einsum(
        "bhqk,bqhd->bkhd", grad_scores_low, queries, preferred_element_type=jnp.float32
    )
    grad_qkv = jnp.stack((grad_queries, grad_keys, grad_values), axis=2).reshape(
        row_count, 3 * width_all
    )
    grad_qkv_low = grad_qkv.astype(jnp.bfloat16)
    grad_w_qkv = inner_rows(attn_in, grad_qkv_low)
    grad_norm1_in = times_transposed(grad_qkv_low, w_qkv)
    grad_from_norm1, grad_ln1 = plain_norm_back(grad_norm1_in, normed1, inv_std1, ln1_gain)
    grad_tokens = grad_hidden1 + grad_from_norm1
    summed = (
        lax.psum_scatter(grad_ln1, ("dp", "replica"), scatter_dimension=0, tiled=True),
        lax.psum_scatter(grad_w_qkv, ("dp", "replica"), scatter_dimension=0, tiled=True),
        lax.psum_scatter(grad_w_attn_out, ("dp", "replica"), scatter_dimension=0, tiled=True),
        lax.psum_scatter(grad_ln2, ("dp", "replica"), scatter_dimension=0, tiled=True),
        lax.psum_scatter(grad_w_mlp_in, ("dp", "replica"), scatter_dimension=0, tiled=True),
        lax.psum_scatter(grad_w_mlp_out, ("dp", "replica"), scatter_dimension=0, tiled=True),
        lax.psum_scatter(grad_w_down, ("dp", "replica"), scatter_dimension=0, tiled=True),
        lax.psum_scatter(grad_w_up, ("dp", "replica"), scatter_dimension=1, tiled=True),
    )
    grad_scale = (row_count * lax.axis_size(("dp", "replica"))) ** (-0.5)
    return (
        decoded,
        entropy_loss,
        grad_tokens,
        summed[0] * grad_scale,
        summed[1] * grad_scale,
        summed[2] * grad_scale,
        summed[3] * grad_scale,
        summed[4] * grad_scale,
        summed[5] * grad_scale,
        summed[6] * grad_scale,
        summed[7] * grad_scale,
    )


def solution(mesh):
    in_specs = (
        P(("dp", "replica"), None),
        P(),
        P(("dp", "replica"), None),
        P(("dp", "replica"), None),
        P(),
        P(),
        P(),
        P(),
        P(),
        P(),
        P(),
        P(),
    )
    out_specs = (
        P(("dp", "replica"), None),
        P(),
        P(("dp", "replica"), None),
        P(("dp", "replica")),
        P(("dp", "replica"), None),
        P(("dp", "replica"), None),
        P(("dp", "replica")),
        P(("dp", "replica"), None),
        P(("dp", "replica"), None),
        P(("dp", "replica"), None),
        P(None, ("dp", "replica")),
    )
    body = kernel_body if (mesh.shape["dp"], mesh.shape["replica"]) == (8, 4) else plain_body
    return jax.shard_map(body, mesh=mesh, in_specs=in_specs, out_specs=out_specs, check_vma=False)
```

```python
import functools
import math

import jax
import jax.numpy as jnp
from jax import lax
from jax.experimental import pallas as pl
from jax.experimental.pallas import tpu as pltpu
from jax.sharding import PartitionSpec as P

HEADS, HEAD, BITS, SEQ = 12, 64, 18, 384
D, FF = 768, 3072
EPS = 1e-06
bf16, f32 = jnp.bfloat16, jnp.float32

def dot(a, b, ca=1, cb=0):
    return lax.dot_general(a, b, (((ca,), (cb,)), ((), ())), preferred_element_type=f32)

def norm_stats(v):
    mean = jnp.sum(v, axis=1, keepdims=True) * (1.0 / D)
    cen = v - mean
    var = jnp.sum(cen * cen, axis=1, keepdims=True) * (1.0 / D)
    inv = lax.rsqrt(var + EPS)
    return cen * inv, inv

def cols(i, n):
    return pl.ds(pl.multiple_of(i * n, n), n)

def lanes_of(rows, width=128):
    return lax.broadcasted_iota(jnp.int32, (rows, width), 1)

def widen(ref, rows):
    ref[...] = jnp.zeros_like(ref)
    for j in range(4):
        ref[32 * j:32 * j + BITS, :] = rows

def gelu_parts(x):
    cdf = 0.5 + 0.5 * lax.erf(x * math.sqrt(0.5))
    pdf = jnp.exp(x * x * -0.5) * (1.0 / math.sqrt(2.0 * math.pi))
    return x * cdf, cdf + x * pdf

MESH = pl.DeviceIdType.MESH
W = 256
CHUNKS = 25
LAGS = (0, 1, 6, 10, 14, 18)

def place():
    dp, rp = lax.axis_index("dp"), lax.axis_index("replica")
    return dp // 2, dp % 2, rp // 2, rp % 2

def device(z, x, y, c):
    return (z * 2 + x, y * 2 + c)

def near():
    z, x, y, c = place()
    flip = lambda v, n: 1 - v if n else v
    return [device(z, flip(x, n & 4), flip(y, n & 2), flip(c, n & 1)) for n in range(1, 8)]

def column():
    z, x, y, c = place()
    return [device((z + d) % 4, x, y, c) for d in (1, 2, 3)]

def arrive():
    for p in near() + column():
        pl.semaphore_signal(pltpu.get_barrier_semaphore(), inc=1, device_id=p, device_id_type=MESH)

def all_arrived():
    pl.semaphore_wait(pltpu.get_barrier_semaphore(), len(near() + column()))

def planar(k):
    if isinstance(k, int):
        return int(k % 6 == 5 if k <= 12 else (k + 3) % 4 >= 2)
    return jnp.where(k <= 12, jnp.where(lax.rem(k, 6) == 5, 1, 0), jnp.where(lax.rem(k + 3, 4) >= 2, 1, 0))

class Scatter:
    def __init__(self, bufs, result):
        self.g, self.r, (self.send, self.recv) = bufs[0], bufs[1:6], bufs[6:8]
        self.result = result
        self.at = place()
    def route(self, k, h, n):
        z, x, y, c = self.at
        p, zl, zh = planar(k), z % 2, z // 2
        first, other = (x, y) if h == 0 else (y, x)
        def to(flip_first, flip_other, nz):
            f, o = first + flip_first * (1 - 2 * first), other + flip_other * (1 - 2 * other)
            return device(nz, *((f, o) if h == 0 else (o, f)), c)
        lowz, highz = z + 1 - 2 * zl, z + 2 - 4 * zh
        if n == 1:
            return first, to(1, 0, z)
        if n == 2:
            return p * other + (1 - p) * zl, to(0, p, p * z + (1 - p) * lowz)
        if n == 3:
            return p * zl + (1 - p) * zh, to(0, 0, p * lowz + (1 - p) * highz)
        return p * zh + (1 - p) * other, to(0, 1 - p, p * highz + (1 - p) * z)
    def copy(self, k, h, n):
        _, to = self.route(k, h, n)
        bit = self.route(k, h, n)[0]
        i = 2 * n - 1 + h
        return pltpu.make_async_remote_copy(self.r[n - 1].at[k, h, 1 - bit], self.r[n].at[k, h], self.send.at[k, i], self.recv.at[k, i],
                                            device_id=to, device_id_type=MESH)
    def pair(self, k, slot):
        z, x, y, c = self.at
        return pltpu.make_async_remote_copy(self.g.at[slot, 1 - c], self.r[0].at[k], self.send.at[k, 0], self.recv.at[k, 0],
                                            device_id=device(z, x, y, 1 - c), device_id_type=MESH)
    def put(self, slot, p, v, h):
        for o in range(32):
            z, x, y, c = o // 8, o // 4 % 2, o // 2 % 2, o % 2
            f, s = (x, y) if h == 0 else (y, x)
            order = (f, s, z % 2, z // 2) if p else (f, z % 2, z // 2, s)
            self.g[(slot, c, h, *order)] = v[o * 24:o * 24 + 24]
    def kept(self, k, h, n):
        bit, _ = self.route(k, h, n)
        return jnp.where(bit == 0, self.r[n - 1][k, h, 0], self.r[n - 1][k, h, 1])
    def step(self, s, k):
        for h in range(2):
            self.copy(k, h, s - 1).wait()
            v = self.r[s - 1][k, h] + self.kept(k, h, s - 1)
            if s == 5:
                self.result(k, h, v)
            else:
                self.r[s - 1][k, h] = v
                self.copy(k, h, s).start()
    def begin(self, k, slot):
        self.pair(k, slot).start()
    def join(self, k, slot):
        self.pair(k, slot).wait()
        self.r[0][k] += self.g[slot, self.at[3]]
        for h in range(2):
            self.copy(k, h, 1).start()
    def late(self, t):
        for s in (5, 4, 3, 2):
            k = t - LAGS[s]
            if isinstance(t, int):
                if 0 <= k < CHUNKS:
                    self.step(s, k)
            else:
                pl.when(k >= 0)(functools.partial(self.step, s, k))
    def early(self, t, slot):
        k = t - 1
        if isinstance(t, int):
            if k >= 0:
                self.join(k, 1 - slot)
            if t < CHUNKS:
                self.begin(t, slot)
        else:
            pl.when(k >= 0)(functools.partial(self.join, k, 1 - slot))
            self.begin(t, slot)

def scatter_bufs():
    blocks = [(2,) * (5 - n) for n in range(5)]
    return [pltpu.VMEM((2, 2, 2, 2, 2, 2, 2, 24, 128), f32)] + [pltpu.VMEM((CHUNKS,) + b + (24, 128), f32) for b in blocks] + [pltpu.SemaphoreType.DMA((CHUNKS, 9))] * 2

def norm_back(grad, normed, inv, gain):
    gn = grad * gain
    spread = jnp.sum(gn * normed, axis=1, keepdims=True) * (1.0 / D)
    mean = jnp.sum(gn, axis=1, keepdims=True) * (1.0 / D)
    return inv * (gn - mean - normed * spread)

RB = 256
MC = 1024
def train_kernel(counts, bitsT, wup, wdownT, g1, g2, tokens_h, outgrad_h, wqkv_h, wao_h, win_h, wout_h,
                 gtok_h, loss_o, grads_o, qkv_h, e_h, linv_h,
                 hid, big, win, wout, wao, e, ctx, mlpin, act, slope, mlpinT, ainT, dattn, draw, drawT, unit_s, target, raw, mc,
                 wide, wd4t, smallT, quantT, s8, zs, sem, osem, ssem, rsem, esem, *bufs):
    def result(k, h, v):
        grads_o[k, :, h * 128:(h + 1) * 128] = v
    main = Scatter(bufs, result)
    z, x, y, c = place()
    loads = {n: pltpu.make_async_copy(src, dst, sem.at[i]) for i, (n, src, dst) in enumerate((
        ("tokens", tokens_h, hid), ("wqkv", wqkv_h, win.at[:, :3 * D]), ("wao", wao_h, wao), ("win", win_h, win), ("wout", wout_h, wout),
        ("outgrad", outgrad_h, big), ("qkv", qkv_h, wout.at[:3 * D]), ("linv", linv_h, big), ("wqkv2", wqkv_h, win.at[:, :3 * D]), ("tokens2", tokens_h, big)))}
    saves = {n: pltpu.make_async_copy(src, dst, osem.at[i]) for i, (n, src, dst) in enumerate((
        ("qkv", wout.at[:3 * D], qkv_h), ("linv", big, linv_h), ("gtok", hid, gtok_h)))}
    def load_e(g, img):
        return pltpu.make_async_copy(e_h.at[pl.ds(img * HEADS + g * 4, 4)], e.at[img], esem.at[img])
    def save_e(g, img):
        return pltpu.make_async_copy(e.at[img], e_h.at[pl.ds(img * HEADS + g * 4, 4)], esem.at[2 + img])
    arrive()
    for n in ("tokens", "wqkv", "wao"):
        loads[n].start()
    first = (lax.axis_index("dp") * lax.axis_size("replica") + lax.axis_index("replica")) * 2
    n0, n1 = counts[first], counts[first + 1]
    total = lax.fori_loop(0, counts.shape[0], lambda i, a: a + counts[i], jnp.int32(0)).astype(f32)
    def live(i):
        row = lax.broadcasted_iota(jnp.int32, (RB, 128), 0) + i * RB
        return row < jnp.where(row < SEQ, n0, n1 + SEQ)
    low = lanes_of(SEQ) < HEAD
    widen(wide, wdownT[...].astype(f32))
    wd4t[...] = wide[...].astype(bf16)
    widen(wide, (2.0 * bitsT[...].astype(f32) - 1.0) * BITS ** -0.5)
    target[...] = wide[...].T
    loads["tokens"].wait()
    def fwd_ln1(i, _):
        r = cols(i, 256)
        n, _inv = norm_stats(hid[r, :])
        dattn[r, :] = (n * g1[...].reshape(1, D)).astype(bf16)
        return 0
    lax.fori_loop(0, 3, fwd_ln1, 0)
    loads["wqkv"].wait()
    def proj(i, _):
        v = dot(dattn[...], win[:, cols(i, 768)])
        v = v * jnp.where(i == 0, 0.125, 1.0)
        wout[cols(i, D), :] = v.astype(bf16)
        return 0
    lax.fori_loop(0, 3, proj, 0)
    loads["win"].start()
    saves["qkv"].start()
    def heads_of(img, o):
        return (wout[pl.ds(pl.multiple_of(b * D + img * SEQ, 128), SEQ), cols(o, 128)] for b in range(3))
    def att(g, _):
        def image(img, _):
            n = jnp.where(img == 0, n0, n1)
            r = pl.ds(pl.multiple_of(img * SEQ, SEQ), SEQ)
            ok = lax.broadcasted_iota(jnp.int32, (1, SEQ), 1) < n
            one = jnp.ones((SEQ, 128), bf16)
            @pl.when(g > 0)
            def _():
                save_e(g - 1, img).wait()
            for j in range(2):
                o = g * 2 + j
                q2, k2, v2 = heads_of(img, o)
                zero = jnp.zeros_like(q2)
                vo = jnp.concatenate([v2, one], axis=1)
                res = []
                for h in range(2):
                    q = jnp.where(low, q2, zero) if h == 0 else jnp.where(low, zero, q2)
                    s = jnp.where(ok, dot(q, k2, 1, 1), -1e30)
                    m = jnp.max(s, axis=1, keepdims=True)
                    p = jnp.exp(s - m).astype(bf16)
                    e[img, 2 * j + h] = p
                    ov = dot(p, vo)
                    inv = 1.0 / ov[:, 128:]
                    res.append((ov[:, :128] * inv, inv))
                ctx[r, cols(o, 128)] = jnp.where(low, res[0][0], res[1][0]).astype(bf16)
                big[r, cols(o, 128)] = jnp.where(low, res[0][1], res[1][1])
            save_e(g, img).start()
            return 0
        lax.fori_loop(0, 2, image, 0)
        return 0
    lax.fori_loop(0, 3, att, 0)
    saves["linv"].start()
    saves["qkv"].wait()
    loads["wout"].start()
    loads["wao"].wait()
    def ao(i, _):
        r = cols(i, 256)
        h = hid[r, :] + dot(ctx[r, :], wao[...])
        hid[r, :] = h
        n, _inv = norm_stats(h)
        mlpin[r, :] = (n * g2[...].reshape(1, D)).astype(bf16)
        return 0
    lax.fori_loop(0, 3, ao, 0)
    saves["linv"].wait()
    loads["outgrad"].start()
    loads["win"].wait()
    for img in range(2):
        save_e(2, img).wait()
        load_e(0, img).start()
    def fwd_mlp(i, _):
        cs = cols(i, MC)
        a, s = gelu_parts(dot(mlpin[...], win[:, cs]))
        act[:, cs] = a.astype(bf16)
        slope[:, cs] = s.astype(bf16)
        return 0
    lax.fori_loop(0, FF // MC, fwd_mlp, 0)
    loads["wout"].wait()
    def mcf(i, _):
        r = cols(i, 768)
        v = dot(wout[r, :], wd4t[...], 1, 1)
        hi = v.astype(bf16).astype(f32)
        mc[r, :] = jnp.where(lanes_of(768) % 64 < 32, hi, v - hi).astype(bf16)
        return 0
    lax.fori_loop(0, 4, mcf, 0)
    rawv = dot(act[...], mc[...])
    raw[...] = rawv + pltpu.roll(rawv, 32, 1) + dot(hid[...].astype(bf16), wd4t[...], 1, 1)
    all_arrived()
    def codes(i):
        r = cols(i, RB)
        rawv = raw[r, :]
        inv_len = lax.rsqrt(jnp.sum(rawv * rawv, axis=1, keepdims=True) * 0.25 + 1.0)
        both = jnp.where(live(i) & (lanes_of(RB) % 32 < BITS), 1.0, 0.0)
        return r, inv_len, rawv * inv_len, both
    def count(i, sums):
        r, inv_len, unit, both = codes(i)
        zl = unit * 8.0
        p = jax.nn.sigmoid(zl)
        miss = unit - target[r, :]
        ent = jnp.maximum(zl, 0.0) + jnp.log1p(jnp.exp(-jnp.abs(zl))) - p * zl
        return tuple(s + jnp.sum(v * both, axis=0, keepdims=True) for s, v in zip(sums, (p, ent, miss * miss)))
    sums = lax.fori_loop(0, 768 // RB, count, (jnp.zeros((1, 128), f32),) * 3)
    rows8 = lax.broadcasted_iota(jnp.int32, (8, 128), 0)
    own = x * 4 + y * 2 + c
    s8[own] = jnp.where(rows8 == 0, sums[0], jnp.where(rows8 == 1, sums[1], jnp.where(rows8 == 2, sums[2], 0.0)))
    def tell(ref, slot, i, to):
        return pltpu.make_async_remote_copy(ref.at[slot], ref.at[slot], ssem.at[i], rsem.at[i], device_id=to, device_id_type=MESH)
    tells = [tell(s8, own, i, p) for i, p in enumerate(near())]
    for t in tells: t.start()
    loads["outgrad"].wait()
    def decode(i, _):
        r = cols(i, RB)
        ok = live(i)
        for j in range(6):
            cs = slice(j * 128, (j + 1) * 128)
            dattn[r, cs] = jnp.where(ok, big[r, cs], 0.0).astype(bf16)
        return 0
    lax.fori_loop(0, 768 // RB, decode, 0)
    quantT[...] = dot(target[...].astype(bf16), dattn[...], 0, 0)
    for t in tells: t.wait_recv()
    s = s8[0]
    for i in range(1, 8):
        s = s + s8[i]
    zs[z] = s
    ztells = [tell(zs, z, 7 + i, p) for i, p in enumerate(column())]
    for t in ztells: t.start()
    for t in tells: t.wait_send()
    widen(wide, wup[...].astype(f32))
    unit_s[...] = dot(dattn[...], wide[...].astype(bf16), 1, 1)
    mlpinT[...] = mlpin[...].T
    for t in ztells: t.wait()
    zsum = zs[0] + zs[1] + zs[2] + zs[3]
    bit8 = lanes_of(8) % 32 < BITS
    mean_prob = jnp.where(bit8, zsum / total, 0.5)[0:1]
    odds = jnp.log(mean_prob / (1.0 - mean_prob))
    g0 = lanes_of(8)[0:1] < BITS
    code_ent = jnp.sum(jnp.where(g0, -mean_prob * jnp.log(mean_prob) - (1.0 - mean_prob) * jnp.log(1.0 - mean_prob), 0.0))
    other = jnp.sum(jnp.where(g0, 0.25 * zsum[2:3] + zsum[1:2], 0.0))
    loss_o[0, 0] = other / total - code_ent
    def unit_back(i, _):
        r, inv_len, unit, both = codes(i)
        zl = unit * 8.0
        p = jax.nn.sigmoid(zl)
        gunit = unit_s[r, :] + both * (8.0 * p * (1.0 - p) * (odds - zl) + 0.5 * (unit - target[r, :]))
        graw = inv_len * (gunit - unit * (jnp.sum(gunit * unit, axis=1, keepdims=True) * 0.25))
        draw[r, :] = graw.astype(bf16)
        return 0
    lax.fori_loop(0, 768 // RB, unit_back, 0)
    def put(t, p, v):
        for h in range(2):
            main.put(t % 2, p, v[:, h * 128:(h + 1) * 128], h)
    def mlp(i, _):
        for j in range(6):
            t = 6 * i + j
            cs = cols(t, W)
            d = dot(draw[...], mc[cs, :], 1, 1) * 0.5
            dp = (slope[:, cs].astype(f32) * d).astype(bf16)
            slope[:, cs] = dp
            main.late(t)
            put(j, planar(j), dot(mlpinT[...], dp))
            main.early(t, j % 2)
        return 0
    lax.fori_loop(0, 2, mlp, 0)
    main.late(12)
    drawT[...] = draw[...].T
    for q in range(4):
        big[128 * q:128 * q + 128, :] = dot(drawT[...], act[:, q * D:(q + 1) * D])
    for b in range(8):
        t = big[b // 2 * 128:b // 2 * 128 + 128, b % 2 * 384:b % 2 * 384 + 384].T.reshape(4, 4, 24, 128)
        l4 = lax.broadcasted_iota(jnp.int32, (4, 24, 128), 2) // 32
        s = jnp.where(l4 == 0, t[:, 0], 0.0)
        for j in range(1, 4):
            s = jnp.where(l4 == j, t[:, j], s)
        unit_s[b * 96:(b + 1) * 96, :] = s.reshape(96, 128)
    main.put(0, planar(12), unit_s[...], 0)
    gwd = dot(drawT[...], hid[...].astype(bf16))
    for q in range(4):
        gv = big[128 * q:128 * q + 128, :]
        hi = gv.astype(bf16)
        lo = (gv - hi.astype(f32)).astype(bf16)
        w = wout[q * D:(q + 1) * D, :]
        gwd = gwd + (dot(hi, w) + dot(lo, w))
    r128 = lax.broadcasted_iota(jnp.int32, (128, D), 0)
    smallT[...] = jnp.where(r128 < 32, gwd, quantT[...])
    for i in range(6):
        unit_s[i * 128:(i + 1) * 128, :] = smallT[:, i * 128:(i + 1) * 128].T
    main.put(0, planar(12), unit_s[...], 1)
    main.early(12, 0)
    loads["linv"].start()
    loads["qkv"].start()
    main.late(13)
    def ln2(i, _):
        r = cols(i, 256)
        dn = dot(slope[r, :], win[...], 1, 1)
        nrm, inv = norm_stats(hid[r, :])
        v = norm_back(dn, nrm, inv, g2[...].reshape(1, D)) + dot(draw[r, :], wd4t[...]) * 0.25
        hid[r, :] = v
        dattn[r, :] = v.astype(bf16)
        return 0
    lax.fori_loop(0, 3, ln2, 0)
    loads["wqkv2"].start()
    loads["linv"].wait()
    mlpinT[...] = ctx[...].T
    def dctx(i, _):
        r = cols(i, 256)
        mlpin[r, :] = (dot(dattn[r, :], wao[...], 1, 1) * big[r, :]).astype(bf16)
        return 0
    lax.fori_loop(0, 3, dctx, 0)
    loads["tokens2"].start()
    loads["qkv"].wait()
    loads["tokens2"].wait()
    for i in range(6):
        r = pl.ds(i * 128, 128)
        nrm, inv = norm_stats(big[r, :])
        ainT[:, i * 128:(i + 1) * 128] = (nrm * g1[...].reshape(1, D)).astype(bf16).T
    def group(g, _):
        t0 = 13 + 4 * g
        main.late(t0 + 1)
        put(1, planar(13), dot(mlpinT[...], dattn[:, cols(g, W)]))
        main.early(t0, 1)
        def image(img, _):
            load_e(g, img).wait()
            r = pl.ds(pl.multiple_of(img * SEQ, SEQ), SEQ)
            for j in range(2):
                o = g * 2 + j
                q2, k2, v2 = heads_of(img, o)
                cs = cols(o, 128)
                d2, c2 = mlpin[r, cs], ctx[r, cs]
                prod = d2.astype(f32) * c2.astype(f32)
                zero_ = jnp.zeros_like(q2)
                dq = dk = dv = None
                for h in range(2):
                    mine = low if h == 0 else jnp.logical_not(low)
                    pick = lambda a: jnp.where(mine, a, zero_)
                    dh = pick(d2)
                    ev = e[img, 2 * j + h]
                    dd = jnp.sum(jnp.where(mine, prod, 0.0), axis=1, keepdims=True)
                    ds = (ev.astype(f32) * (dot(dh, v2, 1, 1) - dd)).astype(bf16)
                    a, b, cc = dot(ds, pick(k2)), dot(ds, pick(q2), 0, 0), dot(ev, dh, 0, 0)
                    dq, dk, dv = (a, b, cc) if h == 0 else (dq + a, dk + b, dv + cc)
                for b, v in enumerate((dq * 0.125, dk, dv)):
                    act[r, pl.ds(pl.multiple_of(b * D + o * 128, 128), 128)] = v.astype(bf16)
            @pl.when(g < 2)
            def _():
                load_e(g + 1, img).start()
            main.late(t0 + 2 + img)
            return 0
        lax.fori_loop(0, 2, image, 0)
        for j in range(3):
            put(j, planar(14 + j), dot(ainT[...], act[:, pl.ds(pl.multiple_of(j * D + g * W, W), W)]))
            main.early(t0 + 1 + j, j % 2)
            if j == 1:
                main.late(t0 + 4)
        return 0
    lax.fori_loop(0, 3, group, 0)
    main.early(25, 1)
    main.late(26)
    loads["wqkv2"].wait()
    def ln1(i, _):
        r = cols(i, 256)
        dn = dot(act[r, :3 * D], win[:, :3 * D], 1, 1)
        nrm, inv = norm_stats(big[r, :])
        hid[r, :] += norm_back(dn, nrm, inv, g1[...].reshape(1, D))
        main.late(27 + i)
        return 0
    lax.fori_loop(0, 3, ln1, 0)
    saves["gtok"].start()
    for t in range(30, CHUNKS + LAGS[5]):
        main.late(t)
    saves["gtok"].wait()

def train(*args):
    T = 768
    any_, vm, sm = pl.BlockSpec(memory_space=pl.ANY), pl.BlockSpec(memory_space=pltpu.VMEM), pl.BlockSpec(memory_space=pltpu.SMEM)
    V, S = pltpu.VMEM, pltpu.SemaphoreType.DMA
    shapes = [((T, D), f32), ((1, 1), f32), ((CHUNKS, 24, W), f32), ((3 * T, D), bf16), ((24, SEQ, SEQ), bf16), ((T, D), f32)]
    return pl.pallas_call(train_kernel,
        out_shape=[jax.ShapeDtypeStruct(*s) for s in shapes],
        in_specs=[sm] + [vm] * 5 + [any_] * 6,
        out_specs=[any_, sm, vm] + [any_] * 3,
        scratch_shapes=[V((T, D), f32), V((T, D), f32), V((D, FF), bf16), V((FF, D), bf16), V((D, D), bf16), V((2, 4, SEQ, SEQ), bf16),
            V((T, D), bf16), V((T, D), bf16), V((T, FF), bf16), V((T, FF), bf16), V((D, T), bf16), V((D, T), bf16), V((T, D), bf16),
            V((T, 128), bf16), V((128, T), bf16), V((T, 128), f32), V((T, 128), f32), V((T, 128), f32), V((FF, 128), bf16),
            V((128, D), f32), V((128, D), bf16), V((128, D), f32), V((128, D), f32), V((8, 8, 128), f32), V((4, 8, 128), f32),
            S((10,)), S((3,)), S((10,)), S((10,)), S((4,))] + scatter_bufs(),
        compiler_params=pltpu.CompilerParams(vmem_limit_bytes=64 << 20, collective_id=1, has_side_effects=True),
        name="train")(*args)

PIECES = 4
def finish_kernel(scale, counts, gtok_i, loss_i, wqkv_h, win_h, grads, wdownT, g1, g2, bitsT, wup,
                  dec_h, gtok_o, loss_o, gln1, gwqkv, gwao, gln2, gwin, gwout, gwdown, gwup, wq, wi, wide, held, dec, sem, csem):
    part = lambda i: pl.ds(i * (768 // PIECES), 768 // PIECES)
    take = [pltpu.make_async_copy(gtok_i.at[part(i)], held.at[part(i)], csem.at[0, i]) for i in range(PIECES)]
    give = [pltpu.make_async_copy(held.at[part(i)], gtok_o.at[part(i)], csem.at[1, i]) for i in range(PIECES)]
    show = [pltpu.make_async_copy(dec.at[part(i)], dec_h.at[part(i)], csem.at[2, i]) for i in range(PIECES)]
    for t in take: t.start()
    me = lax.axis_index("dp") * lax.axis_size("replica") + lax.axis_index("replica")
    start = pl.multiple_of((me * 24) // 16 * 16, 16)
    reads = [pltpu.make_async_copy(h.at[pl.ds(start, 32)], v, sem.at[i]) for i, (h, v) in ((0, (wqkv_h, wq)), (1, (win_h, wi)))]
    for r in reads: r.start()
    loss_o[0, 0] = loss_i[0, 0]
    n0, n1 = counts[2 * me], counts[2 * me + 1]
    widen(wide, wup[...].astype(f32))
    up = wide[...].astype(bf16)
    widen(wide, (2.0 * bitsT[...].astype(f32) - 1.0) * BITS ** -0.5)
    target = (wide[...].T * 0.25).astype(bf16)
    rows = 768 // PIECES
    for i in range(PIECES):
        row = lax.broadcasted_iota(jnp.int32, (rows, D), 0) + i * rows
        live = row < jnp.where(row < SEQ, n0, n1 + SEQ)
        dec[part(i), :] = jnp.where(live, dot(target[i * rows:(i + 1) * rows], up), 0.0)
        show[i].start()
        take[i].wait()
        give[i].start()
    for k in range(12):
        gwin[:, k * W:(k + 1) * W] = grads[k] * scale
    for g in range(3):
        gwao[:, g * W:(g + 1) * W] = grads[13 + 4 * g] * scale
        for j in range(3):
            gwqkv[:, j * D + g * W:j * D + (g + 1) * W] = grads[14 + 4 * g + j] * scale
    widen(wide, wdownT[...].astype(f32))
    wd = wide[...].astype(bf16)
    code, other = grads[12, :, :128] * scale, grads[12, :, 128:] * scale
    lane = lanes_of(24)
    for j in range(4):
        v = jnp.where(lane // 32 == j, code, 0.0)
        hi = v.astype(bf16)
        lo = (v - hi.astype(f32)).astype(bf16)
        gwout[24 * j:24 * j + 24, :] = dot(hi, wd) + dot(lo, wd)
    gwdown[...] = other[:, :BITS]
    for r in reads: r.wait()
    odd = me % 2
    own = lax.broadcasted_iota(jnp.int32, (24, D), 1) == lax.broadcasted_iota(jnp.int32, (24, D), 0) + me * 24
    def gain(weights, grad, g, lane_at, into):
        w = weights[...].astype(f32)
        w = jnp.where(odd == 1, w[8:32], w[0:24])
        mine = jnp.sum(jnp.where(own, g[...].reshape(1, D), 0.0), axis=1, keepdims=True)
        return jnp.where(lane == lane_at, jnp.sum(w * grad[...], axis=1, keepdims=True) / mine, into)
    flat = gain(wi, gwin, g2, 65, gain(wq, gwqkv, g1, 64, other))
    turned = jnp.concatenate([flat, jnp.zeros((104, 128), f32)], axis=0).T
    gwup[...] = turned[32:32 + BITS, :24]
    gln1[...] = turned[64:65, :24]
    gln2[...] = turned[65:66, :24]
    for t in give + show: t.wait()

def finish(scale, counts, gtok, *rest):
    any_, vm, sm = pl.BlockSpec(memory_space=pl.ANY), pl.BlockSpec(memory_space=pltpu.VMEM), pl.BlockSpec(memory_space=pltpu.SMEM)
    shapes = [gtok.shape, gtok.shape, (1, 1), (1, 24), (24, 3 * D), (24, D), (1, 24), (24, FF), (96, D), (24, BITS), (BITS, 24)]
    return pl.pallas_call(functools.partial(finish_kernel, scale),
        out_shape=[jax.ShapeDtypeStruct(s, f32) for s in shapes],
        in_specs=[sm, any_, sm, any_, any_] + [vm] * 6,
        out_specs=[any_, any_, sm] + [vm] * 8,
        scratch_shapes=[pltpu.VMEM((32, 3 * D), bf16), pltpu.VMEM((32, FF), bf16), pltpu.VMEM((128, D), f32), pltpu.VMEM(gtok.shape, f32), pltpu.VMEM(gtok.shape, f32),
            pltpu.SemaphoreType.DMA((2,)), pltpu.SemaphoreType.DMA((3, PIECES))],
        name="finish")(counts, gtok, *rest)

def kernel_body(tokens, counts, bits, outgrad, g1, wqkv, wao, g2, win, wout, wdown, wup):
    bitsT, wdownT = bits.T, wdown.T
    gtok, loss, grads = train(counts, bitsT, wup, wdownT, g1, g2, tokens, outgrad, wqkv, wao, win, wout)[:3]
    scale = (tokens.shape[0] * lax.axis_size(("dp", "replica"))) ** -0.5
    decoded, gtok, loss, gln1, gwqkv, gwao, gln2, gwin, gwout, gwdown, gwup = finish(scale, counts, gtok, loss, wqkv, win, grads, wdownT, g1, g2, bitsT, wup)
    return (decoded, loss.reshape(()), gtok, gln1.reshape(24), gwqkv, gwao, gln2.reshape(24), gwin, gwout, gwdown, gwup)

eps_norm = 1e-06
neg_big = -1e30
sharpness = 8.0
commit_weight = 0.25


def exact_gelu(values):
    return jax.nn.gelu(values, approximate=False)


def layer_norm(values, gain):
    centered = values - jnp.mean(values, axis=-1, keepdims=True)
    inv_std = lax.rsqrt(jnp.mean(centered * centered, axis=-1, keepdims=True) + eps_norm)
    normed = centered * inv_std
    return (normed * gain, normed, inv_std)


def plain_norm_back(grad_out, normed, inv_std, gain):
    grad_normed = grad_out * gain
    grad_gain = jnp.sum(grad_out * normed, axis=0)
    spread_part = jnp.mean(grad_normed * normed, axis=-1, keepdims=True)
    grad_in = inv_std * (
        grad_normed - jnp.mean(grad_normed, axis=-1, keepdims=True) - normed * spread_part
    )
    return (grad_in, grad_gain)


def inner_rows(left, right):
    return lax.dot_general(
        left, right, (((0,), (0,)), ((), ())), preferred_element_type=jnp.float32
    )


def times_transposed(left, right):
    return lax.dot_general(
        left, right, (((1,), (1,)), ((), ())), preferred_element_type=jnp.float32
    )


def attention_logits(queries, key_rows, key_valid):
    scores = jnp.einsum("bqhd,bkhd->bhqk", queries, key_rows, preferred_element_type=jnp.float32)
    return jnp.where(key_valid, scores * HEAD ** (-0.5), neg_big)


def plain_body(
    tokens,
    patch_counts,
    code_bits,
    out_grad,
    ln1_gain,
    w_qkv,
    w_attn_out,
    ln2_gain,
    w_mlp_in,
    w_mlp_out,
    w_down,
    w_up,
):
    row_count = tokens.shape[0]
    images = row_count // SEQ
    width_all = tokens.shape[1]
    first_image = lax.axis_index(("dp", "replica")) * images
    counts = lax.dynamic_slice_in_dim(patch_counts, first_image, images)
    total_count = jnp.sum(patch_counts).astype(jnp.float32)
    valid_slots = jnp.arange(SEQ, dtype=jnp.int32)[None, :] < counts[:, None]
    key_valid = valid_slots[:, None, None, :]
    row_valid = valid_slots.reshape(row_count).astype(jnp.float32)[:, None]
    target = (2.0 * code_bits.astype(jnp.float32) - 1.0) * BITS ** (-0.5)
    normed1_out, normed1, inv_std1 = layer_norm(tokens, ln1_gain)
    attn_in = normed1_out.astype(jnp.bfloat16)
    qkv_rows = jnp.dot(attn_in, w_qkv, preferred_element_type=jnp.float32).astype(jnp.bfloat16)
    qkv_rows = qkv_rows.reshape(images, SEQ, 3, HEADS, HEAD)
    queries = qkv_rows[:, :, 0]
    key_rows = qkv_rows[:, :, 1]
    value_rows = qkv_rows[:, :, 2]
    logits = attention_logits(queries, key_rows, key_valid)
    row_max = jnp.max(logits, axis=-1, keepdims=True)
    weights = jnp.exp(logits - row_max)
    row_total = jnp.sum(weights, axis=-1, keepdims=True)
    log_total = row_max + jnp.log(row_total)
    prob_low = (weights / row_total).astype(jnp.bfloat16)
    context = jnp.einsum(
        "bhqk,bkhd->bqhd", prob_low, value_rows, preferred_element_type=jnp.float32
    )
    context_low = context.astype(jnp.bfloat16).reshape(row_count, width_all)
    hidden1 = tokens + jnp.dot(context_low, w_attn_out, preferred_element_type=jnp.float32)
    normed2_out, normed2, inv_std2 = layer_norm(hidden1, ln2_gain)
    mlp_in = normed2_out.astype(jnp.bfloat16)
    pre_act = jnp.dot(mlp_in, w_mlp_in, preferred_element_type=jnp.float32)
    activation, gelu_back = jax.vjp(exact_gelu, pre_act)
    activation_low = activation.astype(jnp.bfloat16)
    hidden2 = hidden1 + jnp.dot(activation_low, w_mlp_out, preferred_element_type=jnp.float32)
    hidden2_low = hidden2.astype(jnp.bfloat16)
    raw_code = jnp.dot(hidden2_low, w_down, preferred_element_type=jnp.float32)
    inv_len = lax.rsqrt(jnp.sum(raw_code * raw_code, axis=-1, keepdims=True) + 1.0)
    unit_code = raw_code * inv_len
    quant_low = target.astype(jnp.bfloat16)
    decoded = row_valid * jnp.dot(quant_low, w_up, preferred_element_type=jnp.float32)
    logit_bits = unit_code * sharpness
    soft_prob = jax.nn.sigmoid(logit_bits)
    token_ent = jax.nn.softplus(logit_bits) - soft_prob * logit_bits
    code_miss = unit_code - target
    prob_sum = jnp.sum(soft_prob * row_valid, axis=0)
    ent_sum = jnp.sum(token_ent * row_valid)
    commit_sum = jnp.sum(code_miss * code_miss * row_valid)
    prob_sum, ent_sum, commit_sum = lax.psum((prob_sum, ent_sum, commit_sum), ("dp", "replica"))
    mean_prob = prob_sum / total_count
    code_ent = jnp.sum(
        -mean_prob * jnp.log(mean_prob) - (1.0 - mean_prob) * jnp.log(1.0 - mean_prob)
    )
    entropy_loss = (commit_weight * commit_sum + ent_sum) / total_count - code_ent
    grad_dec_low = (row_valid * out_grad).astype(jnp.bfloat16)
    grad_w_up = inner_rows(quant_low, grad_dec_low)
    grad_quant = times_transposed(grad_dec_low, w_up)
    prob_logit = jnp.log(mean_prob / (1.0 - mean_prob))
    loss_part = (
        sharpness * soft_prob * (1.0 - soft_prob) * (prob_logit - logit_bits)
        + 2.0 * commit_weight * code_miss
    )
    grad_unit = grad_quant + row_valid * loss_part
    grad_raw = inv_len * (
        grad_unit - unit_code * jnp.sum(grad_unit * unit_code, axis=-1, keepdims=True)
    )
    grad_raw_low = grad_raw.astype(jnp.bfloat16)
    grad_w_down = inner_rows(hidden2_low, grad_raw_low)
    grad_hidden2 = times_transposed(grad_raw_low, w_down)
    grad_mlp_low = grad_hidden2.astype(jnp.bfloat16)
    grad_w_mlp_out = inner_rows(activation_low, grad_mlp_low)
    grad_activation = times_transposed(grad_mlp_low, w_mlp_out)
    grad_pre_low = gelu_back(grad_activation)[0].astype(jnp.bfloat16)
    grad_w_mlp_in = inner_rows(mlp_in, grad_pre_low)
    grad_norm2_in = times_transposed(grad_pre_low, w_mlp_in)
    grad_from_norm2, grad_ln2 = plain_norm_back(grad_norm2_in, normed2, inv_std2, ln2_gain)
    grad_hidden1 = grad_hidden2 + grad_from_norm2
    grad_attn_low = grad_hidden1.astype(jnp.bfloat16)
    grad_w_attn_out = inner_rows(context_low, grad_attn_low)
    grad_context = times_transposed(grad_attn_low, w_attn_out).astype(jnp.bfloat16)
    grad_context = grad_context.reshape(images, SEQ, HEADS, HEAD)
    grad_values = jnp.einsum(
        "bhqk,bqhd->bkhd", prob_low, grad_context, preferred_element_type=jnp.float32
    )
    grad_prob = jnp.einsum(
        "bqhd,bkhd->bhqk", grad_context, value_rows, preferred_element_type=jnp.float32
    )
    attn_prob = jnp.exp(attention_logits(queries, key_rows, key_valid) - log_total)
    grad_scores = (
        attn_prob
        * (grad_prob - jnp.sum(grad_prob * attn_prob, axis=-1, keepdims=True))
        * HEAD ** (-0.5)
    )
    grad_scores_low = grad_scores.astype(jnp.bfloat16)
    grad_queries = jnp.einsum(
        "bhqk,bkhd->bqhd", grad_scores_low, key_rows, preferred_element_type=jnp.float32
    )
    grad_keys = jnp.einsum(
        "bhqk,bqhd->bkhd", grad_scores_low, queries, preferred_element_type=jnp.float32
    )
    grad_qkv = jnp.stack((grad_queries, grad_keys, grad_values), axis=2).reshape(
        row_count, 3 * width_all
    )
    grad_qkv_low = grad_qkv.astype(jnp.bfloat16)
    grad_w_qkv = inner_rows(attn_in, grad_qkv_low)
    grad_norm1_in = times_transposed(grad_qkv_low, w_qkv)
    grad_from_norm1, grad_ln1 = plain_norm_back(grad_norm1_in, normed1, inv_std1, ln1_gain)
    grad_tokens = grad_hidden1 + grad_from_norm1
    summed = (
        lax.psum_scatter(grad_ln1, ("dp", "replica"), scatter_dimension=0, tiled=True),
        lax.psum_scatter(grad_w_qkv, ("dp", "replica"), scatter_dimension=0, tiled=True),
        lax.psum_scatter(grad_w_attn_out, ("dp", "replica"), scatter_dimension=0, tiled=True),
        lax.psum_scatter(grad_ln2, ("dp", "replica"), scatter_dimension=0, tiled=True),
        lax.psum_scatter(grad_w_mlp_in, ("dp", "replica"), scatter_dimension=0, tiled=True),
        lax.psum_scatter(grad_w_mlp_out, ("dp", "replica"), scatter_dimension=0, tiled=True),
        lax.psum_scatter(grad_w_down, ("dp", "replica"), scatter_dimension=0, tiled=True),
        lax.psum_scatter(grad_w_up, ("dp", "replica"), scatter_dimension=1, tiled=True),
    )
    grad_scale = (row_count * lax.axis_size(("dp", "replica"))) ** (-0.5)
    return (
        decoded,
        entropy_loss,
        grad_tokens,
        summed[0] * grad_scale,
        summed[1] * grad_scale,
        summed[2] * grad_scale,
        summed[3] * grad_scale,
        summed[4] * grad_scale,
        summed[5] * grad_scale,
        summed[6] * grad_scale,
        summed[7] * grad_scale,
    )


def solution(mesh):
    in_specs = (
        P(("dp", "replica"), None),
        P(),
        P(("dp", "replica"), None),
        P(("dp", "replica"), None),
        P(),
        P(),
        P(),
        P(),
        P(),
        P(),
        P(),
        P(),
    )
    out_specs = (
        P(("dp", "replica"), None),
        P(),
        P(("dp", "replica"), None),
        P(("dp", "replica")),
        P(("dp", "replica"), None),
        P(("dp", "replica"), None),
        P(("dp", "replica")),
        P(("dp", "replica"), None),
        P(("dp", "replica"), None),
        P(("dp", "replica"), None),
        P(None, ("dp", "replica")),
    )
    body = kernel_body if (mesh.shape["dp"], mesh.shape["replica"]) == (8, 4) else plain_body
    return jax.shard_map(body, mesh=mesh, in_specs=in_specs, out_specs=out_specs, check_vma=False)
```

```python
import functools
import math

import jax
import jax.numpy as jnp
from jax import lax
from jax.experimental import pallas as pl
from jax.experimental.pallas import tpu as pltpu
from jax.sharding import PartitionSpec as P

HEADS, HEAD, BITS, SEQ = 12, 64, 18, 384
D, FF = 768, 3072
EPS = 1e-06
bf16, f32 = jnp.bfloat16, jnp.float32

def dot(a, b, ca=1, cb=0):
    return lax.dot_general(a, b, (((ca,), (cb,)), ((), ())), preferred_element_type=f32)

def norm_stats(v):
    mean = jnp.sum(v, axis=1, keepdims=True) * (1.0 / D)
    cen = v - mean
    var = jnp.sum(cen * cen, axis=1, keepdims=True) * (1.0 / D)
    inv = lax.rsqrt(var + EPS)
    return cen * inv, inv

def cols(i, n):
    return pl.ds(pl.multiple_of(i * n, n), n)

def lanes_of(rows, width=128):
    return lax.broadcasted_iota(jnp.int32, (rows, width), 1)

def widen(ref, rows):
    ref[...] = jnp.zeros_like(ref)
    for j in range(4):
        ref[32 * j:32 * j + BITS, :] = rows

def gelu_parts(x):
    cdf = 0.5 + 0.5 * lax.erf(x * math.sqrt(0.5))
    pdf = jnp.exp(x * x * -0.5) * (1.0 / math.sqrt(2.0 * math.pi))
    return x * cdf, cdf + x * pdf

MESH = pl.DeviceIdType.MESH
W = 256
CHUNKS = 25
LAGS = (0, 1, 6, 10, 14, 18)

def place():
    dp, rp = lax.axis_index("dp"), lax.axis_index("replica")
    return dp // 2, dp % 2, rp // 2, rp % 2

def device(z, x, y, c):
    return (z * 2 + x, y * 2 + c)

def near():
    z, x, y, c = place()
    flip = lambda v, n: 1 - v if n else v
    return [device(z, flip(x, n & 4), flip(y, n & 2), flip(c, n & 1)) for n in range(1, 8)]

def column():
    z, x, y, c = place()
    return [device((z + d) % 4, x, y, c) for d in (1, 2, 3)]

def arrive():
    for p in near() + column():
        pl.semaphore_signal(pltpu.get_barrier_semaphore(), inc=1, device_id=p, device_id_type=MESH)

def all_arrived():
    pl.semaphore_wait(pltpu.get_barrier_semaphore(), len(near() + column()))

def planar(k):
    if isinstance(k, int):
        return int(k % 6 == 5 if k <= 12 else (k + 3) % 4 >= 2)
    return jnp.where(k <= 12, jnp.where(lax.rem(k, 6) == 5, 1, 0), jnp.where(lax.rem(k + 3, 4) >= 2, 1, 0))

class Scatter:
    def __init__(self, bufs, result):
        self.g, self.r, (self.send, self.recv) = bufs[0], bufs[1:6], bufs[6:8]
        self.result = result
        self.at = place()
    def route(self, k, h, n):
        z, x, y, c = self.at
        p, zl, zh = planar(k), z % 2, z // 2
        first, other = (x, y) if h == 0 else (y, x)
        def to(flip_first, flip_other, nz):
            f, o = first + flip_first * (1 - 2 * first), other + flip_other * (1 - 2 * other)
            return device(nz, *((f, o) if h == 0 else (o, f)), c)
        lowz, highz = z + 1 - 2 * zl, z + 2 - 4 * zh
        if n == 1:
            return first, to(1, 0, z)
        if n == 2:
            return p * other + (1 - p) * zl, to(0, p, p * z + (1 - p) * lowz)
        if n == 3:
            return p * zl + (1 - p) * zh, to(0, 0, p * lowz + (1 - p) * highz)
        return p * zh + (1 - p) * other, to(0, 1 - p, p * highz + (1 - p) * z)
    def copy(self, k, h, n):
        _, to = self.route(k, h, n)
        bit = self.route(k, h, n)[0]
        i = 2 * n - 1 + h
        return pltpu.make_async_remote_copy(self.r[n - 1].at[k, h, 1 - bit], self.r[n].at[k, h], self.send.at[k, i], self.recv.at[k, i],
                                            device_id=to, device_id_type=MESH)
    def pair(self, k, slot):
        z, x, y, c = self.at
        return pltpu.make_async_remote_copy(self.g.at[slot, 1 - c], self.r[0].at[k], self.send.at[k, 0], self.recv.at[k, 0],
                                            device_id=device(z, x, y, 1 - c), device_id_type=MESH)
    def put(self, slot, p, v, h):
        for o in range(32):
            z, x, y, c = o // 8, o // 4 % 2, o // 2 % 2, o % 2
            f, s = (x, y) if h == 0 else (y, x)
            order = (f, s, z % 2, z // 2) if p else (f, z % 2, z // 2, s)
            self.g[(slot, c, h, *order)] = v[o * 24:o * 24 + 24]
    def kept(self, k, h, n):
        bit, _ = self.route(k, h, n)
        return jnp.where(bit == 0, self.r[n - 1][k, h, 0], self.r[n - 1][k, h, 1])
    def step(self, s, k):
        for h in range(2):
            self.copy(k, h, s - 1).wait()
            v = self.r[s - 1][k, h] + self.kept(k, h, s - 1)
            if s == 5:
                self.result(k, h, v)
            else:
                self.r[s - 1][k, h] = v
                self.copy(k, h, s).start()
    def begin(self, k, slot):
        self.pair(k, slot).start()
    def join(self, k, slot):
        self.pair(k, slot).wait()
        self.r[0][k] += self.g[slot, self.at[3]]
        for h in range(2):
            self.copy(k, h, 1).start()
    def late(self, t):
        for s in (5, 4, 3, 2):
            k = t - LAGS[s]
            if isinstance(t, int):
                if 0 <= k < CHUNKS:
                    self.step(s, k)
            else:
                pl.when(k >= 0)(functools.partial(self.step, s, k))
    def early(self, t, slot):
        k = t - 1
        if isinstance(t, int):
            if k >= 0:
                self.join(k, 1 - slot)
            if t < CHUNKS:
                self.begin(t, slot)
        else:
            pl.when(k >= 0)(functools.partial(self.join, k, 1 - slot))
            self.begin(t, slot)

def scatter_bufs():
    blocks = [(2,) * (5 - n) for n in range(5)]
    return [pltpu.VMEM((2, 2, 2, 2, 2, 2, 2, 24, 128), f32)] + [pltpu.VMEM((CHUNKS,) + b + (24, 128), f32) for b in blocks] + [pltpu.SemaphoreType.DMA((CHUNKS, 9))] * 2

def norm_back(grad, normed, inv, gain):
    gn = grad * gain
    spread = jnp.sum(gn * normed, axis=1, keepdims=True) * (1.0 / D)
    mean = jnp.sum(gn, axis=1, keepdims=True) * (1.0 / D)
    return inv * (gn - mean - normed * spread)

RB = 256
MC = 1024
def train_kernel(counts, bitsT, wup, wdownT, g1, g2, tokens_h, outgrad_h, wqkv_h, wao_h, win_h, wout_h,
                 gtok_h, loss_o, grads_o, qkv_h, e_h, linv_h,
                 hid, big, win, wout, wao, e, ctx, mlpin, act, slope, mlpinT, ainT, dattn, draw, drawT, unit_s, target, raw, mc,
                 wide, wd4t, smallT, quantT, s8, zs, sem, osem, ssem, rsem, esem, *bufs):
    def result(k, h, v):
        grads_o[k, :, h * 128:(h + 1) * 128] = v
    main = Scatter(bufs, result)
    z, x, y, c = place()
    loads = {n: pltpu.make_async_copy(src, dst, sem.at[i]) for i, (n, src, dst) in enumerate((
        ("wao", wao_h, wao), ("win", win_h, win), ("wout", wout_h, wout),
        ("outgrad", outgrad_h, big), ("qkv", qkv_h, wout.at[:3 * D]), ("linv", linv_h, big), ("wqkv2", wqkv_h, win.at[:, :3 * D]), ("tokens2", tokens_h, big)))}
    blocks = [pl.ds(i * 256, 256) for i in range(3)]
    parts = [pl.ds(i * D, D) for i in range(3)]
    rows_in = [pltpu.make_async_copy(tokens_h.at[b], hid.at[b], sem.at[8 + i]) for i, b in enumerate(blocks)]
    cols_in = [pltpu.make_async_copy(wqkv_h.at[:, b], win.at[:, b], sem.at[11 + i]) for i, b in enumerate(parts)]
    saves = {n: pltpu.make_async_copy(src, dst, osem.at[i]) for i, (n, src, dst) in enumerate((
        ("qkv", wout.at[:3 * D], qkv_h), ("linv", big, linv_h), ("gtok", hid, gtok_h)))}
    def load_e(g, img):
        return pltpu.make_async_copy(e_h.at[pl.ds(img * HEADS + g * 4, 4)], e.at[img], esem.at[img])
    def save_e(g, img):
        return pltpu.make_async_copy(e.at[img], e_h.at[pl.ds(img * HEADS + g * 4, 4)], esem.at[2 + img])
    arrive()
    for l in rows_in + cols_in + [loads["wao"]]:
        l.start()
    first = (lax.axis_index("dp") * lax.axis_size("replica") + lax.axis_index("replica")) * 2
    n0, n1 = counts[first], counts[first + 1]
    total = lax.fori_loop(0, counts.shape[0], lambda i, a: a + counts[i], jnp.int32(0)).astype(f32)
    def live(i):
        row = lax.broadcasted_iota(jnp.int32, (RB, 128), 0) + i * RB
        return row < jnp.where(row < SEQ, n0, n1 + SEQ)
    low = lanes_of(SEQ) < HEAD
    widen(wide, wdownT[...].astype(f32))
    wd4t[...] = wide[...].astype(bf16)
    widen(wide, (2.0 * bitsT[...].astype(f32) - 1.0) * BITS ** -0.5)
    target[...] = wide[...].T
    for l, r in zip(rows_in, blocks):
        l.wait()
        n, _inv = norm_stats(hid[r, :])
        dattn[r, :] = (n * g1[...].reshape(1, D)).astype(bf16)
    for i, (l, b) in enumerate(zip(cols_in, parts)):
        l.wait()
        v = dot(dattn[...], win[:, b])
        wout[b, :] = (v * 0.125 if i == 0 else v).astype(bf16)
    loads["win"].start()
    saves["qkv"].start()
    def heads_of(img, o):
        return (wout[pl.ds(pl.multiple_of(b * D + img * SEQ, 128), SEQ), cols(o, 128)] for b in range(3))
    def att(g, _):
        def image(img, _):
            n = jnp.where(img == 0, n0, n1)
            r = pl.ds(pl.multiple_of(img * SEQ, SEQ), SEQ)
            ok = lax.broadcasted_iota(jnp.int32, (1, SEQ), 1) < n
            one = jnp.ones((SEQ, 128), bf16)
            @pl.when(g > 0)
            def _():
                save_e(g - 1, img).wait()
            for j in range(2):
                o = g * 2 + j
                q2, k2, v2 = heads_of(img, o)
                zero = jnp.zeros_like(q2)
                vo = jnp.concatenate([v2, one], axis=1)
                res = []
                for h in range(2):
                    q = jnp.where(low, q2, zero) if h == 0 else jnp.where(low, zero, q2)
                    s = jnp.where(ok, dot(q, k2, 1, 1), -1e30)
                    m = jnp.max(s, axis=1, keepdims=True)
                    p = jnp.exp(s - m).astype(bf16)
                    e[img, 2 * j + h] = p
                    ov = dot(p, vo)
                    inv = 1.0 / ov[:, 128:]
                    res.append((ov[:, :128] * inv, inv))
                ctx[r, cols(o, 128)] = jnp.where(low, res[0][0], res[1][0]).astype(bf16)
                big[r, cols(o, 128)] = jnp.where(low, res[0][1], res[1][1])
            save_e(g, img).start()
            return 0
        lax.fori_loop(0, 2, image, 0)
        return 0
    lax.fori_loop(0, 3, att, 0)
    saves["linv"].start()
    saves["qkv"].wait()
    loads["wout"].start()
    loads["wao"].wait()
    def ao(i, _):
        r = cols(i, 256)
        h = hid[r, :] + dot(ctx[r, :], wao[...])
        hid[r, :] = h
        n, _inv = norm_stats(h)
        mlpin[r, :] = (n * g2[...].reshape(1, D)).astype(bf16)
        return 0
    lax.fori_loop(0, 3, ao, 0)
    saves["linv"].wait()
    loads["outgrad"].start()
    loads["win"].wait()
    for img in range(2):
        save_e(2, img).wait()
        load_e(0, img).start()
    def fwd_mlp(i, _):
        cs = cols(i, MC)
        a, s = gelu_parts(dot(mlpin[...], win[:, cs]))
        act[:, cs] = a.astype(bf16)
        slope[:, cs] = s.astype(bf16)
        return 0
    lax.fori_loop(0, FF // MC, fwd_mlp, 0)
    loads["wout"].wait()
    def mcf(i, _):
        r = cols(i, 768)
        v = dot(wout[r, :], wd4t[...], 1, 1)
        hi = v.astype(bf16).astype(f32)
        mc[r, :] = jnp.where(lanes_of(768) % 64 < 32, hi, v - hi).astype(bf16)
        return 0
    lax.fori_loop(0, 4, mcf, 0)
    rawv = dot(act[...], mc[...])
    raw[...] = rawv + pltpu.roll(rawv, 32, 1) + dot(hid[...].astype(bf16), wd4t[...], 1, 1)
    all_arrived()
    def codes(i):
        r = cols(i, RB)
        rawv = raw[r, :]
        inv_len = lax.rsqrt(jnp.sum(rawv * rawv, axis=1, keepdims=True) * 0.25 + 1.0)
        both = jnp.where(live(i) & (lanes_of(RB) % 32 < BITS), 1.0, 0.0)
        return r, inv_len, rawv * inv_len, both
    def count(i, sums):
        r, inv_len, unit, both = codes(i)
        zl = unit * 8.0
        p = jax.nn.sigmoid(zl)
        miss = unit - target[r, :]
        ent = jnp.maximum(zl, 0.0) + jnp.log1p(jnp.exp(-jnp.abs(zl))) - p * zl
        return tuple(s + jnp.sum(v * both, axis=0, keepdims=True) for s, v in zip(sums, (p, ent, miss * miss)))
    sums = lax.fori_loop(0, 768 // RB, count, (jnp.zeros((1, 128), f32),) * 3)
    rows8 = lax.broadcasted_iota(jnp.int32, (8, 128), 0)
    own = x * 4 + y * 2 + c
    s8[own] = jnp.where(rows8 == 0, sums[0], jnp.where(rows8 == 1, sums[1], jnp.where(rows8 == 2, sums[2], 0.0)))
    def tell(ref, slot, i, to):
        return pltpu.make_async_remote_copy(ref.at[slot], ref.at[slot], ssem.at[i], rsem.at[i], device_id=to, device_id_type=MESH)
    tells = [tell(s8, own, i, p) for i, p in enumerate(near())]
    for t in tells: t.start()
    loads["outgrad"].wait()
    def decode(i, _):
        r = cols(i, RB)
        ok = live(i)
        for j in range(6):
            cs = slice(j * 128, (j + 1) * 128)
            dattn[r, cs] = jnp.where(ok, big[r, cs], 0.0).astype(bf16)
        return 0
    lax.fori_loop(0, 768 // RB, decode, 0)
    quantT[...] = dot(target[...].astype(bf16), dattn[...], 0, 0)
    for t in tells: t.wait_recv()
    s = s8[0]
    for i in range(1, 8):
        s = s + s8[i]
    zs[z] = s
    ztells = [tell(zs, z, 7 + i, p) for i, p in enumerate(column())]
    for t in ztells: t.start()
    for t in tells: t.wait_send()
    widen(wide, wup[...].astype(f32))
    unit_s[...] = dot(dattn[...], wide[...].astype(bf16), 1, 1)
    mlpinT[...] = mlpin[...].T
    for t in ztells: t.wait()
    zsum = zs[0] + zs[1] + zs[2] + zs[3]
    bit8 = lanes_of(8) % 32 < BITS
    mean_prob = jnp.where(bit8, zsum / total, 0.5)[0:1]
    odds = jnp.log(mean_prob / (1.0 - mean_prob))
    g0 = lanes_of(8)[0:1] < BITS
    code_ent = jnp.sum(jnp.where(g0, -mean_prob * jnp.log(mean_prob) - (1.0 - mean_prob) * jnp.log(1.0 - mean_prob), 0.0))
    other = jnp.sum(jnp.where(g0, 0.25 * zsum[2:3] + zsum[1:2], 0.0))
    loss_o[0, 0] = other / total - code_ent
    def unit_back(i, _):
        r, inv_len, unit, both = codes(i)
        zl = unit * 8.0
        p = jax.nn.sigmoid(zl)
        gunit = unit_s[r, :] + both * (8.0 * p * (1.0 - p) * (odds - zl) + 0.5 * (unit - target[r, :]))
        graw = inv_len * (gunit - unit * (jnp.sum(gunit * unit, axis=1, keepdims=True) * 0.25))
        draw[r, :] = graw.astype(bf16)
        return 0
    lax.fori_loop(0, 768 // RB, unit_back, 0)
    def put(t, p, v):
        for h in range(2):
            main.put(t % 2, p, v[:, h * 128:(h + 1) * 128], h)
    def mlp(i, _):
        for j in range(6):
            t = 6 * i + j
            cs = cols(t, W)
            d = dot(draw[...], mc[cs, :], 1, 1) * 0.5
            dp = (slope[:, cs].astype(f32) * d).astype(bf16)
            slope[:, cs] = dp
            main.late(t)
            put(j, planar(j), dot(mlpinT[...], dp))
            main.early(t, j % 2)
        return 0
    lax.fori_loop(0, 2, mlp, 0)
    main.late(12)
    drawT[...] = draw[...].T
    for q in range(4):
        big[128 * q:128 * q + 128, :] = dot(drawT[...], act[:, q * D:(q + 1) * D])
    for b in range(8):
        t = big[b // 2 * 128:b // 2 * 128 + 128, b % 2 * 384:b % 2 * 384 + 384].T.reshape(4, 4, 24, 128)
        l4 = lax.broadcasted_iota(jnp.int32, (4, 24, 128), 2) // 32
        s = jnp.where(l4 == 0, t[:, 0], 0.0)
        for j in range(1, 4):
            s = jnp.where(l4 == j, t[:, j], s)
        unit_s[b * 96:(b + 1) * 96, :] = s.reshape(96, 128)
    main.put(0, planar(12), unit_s[...], 0)
    gwd = dot(drawT[...], hid[...].astype(bf16))
    for q in range(4):
        gv = big[128 * q:128 * q + 128, :]
        hi = gv.astype(bf16)
        lo = (gv - hi.astype(f32)).astype(bf16)
        w = wout[q * D:(q + 1) * D, :]
        gwd = gwd + (dot(hi, w) + dot(lo, w))
    r128 = lax.broadcasted_iota(jnp.int32, (128, D), 0)
    smallT[...] = jnp.where(r128 < 32, gwd, quantT[...])
    for i in range(6):
        unit_s[i * 128:(i + 1) * 128, :] = smallT[:, i * 128:(i + 1) * 128].T
    main.put(0, planar(12), unit_s[...], 1)
    main.early(12, 0)
    loads["linv"].start()
    loads["qkv"].start()
    main.late(13)
    def ln2(i, _):
        r = cols(i, 256)
        dn = dot(slope[r, :], win[...], 1, 1)
        nrm, inv = norm_stats(hid[r, :])
        v = norm_back(dn, nrm, inv, g2[...].reshape(1, D)) + dot(draw[r, :], wd4t[...]) * 0.25
        hid[r, :] = v
        dattn[r, :] = v.astype(bf16)
        return 0
    lax.fori_loop(0, 3, ln2, 0)
    loads["wqkv2"].start()
    loads["linv"].wait()
    mlpinT[...] = ctx[...].T
    def dctx(i, _):
        r = cols(i, 256)
        mlpin[r, :] = (dot(dattn[r, :], wao[...], 1, 1) * big[r, :]).astype(bf16)
        return 0
    lax.fori_loop(0, 3, dctx, 0)
    loads["tokens2"].start()
    loads["qkv"].wait()
    loads["tokens2"].wait()
    for i in range(6):
        r = pl.ds(i * 128, 128)
        nrm, inv = norm_stats(big[r, :])
        ainT[:, i * 128:(i + 1) * 128] = (nrm * g1[...].reshape(1, D)).astype(bf16).T
    def group(g, _):
        t0 = 13 + 4 * g
        main.late(t0 + 1)
        put(1, planar(13), dot(mlpinT[...], dattn[:, cols(g, W)]))
        main.early(t0, 1)
        def image(img, _):
            load_e(g, img).wait()
            r = pl.ds(pl.multiple_of(img * SEQ, SEQ), SEQ)
            for j in range(2):
                o = g * 2 + j
                q2, k2, v2 = heads_of(img, o)
                cs = cols(o, 128)
                d2, c2 = mlpin[r, cs], ctx[r, cs]
                prod = d2.astype(f32) * c2.astype(f32)
                zero_ = jnp.zeros_like(q2)
                dq = dk = dv = None
                for h in range(2):
                    mine = low if h == 0 else jnp.logical_not(low)
                    pick = lambda a: jnp.where(mine, a, zero_)
                    dh = pick(d2)
                    ev = e[img, 2 * j + h]
                    dd = jnp.sum(jnp.where(mine, prod, 0.0), axis=1, keepdims=True)
                    ds = (ev.astype(f32) * (dot(dh, v2, 1, 1) - dd)).astype(bf16)
                    a, b, cc = dot(ds, pick(k2)), dot(ds, pick(q2), 0, 0), dot(ev, dh, 0, 0)
                    dq, dk, dv = (a, b, cc) if h == 0 else (dq + a, dk + b, dv + cc)
                for b, v in enumerate((dq * 0.125, dk, dv)):
                    act[r, pl.ds(pl.multiple_of(b * D + o * 128, 128), 128)] = v.astype(bf16)
            @pl.when(g < 2)
            def _():
                load_e(g + 1, img).start()
            main.late(t0 + 2 + img)
            return 0
        lax.fori_loop(0, 2, image, 0)
        for j in range(3):
            put(j, planar(14 + j), dot(ainT[...], act[:, pl.ds(pl.multiple_of(j * D + g * W, W), W)]))
            main.early(t0 + 1 + j, j % 2)
            if j == 1:
                main.late(t0 + 4)
        return 0
    lax.fori_loop(0, 3, group, 0)
    main.early(25, 1)
    main.late(26)
    loads["wqkv2"].wait()
    def ln1(i, _):
        r = cols(i, 256)
        dn = dot(act[r, :3 * D], win[:, :3 * D], 1, 1)
        nrm, inv = norm_stats(big[r, :])
        hid[r, :] += norm_back(dn, nrm, inv, g1[...].reshape(1, D))
        main.late(27 + i)
        return 0
    lax.fori_loop(0, 3, ln1, 0)
    saves["gtok"].start()
    for t in range(30, CHUNKS + LAGS[5]):
        main.late(t)
    saves["gtok"].wait()

def train(*args):
    T = 768
    any_, vm, sm = pl.BlockSpec(memory_space=pl.ANY), pl.BlockSpec(memory_space=pltpu.VMEM), pl.BlockSpec(memory_space=pltpu.SMEM)
    V, S = pltpu.VMEM, pltpu.SemaphoreType.DMA
    shapes = [((T, D), f32), ((1, 1), f32), ((CHUNKS, 24, W), f32), ((3 * T, D), bf16), ((24, SEQ, SEQ), bf16), ((T, D), f32)]
    return pl.pallas_call(train_kernel,
        out_shape=[jax.ShapeDtypeStruct(*s) for s in shapes],
        in_specs=[sm] + [vm] * 5 + [any_] * 6,
        out_specs=[any_, sm, vm] + [any_] * 3,
        scratch_shapes=[V((T, D), f32), V((T, D), f32), V((D, FF), bf16), V((FF, D), bf16), V((D, D), bf16), V((2, 4, SEQ, SEQ), bf16),
            V((T, D), bf16), V((T, D), bf16), V((T, FF), bf16), V((T, FF), bf16), V((D, T), bf16), V((D, T), bf16), V((T, D), bf16),
            V((T, 128), bf16), V((128, T), bf16), V((T, 128), f32), V((T, 128), f32), V((T, 128), f32), V((FF, 128), bf16),
            V((128, D), f32), V((128, D), bf16), V((128, D), f32), V((128, D), f32), V((8, 8, 128), f32), V((4, 8, 128), f32),
            S((14,)), S((3,)), S((10,)), S((10,)), S((4,))] + scatter_bufs(),
        compiler_params=pltpu.CompilerParams(vmem_limit_bytes=64 << 20, collective_id=1, has_side_effects=True),
        name="train")(*args)

PIECES = 4
def finish_kernel(scale, counts, gtok_i, loss_i, wqkv_h, win_h, grads, wdownT, g1, g2, bitsT, wup,
                  dec_h, gtok_o, loss_o, gln1, gwqkv, gwao, gln2, gwin, gwout, gwdown, gwup, wq, wi, wide, held, dec, sem, csem):
    part = lambda i: pl.ds(i * (768 // PIECES), 768 // PIECES)
    take = [pltpu.make_async_copy(gtok_i.at[part(i)], held.at[part(i)], csem.at[0, i]) for i in range(PIECES)]
    give = [pltpu.make_async_copy(held.at[part(i)], gtok_o.at[part(i)], csem.at[1, i]) for i in range(PIECES)]
    show = [pltpu.make_async_copy(dec.at[part(i)], dec_h.at[part(i)], csem.at[2, i]) for i in range(PIECES)]
    for t in take: t.start()
    me = lax.axis_index("dp") * lax.axis_size("replica") + lax.axis_index("replica")
    start = pl.multiple_of((me * 24) // 16 * 16, 16)
    reads = [pltpu.make_async_copy(h.at[pl.ds(start, 32)], v, sem.at[i]) for i, (h, v) in ((0, (wqkv_h, wq)), (1, (win_h, wi)))]
    for r in reads: r.start()
    loss_o[0, 0] = loss_i[0, 0]
    n0, n1 = counts[2 * me], counts[2 * me + 1]
    widen(wide, wup[...].astype(f32))
    up = wide[...].astype(bf16)
    widen(wide, (2.0 * bitsT[...].astype(f32) - 1.0) * BITS ** -0.5)
    target = (wide[...].T * 0.25).astype(bf16)
    rows = 768 // PIECES
    for i in range(PIECES):
        row = lax.broadcasted_iota(jnp.int32, (rows, D), 0) + i * rows
        live = row < jnp.where(row < SEQ, n0, n1 + SEQ)
        dec[part(i), :] = jnp.where(live, dot(target[i * rows:(i + 1) * rows], up), 0.0)
        show[i].start()
        take[i].wait()
        give[i].start()
    for k in range(12):
        gwin[:, k * W:(k + 1) * W] = grads[k] * scale
    for g in range(3):
        gwao[:, g * W:(g + 1) * W] = grads[13 + 4 * g] * scale
        for j in range(3):
            gwqkv[:, j * D + g * W:j * D + (g + 1) * W] = grads[14 + 4 * g + j] * scale
    widen(wide, wdownT[...].astype(f32))
    wd = wide[...].astype(bf16)
    code, other = grads[12, :, :128] * scale, grads[12, :, 128:] * scale
    lane = lanes_of(24)
    for j in range(4):
        v = jnp.where(lane // 32 == j, code, 0.0)
        hi = v.astype(bf16)
        lo = (v - hi.astype(f32)).astype(bf16)
        gwout[24 * j:24 * j + 24, :] = dot(hi, wd) + dot(lo, wd)
    gwdown[...] = other[:, :BITS]
    for r in reads: r.wait()
    odd = me % 2
    own = lax.broadcasted_iota(jnp.int32, (24, D), 1) == lax.broadcasted_iota(jnp.int32, (24, D), 0) + me * 24
    def gain(weights, grad, g, lane_at, into):
        w = weights[...].astype(f32)
        w = jnp.where(odd == 1, w[8:32], w[0:24])
        mine = jnp.sum(jnp.where(own, g[...].reshape(1, D), 0.0), axis=1, keepdims=True)
        return jnp.where(lane == lane_at, jnp.sum(w * grad[...], axis=1, keepdims=True) / mine, into)
    flat = gain(wi, gwin, g2, 65, gain(wq, gwqkv, g1, 64, other))
    turned = jnp.concatenate([flat, jnp.zeros((104, 128), f32)], axis=0).T
    gwup[...] = turned[32:32 + BITS, :24]
    gln1[...] = turned[64:65, :24]
    gln2[...] = turned[65:66, :24]
    for t in give + show: t.wait()

def finish(scale, counts, gtok, *rest):
    any_, vm, sm = pl.BlockSpec(memory_space=pl.ANY), pl.BlockSpec(memory_space=pltpu.VMEM), pl.BlockSpec(memory_space=pltpu.SMEM)
    shapes = [gtok.shape, gtok.shape, (1, 1), (1, 24), (24, 3 * D), (24, D), (1, 24), (24, FF), (96, D), (24, BITS), (BITS, 24)]
    return pl.pallas_call(functools.partial(finish_kernel, scale),
        out_shape=[jax.ShapeDtypeStruct(s, f32) for s in shapes],
        in_specs=[sm, any_, sm, any_, any_] + [vm] * 6,
        out_specs=[any_, any_, sm] + [vm] * 8,
        scratch_shapes=[pltpu.VMEM((32, 3 * D), bf16), pltpu.VMEM((32, FF), bf16), pltpu.VMEM((128, D), f32), pltpu.VMEM(gtok.shape, f32), pltpu.VMEM(gtok.shape, f32),
            pltpu.SemaphoreType.DMA((2,)), pltpu.SemaphoreType.DMA((3, PIECES))],
        name="finish")(counts, gtok, *rest)

def kernel_body(tokens, counts, bits, outgrad, g1, wqkv, wao, g2, win, wout, wdown, wup):
    bitsT, wdownT = bits.T, wdown.T
    gtok, loss, grads = train(counts, bitsT, wup, wdownT, g1, g2, tokens, outgrad, wqkv, wao, win, wout)[:3]
    scale = (tokens.shape[0] * lax.axis_size(("dp", "replica"))) ** -0.5
    decoded, gtok, loss, gln1, gwqkv, gwao, gln2, gwin, gwout, gwdown, gwup = finish(scale, counts, gtok, loss, wqkv, win, grads, wdownT, g1, g2, bitsT, wup)
    return (decoded, loss.reshape(()), gtok, gln1.reshape(24), gwqkv, gwao, gln2.reshape(24), gwin, gwout, gwdown, gwup)

eps_norm = 1e-06
neg_big = -1e30
sharpness = 8.0
commit_weight = 0.25


def exact_gelu(values):
    return jax.nn.gelu(values, approximate=False)


def layer_norm(values, gain):
    centered = values - jnp.mean(values, axis=-1, keepdims=True)
    inv_std = lax.rsqrt(jnp.mean(centered * centered, axis=-1, keepdims=True) + eps_norm)
    normed = centered * inv_std
    return (normed * gain, normed, inv_std)


def plain_norm_back(grad_out, normed, inv_std, gain):
    grad_normed = grad_out * gain
    grad_gain = jnp.sum(grad_out * normed, axis=0)
    spread_part = jnp.mean(grad_normed * normed, axis=-1, keepdims=True)
    grad_in = inv_std * (
        grad_normed - jnp.mean(grad_normed, axis=-1, keepdims=True) - normed * spread_part
    )
    return (grad_in, grad_gain)


def inner_rows(left, right):
    return lax.dot_general(
        left, right, (((0,), (0,)), ((), ())), preferred_element_type=jnp.float32
    )


def times_transposed(left, right):
    return lax.dot_general(
        left, right, (((1,), (1,)), ((), ())), preferred_element_type=jnp.float32
    )


def attention_logits(queries, key_rows, key_valid):
    scores = jnp.einsum("bqhd,bkhd->bhqk", queries, key_rows, preferred_element_type=jnp.float32)
    return jnp.where(key_valid, scores * HEAD ** (-0.5), neg_big)


def plain_body(
    tokens,
    patch_counts,
    code_bits,
    out_grad,
    ln1_gain,
    w_qkv,
    w_attn_out,
    ln2_gain,
    w_mlp_in,
    w_mlp_out,
    w_down,
    w_up,
):
    row_count = tokens.shape[0]
    images = row_count // SEQ
    width_all = tokens.shape[1]
    first_image = lax.axis_index(("dp", "replica")) * images
    counts = lax.dynamic_slice_in_dim(patch_counts, first_image, images)
    total_count = jnp.sum(patch_counts).astype(jnp.float32)
    valid_slots = jnp.arange(SEQ, dtype=jnp.int32)[None, :] < counts[:, None]
    key_valid = valid_slots[:, None, None, :]
    row_valid = valid_slots.reshape(row_count).astype(jnp.float32)[:, None]
    target = (2.0 * code_bits.astype(jnp.float32) - 1.0) * BITS ** (-0.5)
    normed1_out, normed1, inv_std1 = layer_norm(tokens, ln1_gain)
    attn_in = normed1_out.astype(jnp.bfloat16)
    qkv_rows = jnp.dot(attn_in, w_qkv, preferred_element_type=jnp.float32).astype(jnp.bfloat16)
    qkv_rows = qkv_rows.reshape(images, SEQ, 3, HEADS, HEAD)
    queries = qkv_rows[:, :, 0]
    key_rows = qkv_rows[:, :, 1]
    value_rows = qkv_rows[:, :, 2]
    logits = attention_logits(queries, key_rows, key_valid)
    row_max = jnp.max(logits, axis=-1, keepdims=True)
    weights = jnp.exp(logits - row_max)
    row_total = jnp.sum(weights, axis=-1, keepdims=True)
    log_total = row_max + jnp.log(row_total)
    prob_low = (weights / row_total).astype(jnp.bfloat16)
    context = jnp.einsum(
        "bhqk,bkhd->bqhd", prob_low, value_rows, preferred_element_type=jnp.float32
    )
    context_low = context.astype(jnp.bfloat16).reshape(row_count, width_all)
    hidden1 = tokens + jnp.dot(context_low, w_attn_out, preferred_element_type=jnp.float32)
    normed2_out, normed2, inv_std2 = layer_norm(hidden1, ln2_gain)
    mlp_in = normed2_out.astype(jnp.bfloat16)
    pre_act = jnp.dot(mlp_in, w_mlp_in, preferred_element_type=jnp.float32)
    activation, gelu_back = jax.vjp(exact_gelu, pre_act)
    activation_low = activation.astype(jnp.bfloat16)
    hidden2 = hidden1 + jnp.dot(activation_low, w_mlp_out, preferred_element_type=jnp.float32)
    hidden2_low = hidden2.astype(jnp.bfloat16)
    raw_code = jnp.dot(hidden2_low, w_down, preferred_element_type=jnp.float32)
    inv_len = lax.rsqrt(jnp.sum(raw_code * raw_code, axis=-1, keepdims=True) + 1.0)
    unit_code = raw_code * inv_len
    quant_low = target.astype(jnp.bfloat16)
    decoded = row_valid * jnp.dot(quant_low, w_up, preferred_element_type=jnp.float32)
    logit_bits = unit_code * sharpness
    soft_prob = jax.nn.sigmoid(logit_bits)
    token_ent = jax.nn.softplus(logit_bits) - soft_prob * logit_bits
    code_miss = unit_code - target
    prob_sum = jnp.sum(soft_prob * row_valid, axis=0)
    ent_sum = jnp.sum(token_ent * row_valid)
    commit_sum = jnp.sum(code_miss * code_miss * row_valid)
    prob_sum, ent_sum, commit_sum = lax.psum((prob_sum, ent_sum, commit_sum), ("dp", "replica"))
    mean_prob = prob_sum / total_count
    code_ent = jnp.sum(
        -mean_prob * jnp.log(mean_prob) - (1.0 - mean_prob) * jnp.log(1.0 - mean_prob)
    )
    entropy_loss = (commit_weight * commit_sum + ent_sum) / total_count - code_ent
    grad_dec_low = (row_valid * out_grad).astype(jnp.bfloat16)
    grad_w_up = inner_rows(quant_low, grad_dec_low)
    grad_quant = times_transposed(grad_dec_low, w_up)
    prob_logit = jnp.log(mean_prob / (1.0 - mean_prob))
    loss_part = (
        sharpness * soft_prob * (1.0 - soft_prob) * (prob_logit - logit_bits)
        + 2.0 * commit_weight * code_miss
    )
    grad_unit = grad_quant + row_valid * loss_part
    grad_raw = inv_len * (
        grad_unit - unit_code * jnp.sum(grad_unit * unit_code, axis=-1, keepdims=True)
    )
    grad_raw_low = grad_raw.astype(jnp.bfloat16)
    grad_w_down = inner_rows(hidden2_low, grad_raw_low)
    grad_hidden2 = times_transposed(grad_raw_low, w_down)
    grad_mlp_low = grad_hidden2.astype(jnp.bfloat16)
    grad_w_mlp_out = inner_rows(activation_low, grad_mlp_low)
    grad_activation = times_transposed(grad_mlp_low, w_mlp_out)
    grad_pre_low = gelu_back(grad_activation)[0].astype(jnp.bfloat16)
    grad_w_mlp_in = inner_rows(mlp_in, grad_pre_low)
    grad_norm2_in = times_transposed(grad_pre_low, w_mlp_in)
    grad_from_norm2, grad_ln2 = plain_norm_back(grad_norm2_in, normed2, inv_std2, ln2_gain)
    grad_hidden1 = grad_hidden2 + grad_from_norm2
    grad_attn_low = grad_hidden1.astype(jnp.bfloat16)
    grad_w_attn_out = inner_rows(context_low, grad_attn_low)
    grad_context = times_transposed(grad_attn_low, w_attn_out).astype(jnp.bfloat16)
    grad_context = grad_context.reshape(images, SEQ, HEADS, HEAD)
    grad_values = jnp.einsum(
        "bhqk,bqhd->bkhd", prob_low, grad_context, preferred_element_type=jnp.float32
    )
    grad_prob = jnp.einsum(
        "bqhd,bkhd->bhqk", grad_context, value_rows, preferred_element_type=jnp.float32
    )
    attn_prob = jnp.exp(attention_logits(queries, key_rows, key_valid) - log_total)
    grad_scores = (
        attn_prob
        * (grad_prob - jnp.sum(grad_prob * attn_prob, axis=-1, keepdims=True))
        * HEAD ** (-0.5)
    )
    grad_scores_low = grad_scores.astype(jnp.bfloat16)
    grad_queries = jnp.einsum(
        "bhqk,bkhd->bqhd", grad_scores_low, key_rows, preferred_element_type=jnp.float32
    )
    grad_keys = jnp.einsum(
        "bhqk,bqhd->bkhd", grad_scores_low, queries, preferred_element_type=jnp.float32
    )
    grad_qkv = jnp.stack((grad_queries, grad_keys, grad_values), axis=2).reshape(
        row_count, 3 * width_all
    )
    grad_qkv_low = grad_qkv.astype(jnp.bfloat16)
    grad_w_qkv = inner_rows(attn_in, grad_qkv_low)
    grad_norm1_in = times_transposed(grad_qkv_low, w_qkv)
    grad_from_norm1, grad_ln1 = plain_norm_back(grad_norm1_in, normed1, inv_std1, ln1_gain)
    grad_tokens = grad_hidden1 + grad_from_norm1
    summed = (
        lax.psum_scatter(grad_ln1, ("dp", "replica"), scatter_dimension=0, tiled=True),
        lax.psum_scatter(grad_w_qkv, ("dp", "replica"), scatter_dimension=0, tiled=True),
        lax.psum_scatter(grad_w_attn_out, ("dp", "replica"), scatter_dimension=0, tiled=True),
        lax.psum_scatter(grad_ln2, ("dp", "replica"), scatter_dimension=0, tiled=True),
        lax.psum_scatter(grad_w_mlp_in, ("dp", "replica"), scatter_dimension=0, tiled=True),
        lax.psum_scatter(grad_w_mlp_out, ("dp", "replica"), scatter_dimension=0, tiled=True),
        lax.psum_scatter(grad_w_down, ("dp", "replica"), scatter_dimension=0, tiled=True),
        lax.psum_scatter(grad_w_up, ("dp", "replica"), scatter_dimension=1, tiled=True),
    )
    grad_scale = (row_count * lax.axis_size(("dp", "replica"))) ** (-0.5)
    return (
        decoded,
        entropy_loss,
        grad_tokens,
        summed[0] * grad_scale,
        summed[1] * grad_scale,
        summed[2] * grad_scale,
        summed[3] * grad_scale,
        summed[4] * grad_scale,
        summed[5] * grad_scale,
        summed[6] * grad_scale,
        summed[7] * grad_scale,
    )


def solution(mesh):
    in_specs = (
        P(("dp", "replica"), None),
        P(),
        P(("dp", "replica"), None),
        P(("dp", "replica"), None),
        P(),
        P(),
        P(),
        P(),
        P(),
        P(),
        P(),
        P(),
    )
    out_specs = (
        P(("dp", "replica"), None),
        P(),
        P(("dp", "replica"), None),
        P(("dp", "replica")),
        P(("dp", "replica"), None),
        P(("dp", "replica"), None),
        P(("dp", "replica")),
        P(("dp", "replica"), None),
        P(("dp", "replica"), None),
        P(("dp", "replica"), None),
        P(None, ("dp", "replica")),
    )
    body = kernel_body if (mesh.shape["dp"], mesh.shape["replica"]) == (8, 4) else plain_body
    return jax.shard_map(body, mesh=mesh, in_specs=in_specs, out_specs=out_specs, check_vma=False)
```
